32 devices in a mesh: dp: 4 (over z), expert: 4 (over y, core), hidden: 2 (over x).
Axes of the slice: x: 2, y: 2, z: 4, core: 2. Of those that a mesh axis runs over, the one named last changes fastest.
Arguments:
- layer_input: bfloat16 [4, 256, 3072], P('dp', 'expert'), may hold values from -6 to 6
- grad_out: bfloat16 [4, 256, 3072], P('dp', 'expert'), may hold values from -6 to 6
- picks: int32 [4, 4, 4, 8], P('dp', 'expert'), may hold values from 0 to 63, as said below
- gates: float32 [4, 4, 4, 8], P('dp', 'expert'), may hold values from 0.1 to 1
- w_up: bfloat16 [4, 3072, 2048], P('expert', None, 'hidden'), may hold values from -0.109375 to 0.109375
- w_down: bfloat16 [4, 3072, 2048], P('expert', None, 'hidden'), may hold values from -0.125 to 0.125
Outputs:
- grad_in: bfloat16 [4, 256, 3072], P('dp', 'expert', 'hidden')
- grad_up: float32 [4, 3072, 2048], P('expert', 'dp', 'hidden')
- grad_down: float32 [4, 3072, 2048], P('expert', 'dp', 'hidden')
The draws below stay inside these ranges and needn't reach their ends.
Inputs may be any that keep to these rules, and one draw needn't show every extreme that they name: `picks`: for every group, block and expert, the 8 positions are distinct, so each expert takes exactly 8 tokens from every block of 64 tokens.
All inputs are finite; a program needn't handle non-finite values.
Results may differ from the reference program's by a relative error of at most 0.015.
Values may be sent and summed in bfloat16 or wider, within the bound.
No kernel may reach another device: no remote copies, remote signals or barrier semaphores. Data moves between devices by JAX's collectives and lax.ppermute only.
A program may use at most 64 MiB of HBM per device.

```python
import math
import jax
import jax.numpy as jnp
from jax import lax

D = 3072
FF = 2048
TOK_DEV = 64
PICK = 8
GROUPS = 4
BLOCKS = 4
EXPERTS = 4
GROUP_TOK = 256
N_HIDDEN = 2


def draw_picks(key, part):
    key = jax.random.fold_in(key, 11)
    scores = jax.random.randint(key, (GROUPS, BLOCKS, EXPERTS, TOK_DEV), 0, 1 << 20)
    distinct = scores * TOK_DEV + jnp.arange(TOK_DEV, dtype=jnp.int32)
    values, chosen = lax.top_k(distinct, PICK)
    return chosen.astype(jnp.int32)


def shard_levels(own_key, extent, split, low, high):
    factor_of = 1.0
    for axis_at, blocks in split:
        draws = jax.random.uniform(jax.random.fold_in(jax.random.fold_in(own_key, 6), axis_at), (blocks,), jnp.float32, low / len(split), high / len(split))
        factor_of = factor_of * jnp.repeat(jnp.exp(draws), extent[axis_at] // blocks).reshape((-1,) + (1,) * (len(extent) - 1 - axis_at))
    return factor_of


def noise(rng, extent, spread, reach, cuts=(), kind=jnp.bfloat16):
    level = shard_levels(rng, extent, cuts, -0.22, 0.18) if cuts else 1.0
    result = jax.random.normal(rng, extent, jnp.float32) * spread * level
    return jnp.minimum(jnp.maximum(result, -reach), reach).astype(kind)


def setup_inputs(seed: int = 0) -> dict:
    splits = jax.random.split(jax.random.key(seed), 7)
    return {
        "layer_input": noise(splits[0], (GROUPS, GROUP_TOK, D), 1.0, 6.0, ((0, 4), (1, 4))),
        "grad_out": noise(splits[1], (GROUPS, GROUP_TOK, D), 1.0, 6.0, ((0, 4), (1, 4))),
        "picks": draw_picks(jax.random.fold_in(splits[6], 71), 0),
        "gates": jnp.clip(jnp.exp(math.log(1.0) - 2.3025851 * jax.random.uniform(splits[3], (GROUPS, EXPERTS, BLOCKS, PICK), jnp.float32) ** shard_levels(splits[3], (GROUPS, EXPERTS, BLOCKS, PICK), ((0, 4), (1, 4)), -0.2, 0.2)), 0.1, 1.0),
        "w_up": noise(splits[4], (EXPERTS, D, FF), D ** -0.5, 0.109375, ((0, 4), (2, 2))),
        "w_down": noise(splits[5], (EXPERTS, D, FF), FF ** -0.5, 0.125, ((0, 4), (2, 2))),
    }


ROOT_TERM = 0.7978845608028654
CUBIC_TERM = 0.044715


def gelu_value(pre):
    inner = jnp.tanh(ROOT_TERM * (pre + CUBIC_TERM * pre * pre * pre))
    return 0.5 * pre * (1.0 + inner)


def gelu_slope(pre):
    inner = jnp.tanh(ROOT_TERM * (pre + CUBIC_TERM * pre * pre * pre))
    return 0.5 * (1.0 + inner) + 0.5 * pre * (1.0 - inner * inner) * ROOT_TERM * (1.0 + 3.0 * CUBIC_TERM * pre * pre)


def reference(layer_input, grad_out, picks, gates, w_up, w_down):
    groups, group_tok, width = layer_input.shape
    blocks = picks.shape[1]
    n_exp = picks.shape[2]
    n_pick = picks.shape[3]
    slots = blocks * n_pick
    offsets = (jnp.arange(blocks, dtype=jnp.int32) * TOK_DEV)[None, :, None, None]
    slot_token = jnp.transpose(picks + offsets, (0, 2, 1, 3)).reshape(groups, n_exp, slots).astype(jnp.int32)
    gate_slots = gates.reshape(groups, n_exp, slots)
    part_units = FF // N_HIDDEN

    def one_expert(packed):
        index, gate, upper, lower = packed
        rows_in = jnp.take_along_axis(layer_input, index[:, :, None], axis=1)
        rows_out = jnp.take_along_axis(grad_out, index[:, :, None], axis=1)
        scaled = (gate[:, :, None] * rows_out.astype(jnp.float32)).astype(jnp.bfloat16)
        pre = jnp.einsum("gsd,df->gsf", rows_in.astype(jnp.float32), upper.astype(jnp.float32))
        act = gelu_value(pre).astype(jnp.bfloat16)
        back = jnp.einsum("gsd,df->gsf", scaled.astype(jnp.float32), lower.astype(jnp.float32))
        grad_pre = (back * gelu_slope(pre)).astype(jnp.bfloat16)
        up_terms = jnp.einsum("gsd,gsf->gdf", rows_in.astype(jnp.float32), grad_pre.astype(jnp.float32))
        up_terms = lax.optimization_barrier(up_terms.astype(jnp.bfloat16))
        grad_upper = jnp.sum(up_terms.astype(jnp.float32), axis=0)
        down_terms = jnp.einsum("gsd,gsf->gdf", scaled.astype(jnp.float32), act.astype(jnp.float32))
        down_terms = lax.optimization_barrier(down_terms.astype(jnp.bfloat16))
        grad_lower = jnp.sum(down_terms.astype(jnp.float32), axis=0)
        split_pre = grad_pre.reshape(groups, slots, N_HIDDEN, part_units).astype(jnp.float32)
        split_up = upper.reshape(width, N_HIDDEN, part_units).astype(jnp.float32)
        pieces = jnp.einsum("gskf,dkf->gskd", split_pre, split_up)
        pieces = lax.optimization_barrier(pieces.astype(jnp.bfloat16))
        slot_grad = jnp.sum(pieces.astype(jnp.float32), axis=2).astype(jnp.bfloat16)
        return grad_upper, grad_lower, slot_grad

    token_major = jnp.transpose(slot_token, (1, 0, 2))
    gate_major = jnp.transpose(gate_slots, (1, 0, 2))
    grad_up, grad_down, slot_grad = lax.map(one_expert, (token_major, gate_major, w_up, w_down))
    group_index = jnp.broadcast_to(jnp.arange(groups, dtype=jnp.int32)[None, :, None], token_major.shape)
    total = jnp.zeros((groups, group_tok, width), jnp.float32)
    total = total.at[group_index, token_major].add(slot_grad.astype(jnp.float32))
    return total.astype(jnp.bfloat16), grad_up, grad_down
```

```python
import functools

import jax
import jax.numpy as jnp
from jax import lax
from jax.experimental import pallas as pl
from jax.experimental.pallas import tpu as pltpu
from jax.sharding import PartitionSpec as P

ROOT_TERM = 0.7978845608028654
CUBIC_TERM = 0.044715


def gelu_pair(pre):
    square = pre * pre
    inner = jnp.tanh(ROOT_TERM * (pre + CUBIC_TERM * square * pre))
    value = 0.5 * pre * (1.0 + inner)
    slope = 0.5 * (1.0 + inner) + 0.5 * pre * (1.0 - inner * inner) * ROOT_TERM * (
        1.0 + 3.0 * CUBIC_TERM * square
    )
    return value, slope


def hop(x, axis, step):
    n = lax.axis_size(axis)
    if step % n == 0:
        return x
    return lax.ppermute(x, axis, [(i, (i + step) % n) for i in range(n)])


def column(ref, order):
    n = ref.shape[-1]
    down = lax.broadcasted_iota(jnp.int32, (n, n), 0)
    along = lax.broadcasted_iota(jnp.int32, (n, n), 1)
    out = []
    for at in order:
        row = ref[0, 0, pl.ds(at, 1), :].astype(jnp.float32)
        out.append(jnp.sum(jnp.where(down == along, row, 0.0), axis=1, keepdims=True))
    return jnp.concatenate(out, axis=0)


def pick_kernel(n_dp, picks_hbm, tokens_hbm, upstream_hbm, rows_ref, *refs):
    *side_refs, picks_ref, tokens_ref, upstream_ref, sems = refs
    n_exp, n_pick = picks_ref.shape[2:]
    tok_dev, width = tokens_ref.shape[1:]
    cols = width // n_dp
    copies = [
        pltpu.make_async_copy(picks_hbm, picks_ref, sems.at[0]),
        pltpu.make_async_copy(tokens_hbm, tokens_ref, sems.at[1]),
        pltpu.make_async_copy(upstream_hbm, upstream_ref, sems.at[2]),
    ]
    for copy in copies:
        copy.start()
    me = lax.axis_index("expert")
    my_dp = lax.axis_index("dp")
    copies[0].wait()
    wanted = column(picks_ref, [(me + s) % n_exp for s in range(n_exp)])
    spots = lax.broadcasted_iota(jnp.int32, (n_exp * n_pick, tok_dev), 1)
    selector = jnp.where(wanted.astype(jnp.int32) == spots, 1.0, 0.0).astype(jnp.bfloat16)
    for at, copy, source in ((0, copies[1], tokens_ref), (width, copies[2], upstream_ref)):
        copy.wait()
        rows_ref[:, at : at + width] = jnp.dot(
            selector, source[0], preferred_element_type=jnp.float32
        ).astype(jnp.bfloat16)
    for s in range(1, n_dp):
        start = ((my_dp + s) % n_dp) * cols
        for half in range(2):
            side_refs[s - 1][:, half * cols : (half + 1) * cols] = rows_ref[
                :, pl.ds(pl.multiple_of(half * width + start, 128), cols)
            ]


def load_kernel(after_ref, gates_hbm, upper_hbm, lower_hbm, gates_ref, upper_ref, lower_ref, sems):
    copies = [
        pltpu.make_async_copy(source, target, sems.at[k])
        for k, (source, target) in enumerate(
            ((gates_hbm, gates_ref), (upper_hbm, upper_ref), (lower_hbm, lower_ref))
        )
    ]
    for copy in copies:
        copy.start()
    for copy in copies:
        copy.wait()


def factor_kernel(gates_ref, rows_ref, upper_ref, lower_ref, out_ref):
    n_exp = gates_ref.shape[2]
    width, units = upper_ref.shape[1:]
    me = lax.axis_index("expert")
    gate = column(gates_ref, [(me + n_exp - s) % n_exp for s in range(n_exp)])
    pre = jnp.dot(rows_ref[:, :width], upper_ref[0], preferred_element_type=jnp.float32)
    back = jnp.dot(rows_ref[:, width:], lower_ref[0], preferred_element_type=jnp.float32)
    value, slope = gelu_pair(pre)
    out_ref[:, :units] = (back * gate * slope).astype(jnp.bfloat16)
    out_ref[:, units:] = (value * gate).astype(jnp.bfloat16)


def piece_kernel(n_hid, factor_ref, upper_ref, out_ref):
    n_pick, part = out_ref.shape[1:]
    width, units = upper_ref.shape[1:]
    n_exp = out_ref.shape[0] // n_hid
    me = lax.axis_index("expert")
    piece = lax.dot_general(
        factor_ref[:, :units], upper_ref[0], (((1,), (1,)), ((), ())), preferred_element_type=jnp.float32
    )
    for s in range(n_exp):
        owner = ((me + n_exp - s) % n_exp) * n_hid
        for h in range(n_hid):
            out_ref[owner + h] = piece[
                s * n_pick : (s + 1) * n_pick, h * part : (h + 1) * part
            ].astype(jnp.bfloat16)


def weight_kernel(chunks, side_ref, factor_ref, up_ref, down_ref, held, sems):
    units = factor_ref.shape[1] // 2
    cols = side_ref.shape[1] // 2
    step = units // chunks
    copies = []
    for which, out in ((0, up_ref), (1, down_ref)):
        for c in range(chunks):
            spot = pl.ds(c * step, step)
            held[which, :, spot] = lax.dot_general(
                side_ref[:, which * cols : (which + 1) * cols],
                factor_ref[:, pl.ds(which * units + c * step, step)],
                (((0,), (0,)), ((), ())),
                preferred_element_type=jnp.float32,
            )
            copy = pltpu.make_async_copy(
                held.at[which, :, spot], out.at[0, :, spot], sems.at[which, c]
            )
            copy.start()
            copies.append(copy)
    for copy in copies:
        copy.wait()


VMEM = pl.BlockSpec(memory_space=pltpu.VMEM)
HBM = pl.BlockSpec(memory_space=pltpu.HBM)
ROOM = pltpu.CompilerParams(vmem_limit_bytes=16 << 20)


def local(layer_input, grad_out, picks, gates, w_up, w_down):
    tok_dev, width = layer_input.shape[1:]
    n_exp, n_pick = picks.shape[2:]
    slots = n_exp * n_pick
    units = w_up.shape[2]
    n_dp = lax.axis_size("dp")
    n_hid = lax.axis_size("hidden")
    cols = width // n_dp
    part = width // n_hid
    bf16 = jnp.bfloat16
    layer_input, grad_out, w_up, w_down = (
        pltpu.with_memory_space_constraint(x, pltpu.HBM)
        for x in (layer_input, grad_out, w_up, w_down)
    )

    send, *side = pl.pallas_call(
        functools.partial(pick_kernel, n_dp),
        out_shape=[jax.ShapeDtypeStruct((slots, 2 * width), bf16)]
        + [jax.ShapeDtypeStruct((slots, 2 * cols), bf16)] * (n_dp - 1),
        in_specs=[HBM] * 3,
        out_specs=[VMEM] * n_dp,
        scratch_shapes=[
            pltpu.VMEM(picks.shape, jnp.int32),
            pltpu.VMEM(layer_input.shape, bf16),
            pltpu.VMEM(grad_out.shape, bf16),
            pltpu.SemaphoreType.DMA((3,)),
        ],
        compiler_params=ROOM,
        name="pick",
    )(picks, layer_input, grad_out)

    rows = jnp.concatenate(
        [hop(send[s * n_pick : (s + 1) * n_pick], "expert", s) for s in range(n_exp)], axis=0
    )
    side = [hop(x, "dp", s + 1).reshape(n_exp, n_pick, 2 * cols) for s, x in enumerate(side)]
    side = jnp.stack(side)
    side = [hop(side[:, s], "expert", s) for s in range(n_exp)]
    side = jnp.stack(side, axis=1).reshape((n_dp - 1) * slots, 2 * cols)
    at = lax.axis_index("dp") * cols
    own = jnp.concatenate(
        [
            lax.dynamic_slice_in_dim(rows, at, cols, 1),
            lax.dynamic_slice_in_dim(rows, width + at, cols, 1),
        ],
        axis=1,
    )
    side = jnp.concatenate([own, side], axis=0)

    gate_held, upper, lower = pl.pallas_call(
        load_kernel,
        out_shape=[jax.ShapeDtypeStruct(x.shape, x.dtype) for x in (gates, w_up, w_down)],
        in_specs=[HBM] * 4,
        out_specs=[VMEM] * 3,
        scratch_shapes=[pltpu.SemaphoreType.DMA((3,))],
        cost_estimate=pl.CostEstimate(
            flops=0, bytes_accessed=4 * w_up.size + 4 * w_down.size, transcendentals=0
        ),
        compiler_params=ROOM,
        name="load",
    )(send, gates, w_up, w_down)
    factors = pl.pallas_call(
        factor_kernel,
        out_shape=jax.ShapeDtypeStruct((slots, 2 * units), bf16),
        in_specs=[VMEM] * 4,
        out_specs=VMEM,
        compiler_params=ROOM,
        name="factor",
    )(gate_held, rows, upper, lower)

    gathered = jnp.concatenate([hop(factors, "dp", s) for s in range(n_dp)], axis=0)

    piece = pl.pallas_call(
        functools.partial(piece_kernel, n_hid),
        out_shape=jax.ShapeDtypeStruct((n_exp * n_hid, n_pick, part), bf16),
        in_specs=[VMEM, VMEM],
        out_specs=VMEM,
        compiler_params=ROOM,
        name="piece",
    )(factors, upper)
    returned = lax.all_to_all(piece, ("expert", "hidden"), 0, 0)
    twice = jnp.broadcast_to(picks[0, 0][:, None, :], (n_exp, n_hid, n_pick)).reshape(slots * n_hid)
    spread = (jnp.arange(tok_dev, dtype=jnp.int32)[:, None] == twice[None, :]).astype(bf16)
    grad_rows = jnp.dot(
        spread, returned.reshape(slots * n_hid, part), preferred_element_type=jnp.float32
    )

    chunks = max(1, units // 256)
    grads = pl.pallas_call(
        functools.partial(weight_kernel, chunks),
        out_shape=[jax.ShapeDtypeStruct((1, cols, units), jnp.float32)] * 2,
        in_specs=[VMEM, VMEM],
        out_specs=[HBM] * 2,
        scratch_shapes=[
            pltpu.VMEM((2, cols, units), jnp.float32),
            pltpu.SemaphoreType.DMA((2, chunks)),
        ],
        compiler_params=ROOM,
        name="weight",
    )(side, gathered)
    return (grad_rows.astype(bf16)[None], *grads)


def solution(mesh):
    placed = (
        P("dp", "expert", None),
        P("dp", "expert", None),
        P("dp", "expert", None, None),
        P("dp", "expert", None, None),
        P("expert", None, "hidden"),
        P("expert", None, "hidden"),
    )
    return jax.shard_map(
        local,
        mesh=mesh,
        in_specs=placed,
        out_specs=(
            P("dp", "expert", "hidden"),
            P("expert", "dp", "hidden"),
            P("expert", "dp", "hidden"),
        ),
        check_vma=False,
    )
```

```python
import functools

import jax
import jax.numpy as jnp
from jax import lax
from jax.experimental import pallas as pl
from jax.experimental.pallas import tpu as pltpu
from jax.sharding import PartitionSpec as P

ROOT_TERM = 0.7978845608028654
CUBIC_TERM = 0.044715


def gelu_pair(pre):
    square = pre * pre
    inner = jnp.tanh(ROOT_TERM * (pre + CUBIC_TERM * square * pre))
    value = 0.5 * pre * (1.0 + inner)
    slope = 0.5 * (1.0 + inner) + 0.5 * pre * (1.0 - inner * inner) * ROOT_TERM * (
        1.0 + 3.0 * CUBIC_TERM * square
    )
    return value, slope


def hop(x, axis, step):
    n = lax.axis_size(axis)
    if step % n == 0:
        return x
    return lax.ppermute(x, axis, [(i, (i + step) % n) for i in range(n)])


def column(ref, order):
    n = ref.shape[-1]
    down = lax.broadcasted_iota(jnp.int32, (n, n), 0)
    along = lax.broadcasted_iota(jnp.int32, (n, n), 1)
    out = []
    for at in order:
        row = ref[0, 0, pl.ds(at, 1), :].astype(jnp.float32)
        out.append(jnp.sum(jnp.where(down == along, row, 0.0), axis=1, keepdims=True))
    return jnp.concatenate(out, axis=0)


def pick_kernel(n_hid, n_share, picks_hbm, tokens_hbm, upstream_hbm, rows_ref, side_ref, spread_ref, *refs):
    picks_ref, tokens_ref, upstream_ref, sems = refs
    n_exp = picks_ref.shape[2]
    tok_dev, width = tokens_ref.shape[1:]
    copies = [
        pltpu.make_async_copy(picks_hbm, picks_ref, sems.at[0]),
        pltpu.make_async_copy(tokens_hbm, tokens_ref, sems.at[1]),
        pltpu.make_async_copy(upstream_hbm, upstream_ref, sems.at[2]),
    ]
    for copy in copies:
        copy.start()
    me = lax.axis_index("expert")
    copies[0].wait()

    def one_hot(order):
        wanted = column(picks_ref, order).astype(jnp.int32)
        spots = lax.broadcasted_iota(jnp.int32, (wanted.shape[0], tok_dev), 1)
        return jnp.where(wanted == spots, 1.0, 0.0).astype(jnp.bfloat16)

    selector = one_hot([(me + s) % n_exp for s in range(n_exp)])
    spread_ref[...] = one_hot([e for e in range(n_exp) for _ in range(n_hid)])
    for at, copy, source in ((0, copies[1], tokens_ref), (width, copies[2], upstream_ref)):
        copy.wait()
        rows_ref[:, at : at + width] = jnp.dot(
            selector, source[0], preferred_element_type=jnp.float32
        ).astype(jnp.bfloat16)
    blocks, n_pick, span = side_ref.shape
    n_dp = blocks // n_exp
    cols = width // n_dp
    if n_share == 1:
        starts = [0, width]
    else:
        per_half = n_share // 2
        share = lax.axis_index("hidden")
        starts = [(share // per_half) * width + (share % per_half) * span]
    for p in range(n_dp):
        for k, start in enumerate(starts):
            wide = span // len(starts)
            cut = rows_ref[:, pl.ds(pl.multiple_of(start + p * cols, 128), wide)].astype(jnp.float32)
            for s in range(n_exp):
                side_ref[p * n_exp + (me + s) % n_exp, :, k * wide : (k + 1) * wide] = cut[
                    s * n_pick : (s + 1) * n_pick
                ].astype(jnp.bfloat16)


def load_kernel(after_ref, source, target, sem):
    copy = pltpu.make_async_copy(source, target, sem)
    copy.start()
    copy.wait()


def factor_kernel(chunks, gates_hbm, rows_ref, upper_ref, lower_hbm, out_ref, gates_ref, lower_ref, gate_sem, sems):
    n_exp = gates_ref.shape[2]
    width, units = upper_ref.shape[1:]
    step = width // chunks
    gate_copy = pltpu.make_async_copy(gates_hbm, gates_ref, gate_sem)
    gate_copy.start()
    copies = []
    for c in range(chunks):
        spot = pl.ds(c * step, step)
        copies.append(pltpu.make_async_copy(lower_hbm.at[0, spot, :], lower_ref.at[spot, :], sems.at[c]))
        copies[-1].start()
    me = lax.axis_index("expert")
    pre = jnp.dot(rows_ref[:, :width], upper_ref[0], preferred_element_type=jnp.float32)
    value, slope = gelu_pair(pre)
    gate_copy.wait()
    gate = column(gates_ref, [(me + n_exp - s) % n_exp for s in range(n_exp)])
    out_ref[:, units:] = (value * gate).astype(jnp.bfloat16)
    slope = slope * gate
    back = jnp.zeros_like(pre)
    for c in range(chunks):
        copies[c].wait()
        back += jnp.dot(
            rows_ref[:, width + c * step : width + (c + 1) * step],
            lower_ref[c * step : (c + 1) * step, :],
            preferred_element_type=jnp.float32,
        )
    out_ref[:, :units] = (back * slope).astype(jnp.bfloat16)


def piece_kernel(n_hid, factor_ref, upper_ref, out_ref):
    n_pick, part = out_ref.shape[1:]
    width, units = upper_ref.shape[1:]
    n_exp = out_ref.shape[0] // n_hid
    me = lax.axis_index("expert")
    piece = lax.dot_general(
        factor_ref[:, :units], upper_ref[0], (((1,), (1,)), ((), ())), preferred_element_type=jnp.float32
    )
    for s in range(n_exp):
        owner = ((me + n_exp - s) % n_exp) * n_hid
        for h in range(n_hid):
            out_ref[owner + h] = piece[
                s * n_pick : (s + 1) * n_pick, h * part : (h + 1) * part
            ].astype(jnp.bfloat16)


def weight_kernel(chunks, n_dp, after_ref, *refs):
    *part_refs, factor_ref, up_ref, down_ref, side_ref, held, sems = refs
    n_share = len(part_refs)
    units = factor_ref.shape[1] // 2
    cols = side_ref.shape[1] // 2
    n_exp = part_refs[0].shape[0] // n_dp
    slots = side_ref.shape[0] // n_dp
    span = part_refs[0].shape[2]
    me = lax.axis_index("expert")
    my_dp = lax.axis_index("dp")
    my_hid = lax.axis_index("hidden")
    for t, part in enumerate(part_refs):
        at = 0 if n_share == 1 else pl.multiple_of(((my_hid + n_share - t) % n_share) * span, 128)
        for s in range(n_dp):
            first = ((my_dp + n_dp - s) % n_dp) * n_exp
            blocks = [part[first + (me + n_exp - b) % n_exp].astype(jnp.float32) for b in range(n_exp)]
            side_ref[s * slots : (s + 1) * slots, pl.ds(at, span)] = jnp.concatenate(blocks, axis=0).astype(
                jnp.bfloat16
            )
    step = units // chunks
    copies = []
    for which, out in ((0, up_ref), (1, down_ref)):
        for c in range(chunks):
            spot = pl.ds(c * step, step)
            held[which, :, spot] = lax.dot_general(
                side_ref[:, which * cols : (which + 1) * cols],
                factor_ref[:, pl.ds(which * units + c * step, step)],
                (((0,), (0,)), ((), ())),
                preferred_element_type=jnp.float32,
            )
            copy = pltpu.make_async_copy(
                held.at[which, :, spot], out.at[0, :, spot], sems.at[which, c]
            )
            copy.start()
            copies.append(copy)
    for copy in copies:
        copy.wait()


VMEM = pl.BlockSpec(memory_space=pltpu.VMEM)
HBM = pl.BlockSpec(memory_space=pltpu.HBM)
ROOM = pltpu.CompilerParams(vmem_limit_bytes=16 << 20)


def local(layer_input, grad_out, picks, gates, w_up, w_down):
    tok_dev, width = layer_input.shape[1:]
    n_exp, n_pick = picks.shape[2:]
    slots = n_exp * n_pick
    units = w_up.shape[2]
    n_dp = lax.axis_size("dp")
    n_hid = lax.axis_size("hidden")
    cols = width // n_dp
    part = width // n_hid
    bf16 = jnp.bfloat16
    layer_input, grad_out, picks, gates, w_up, w_down = (
        pltpu.with_memory_space_constraint(x, pltpu.HBM)
        for x in (layer_input, grad_out, picks, gates, w_up, w_down)
    )

    n_share = n_hid if n_hid % 2 == 0 and 2 * cols % (n_hid * 128) == 0 else 1
    span = 2 * cols // n_share
    send, side, spread = pl.pallas_call(
        functools.partial(pick_kernel, n_hid, n_share),
        out_shape=[
            jax.ShapeDtypeStruct((slots, 2 * width), bf16),
            jax.ShapeDtypeStruct((n_dp * n_exp, n_pick, span), bf16),
            jax.ShapeDtypeStruct((slots * n_hid, tok_dev), bf16),
        ],
        in_specs=[HBM] * 3,
        out_specs=[VMEM] * 3,
        scratch_shapes=[
            pltpu.VMEM(picks.shape, jnp.int32),
            pltpu.VMEM(layer_input.shape, bf16),
            pltpu.VMEM(grad_out.shape, bf16),
            pltpu.SemaphoreType.DMA((3,)),
        ],
        compiler_params=ROOM,
        name="pick",
    )(picks, layer_input, grad_out)

    rows = jnp.concatenate(
        [hop(send[s * n_pick : (s + 1) * n_pick], "expert", s) for s in range(n_exp)], axis=0
    )
    side = lax.all_to_all(side, ("dp", "expert"), 0, 0)
    parts = [hop(side, "hidden", t) for t in range(n_share)]

    upper = pl.pallas_call(
        load_kernel,
        out_shape=jax.ShapeDtypeStruct(w_up.shape, w_up.dtype),
        in_specs=[HBM] * 2,
        out_specs=VMEM,
        scratch_shapes=[pltpu.SemaphoreType.DMA],
        compiler_params=ROOM,
        cost_estimate=pl.CostEstimate(flops=0, bytes_accessed=4 * w_up.size, transcendentals=0),
        name="load",
    )(send, w_up)
    chunks = max(1, width // 768)
    factors = pl.pallas_call(
        functools.partial(factor_kernel, chunks),
        out_shape=jax.ShapeDtypeStruct((slots, 2 * units), bf16),
        in_specs=[HBM, VMEM, VMEM, HBM],
        out_specs=VMEM,
        scratch_shapes=[
            pltpu.VMEM(gates.shape, jnp.float32),
            pltpu.VMEM(w_down.shape[1:], bf16),
            pltpu.SemaphoreType.DMA,
            pltpu.SemaphoreType.DMA((chunks,)),
        ],
        compiler_params=ROOM,
        cost_estimate=pl.CostEstimate(
            flops=4 * slots * w_up.size, bytes_accessed=4 * w_up.size, transcendentals=slots * units
        ),
        name="factor",
    )(gates, rows, upper, w_down)

    gathered = jnp.concatenate([hop(factors, "dp", s) for s in range(n_dp)], axis=0)

    piece = pl.pallas_call(
        functools.partial(piece_kernel, n_hid),
        out_shape=jax.ShapeDtypeStruct((n_exp * n_hid, n_pick, part), bf16),
        in_specs=[VMEM, VMEM],
        out_specs=VMEM,
        compiler_params=ROOM,
        cost_estimate=pl.CostEstimate(
            flops=2 * slots * w_up.size, bytes_accessed=2 * w_up.size, transcendentals=0
        ),
        name="piece",
    )(factors, upper)
    returned = lax.all_to_all(piece, ("expert", "hidden"), 0, 0)
    grad_rows = lax.dot_general(
        spread,
        returned.reshape(slots * n_hid, part),
        (((0,), (0,)), ((), ())),
        preferred_element_type=jnp.float32,
    ).astype(bf16)

    chunks = max(1, units // 256)
    grads = pl.pallas_call(
        functools.partial(weight_kernel, chunks, n_dp),
        out_shape=[jax.ShapeDtypeStruct((1, cols, units), jnp.float32)] * 2,
        in_specs=[pl.BlockSpec(memory_space=pl.ANY)] + [VMEM] * (n_share + 1),
        out_specs=[HBM] * 2,
        scratch_shapes=[
            pltpu.VMEM((n_dp * slots, 2 * cols), bf16),
            pltpu.VMEM((2, cols, units), jnp.float32),
            pltpu.SemaphoreType.DMA((2, chunks)),
        ],
        compiler_params=ROOM,
        name="weight",
    )(grad_rows, *parts, gathered)
    return (grad_rows[None], *grads)


def solution(mesh):
    placed = (
        P("dp", "expert", None),
        P("dp", "expert", None),
        P("dp", "expert", None, None),
        P("dp", "expert", None, None),
        P("expert", None, "hidden"),
        P("expert", None, "hidden"),
    )
    return jax.shard_map(
        local,
        mesh=mesh,
        in_specs=placed,
        out_specs=(
            P("dp", "expert", "hidden"),
            P("expert", "dp", "hidden"),
            P("expert", "dp", "hidden"),
        ),
        check_vma=False,
    )
```

```python
import functools

import jax
import jax.numpy as jnp
from jax import lax
from jax.experimental import pallas as pl
from jax.experimental.pallas import tpu as pltpu
from jax.sharding import PartitionSpec as P

ROOT_TERM = 0.7978845608028654
CUBIC_TERM = 0.044715


def gelu_pair(pre):
    square = pre * pre
    inner = jnp.tanh(ROOT_TERM * (pre + CUBIC_TERM * square * pre))
    value = 0.5 * pre * (1.0 + inner)
    slope = 0.5 * (1.0 + inner) + 0.5 * pre * (1.0 - inner * inner) * ROOT_TERM * (
        1.0 + 3.0 * CUBIC_TERM * square
    )
    return value, slope


def hop(x, axis, step):
    n = lax.axis_size(axis)
    if step % n == 0:
        return x
    return lax.ppermute(x, axis, [(i, (i + step) % n) for i in range(n)])


def column(ref, order):
    n = ref.shape[-1]
    down = lax.broadcasted_iota(jnp.int32, (n, n), 0)
    along = lax.broadcasted_iota(jnp.int32, (n, n), 1)
    out = []
    for at in order:
        row = ref[0, 0, pl.ds(at, 1), :].astype(jnp.float32)
        out.append(jnp.sum(jnp.where(down == along, row, 0.0), axis=1, keepdims=True))
    return jnp.concatenate(out, axis=0)


def pick_kernel(n_hid, picks_hbm, tokens_hbm, upstream_hbm, rows_ref, spread_ref, *refs):
    picks_ref, tokens_ref, upstream_ref, sems = refs
    n_exp = picks_ref.shape[2]
    tok_dev, width = tokens_ref.shape[1:]
    copies = [
        pltpu.make_async_copy(picks_hbm, picks_ref, sems.at[0]),
        pltpu.make_async_copy(tokens_hbm, tokens_ref, sems.at[1]),
        pltpu.make_async_copy(upstream_hbm, upstream_ref, sems.at[2]),
    ]
    for copy in copies:
        copy.start()
    me = lax.axis_index("expert")
    copies[0].wait()

    def one_hot(order):
        wanted = column(picks_ref, order).astype(jnp.int32)
        spots = lax.broadcasted_iota(jnp.int32, (wanted.shape[0], tok_dev), 1)
        return jnp.where(wanted == spots, 1.0, 0.0).astype(jnp.bfloat16)

    selector = one_hot([(me + s) % n_exp for s in range(n_exp)])
    spread_ref[...] = one_hot([e for e in range(n_exp) for _ in range(n_hid)])
    for at, copy, source in ((0, copies[1], tokens_ref), (width, copies[2], upstream_ref)):
        copy.wait()
        rows_ref[:, at : at + width] = jnp.dot(
            selector, source[0], preferred_element_type=jnp.float32
        ).astype(jnp.bfloat16)


def cut_kernel(after_ref, rows_ref, *out_refs):
    n_dp = len(out_refs) + 1
    share, wide = out_refs[0].shape
    cols = wide // 2
    width = rows_ref.shape[1] // 2
    my_dp = lax.axis_index("dp")
    spot = pl.ds(pl.multiple_of(lax.axis_index("hidden") * share, 16), share)
    for s, out_ref in enumerate(out_refs):
        at = ((my_dp + s + 1) % n_dp) * cols
        for half in range(2):
            out_ref[:, half * cols : (half + 1) * cols] = rows_ref[
                spot, pl.ds(pl.multiple_of(half * width + at, 128), cols)
            ]


def load_kernel(after_ref, gates_hbm, upper_hbm, lower_hbm, gates_ref, upper_ref, lower_ref, sems):
    copies = [
        pltpu.make_async_copy(source, target, sems.at[k])
        for k, (source, target) in enumerate(
            ((gates_hbm, gates_ref), (upper_hbm, upper_ref), (lower_hbm, lower_ref))
        )
    ]
    for copy in copies:
        copy.start()
    for copy in copies:
        copy.wait()


def factor_kernel(after_ref, gates_ref, rows_ref, upper_ref, lower_ref, out_ref):
    n_exp = gates_ref.shape[2]
    width, units = upper_ref.shape[1:]
    me = lax.axis_index("expert")
    gate = column(gates_ref, [(me + n_exp - s) % n_exp for s in range(n_exp)])
    pre = jnp.dot(rows_ref[:, :width], upper_ref[0], preferred_element_type=jnp.float32)
    back = jnp.dot(rows_ref[:, width:], lower_ref[0], preferred_element_type=jnp.float32)
    value, slope = gelu_pair(pre)
    out_ref[:, :units] = (back * gate * slope).astype(jnp.bfloat16)
    out_ref[:, units:] = (value * gate).astype(jnp.bfloat16)


def piece_kernel(n_hid, factor_ref, upper_ref, out_ref):
    n_pick, part = out_ref.shape[1:]
    width, units = upper_ref.shape[1:]
    n_exp = out_ref.shape[0] // n_hid
    me = lax.axis_index("expert")
    piece = lax.dot_general(
        factor_ref[:, :units], upper_ref[0], (((1,), (1,)), ((), ())), preferred_element_type=jnp.float32
    )
    for s in range(n_exp):
        owner = ((me + n_exp - s) % n_exp) * n_hid
        for h in range(n_hid):
            out_ref[owner + h] = piece[
                s * n_pick : (s + 1) * n_pick, h * part : (h + 1) * part
            ].astype(jnp.bfloat16)


def weight_kernel(chunks, shape, own_ref, *refs):
    n_dp, n_hid = shape
    part_refs, refs = refs[:n_hid], refs[n_hid:]
    factor_ref, up_ref, down_ref, side_ref, held, sems = refs
    units = factor_ref.shape[1] // 2
    cols = side_ref.shape[1] // 2
    width = own_ref.shape[1] // 2
    slots = own_ref.shape[0]
    rows = slots // n_hid
    my_hid = lax.axis_index("hidden")
    start = lax.axis_index("dp") * cols
    for half in range(2):
        side_ref[:slots, half * cols : (half + 1) * cols] = own_ref[
            :, pl.ds(pl.multiple_of(half * width + start, 128), cols)
        ]
    for t, part in enumerate(part_refs):
        spot = ((my_hid + n_hid - t) % n_hid) * rows
        for s in range(1, n_dp):
            side_ref[pl.ds(pl.multiple_of(s * slots + spot, 16), rows), :] = part[s - 1]
    step = units // chunks
    copies = []
    for which, out in ((0, up_ref), (1, down_ref)):
        for c in range(chunks):
            spot = pl.ds(c * step, step)
            held[which, :, spot] = lax.dot_general(
                side_ref[:, which * cols : (which + 1) * cols],
                factor_ref[:, pl.ds(which * units + c * step, step)],
                (((0,), (0,)), ((), ())),
                preferred_element_type=jnp.float32,
            )
            copy = pltpu.make_async_copy(
                held.at[which, :, spot], out.at[0, :, spot], sems.at[which, c]
            )
            copy.start()
            copies.append(copy)
    for copy in copies:
        copy.wait()


VMEM = pl.BlockSpec(memory_space=pltpu.VMEM)
ANY = pl.BlockSpec(memory_space=pl.ANY)
HBM = pl.BlockSpec(memory_space=pltpu.HBM)
ROOM = pltpu.CompilerParams(vmem_limit_bytes=16 << 20)


def local(layer_input, grad_out, picks, gates, w_up, w_down):
    tok_dev, width = layer_input.shape[1:]
    n_exp, n_pick = picks.shape[2:]
    slots = n_exp * n_pick
    units = w_up.shape[2]
    n_dp = lax.axis_size("dp")
    n_hid = lax.axis_size("hidden")
    cols = width // n_dp
    part = width // n_hid
    bf16 = jnp.bfloat16
    layer_input, grad_out, picks, gates, w_up, w_down = (
        pltpu.with_memory_space_constraint(x, pltpu.HBM)
        for x in (layer_input, grad_out, picks, gates, w_up, w_down)
    )

    send, spread = pl.pallas_call(
        functools.partial(pick_kernel, n_hid),
        out_shape=[
            jax.ShapeDtypeStruct((slots, 2 * width), bf16),
            jax.ShapeDtypeStruct((slots * n_hid, tok_dev), bf16),
        ],
        in_specs=[HBM] * 3,
        out_specs=[VMEM] * 2,
        scratch_shapes=[
            pltpu.VMEM(picks.shape, jnp.int32),
            pltpu.VMEM(layer_input.shape, bf16),
            pltpu.VMEM(grad_out.shape, bf16),
            pltpu.SemaphoreType.DMA((3,)),
        ],
        compiler_params=ROOM,
        name="pick",
    )(picks, layer_input, grad_out)

    rows = jnp.concatenate(
        [hop(send[s * n_pick : (s + 1) * n_pick], "expert", s) for s in range(n_exp)], axis=0
    )
    gate_held, upper, lower = pl.pallas_call(
        load_kernel,
        out_shape=[jax.ShapeDtypeStruct(x.shape, x.dtype) for x in (gates, w_up, w_down)],
        in_specs=[HBM] * 4,
        out_specs=[VMEM] * 3,
        scratch_shapes=[pltpu.SemaphoreType.DMA((3,))],
        cost_estimate=pl.CostEstimate(
            flops=0, bytes_accessed=4 * w_up.size + 4 * w_down.size, transcendentals=0
        ),
        compiler_params=ROOM,
        name="load",
    )(send, gates, w_up, w_down)
    share = slots // n_hid
    parts = pl.pallas_call(
        cut_kernel,
        out_shape=[jax.ShapeDtypeStruct((share, 2 * cols), bf16)] * (n_dp - 1),
        in_specs=[ANY, VMEM],
        out_specs=[VMEM] * (n_dp - 1),
        compiler_params=ROOM,
        name="cut",
    )(gate_held, rows)
    parts = [hop(x, "dp", s + 1) for s, x in enumerate(parts)]

    factors = pl.pallas_call(
        factor_kernel,
        out_shape=jax.ShapeDtypeStruct((slots, 2 * units), bf16),
        in_specs=[ANY] + [VMEM] * 4,
        out_specs=VMEM,
        compiler_params=ROOM,
        cost_estimate=pl.CostEstimate(
            flops=4 * slots * w_up.size, bytes_accessed=4 * w_up.size, transcendentals=slots * units
        ),
        name="factor",
    )(parts[0], gate_held, rows, upper, lower)
    parts = jnp.stack(parts)
    parts = [hop(parts, "hidden", t) for t in range(n_hid)]

    gathered = jnp.concatenate([hop(factors, "dp", s) for s in range(n_dp)], axis=0)

    piece = pl.pallas_call(
        functools.partial(piece_kernel, n_hid),
        out_shape=jax.ShapeDtypeStruct((n_exp * n_hid, n_pick, part), bf16),
        in_specs=[VMEM, VMEM],
        out_specs=VMEM,
        compiler_params=ROOM,
        cost_estimate=pl.CostEstimate(
            flops=2 * slots * w_up.size, bytes_accessed=2 * w_up.size, transcendentals=0
        ),
        name="piece",
    )(factors, upper)
    returned = lax.all_to_all(piece, ("expert", "hidden"), 0, 0)
    grad_rows = lax.dot_general(
        spread,
        returned.reshape(slots * n_hid, part),
        (((0,), (0,)), ((), ())),
        preferred_element_type=jnp.float32,
    ).astype(bf16)

    chunks = max(1, units // 256)
    grads = pl.pallas_call(
        functools.partial(weight_kernel, chunks, (n_dp, n_hid)),
        out_shape=[jax.ShapeDtypeStruct((1, cols, units), jnp.float32)] * 2,
        in_specs=[VMEM] * (n_hid + 2),
        out_specs=[HBM] * 2,
        scratch_shapes=[
            pltpu.VMEM((n_dp * slots, 2 * cols), bf16),
            pltpu.VMEM((2, cols, units), jnp.float32),
            pltpu.SemaphoreType.DMA((2, chunks)),
        ],
        compiler_params=ROOM,
        cost_estimate=pl.CostEstimate(
            flops=4 * n_dp * slots * cols * units, bytes_accessed=64 * cols * units, transcendentals=0
        ),
        name="weight",
    )(rows, *parts, gathered)
    return (grad_rows[None], *grads)


def solution(mesh):
    placed = (
        P("dp", "expert", None),
        P("dp", "expert", None),
        P("dp", "expert", None, None),
        P("dp", "expert", None, None),
        P("expert", None, "hidden"),
        P("expert", None, "hidden"),
    )
    return jax.shard_map(
        local,
        mesh=mesh,
        in_specs=placed,
        out_specs=(
            P("dp", "expert", "hidden"),
            P("expert", "dp", "hidden"),
            P("expert", "dp", "hidden"),
        ),
        check_vma=False,
    )
```

```python
import functools

import jax
import jax.numpy as jnp
from jax import lax
from jax.experimental import pallas as pl
from jax.experimental.pallas import tpu as pltpu
from jax.sharding import PartitionSpec as P

ROOT_TERM = 0.7978845608028654
CUBIC_TERM = 0.044715


def gelu_pair(pre):
    square = pre * pre
    inner = jnp.tanh(ROOT_TERM * (pre + CUBIC_TERM * square * pre))
    value = 0.5 * pre * (1.0 + inner)
    slope = 0.5 * (1.0 + inner) + 0.5 * pre * (1.0 - inner * inner) * ROOT_TERM * (
        1.0 + 3.0 * CUBIC_TERM * square
    )
    return value, slope


def hop(x, axis, step):
    n = lax.axis_size(axis)
    if step % n == 0:
        return x
    return lax.ppermute(x, axis, [(i, (i + step) % n) for i in range(n)])


def column(ref, order):
    n = ref.shape[-1]
    down = lax.broadcasted_iota(jnp.int32, (n, n), 0)
    along = lax.broadcasted_iota(jnp.int32, (n, n), 1)
    out = []
    for at in order:
        row = ref[0, 0, pl.ds(at, 1), :].astype(jnp.float32)
        out.append(jnp.sum(jnp.where(down == along, row, 0.0), axis=1, keepdims=True))
    return jnp.concatenate(out, axis=0)


def pick_kernel(n_hid, picks_hbm, tokens_hbm, upstream_hbm, rows_ref, spread_ref, *refs):
    picks_ref, tokens_ref, upstream_ref, sems = refs
    n_exp = picks_ref.shape[2]
    tok_dev, width = tokens_ref.shape[1:]
    copies = [
        pltpu.make_async_copy(picks_hbm, picks_ref, sems.at[0]),
        pltpu.make_async_copy(tokens_hbm, tokens_ref, sems.at[1]),
        pltpu.make_async_copy(upstream_hbm, upstream_ref, sems.at[2]),
    ]
    for copy in copies:
        copy.start()
    me = lax.axis_index("expert")
    copies[0].wait()

    def one_hot(order):
        wanted = column(picks_ref, order).astype(jnp.int32)
        spots = lax.broadcasted_iota(jnp.int32, (wanted.shape[0], tok_dev), 1)
        return jnp.where(wanted == spots, 1.0, 0.0).astype(jnp.bfloat16)

    selector = one_hot([(me + s) % n_exp for s in range(n_exp)])
    spread_ref[...] = one_hot([e for e in range(n_exp) for _ in range(n_hid)])
    for at, copy, source in ((0, copies[1], tokens_ref), (width, copies[2], upstream_ref)):
        copy.wait()
        rows_ref[:, at : at + width] = jnp.dot(
            selector, source[0], preferred_element_type=jnp.float32
        ).astype(jnp.bfloat16)


def cut_kernel(after_ref, rows_ref, *out_refs):
    n_dp = len(out_refs) + 1
    cols = out_refs[0].shape[1] // 2
    width = rows_ref.shape[1] // 2
    my_dp = lax.axis_index("dp")
    for s, out_ref in enumerate(out_refs):
        at = ((my_dp + s + 1) % n_dp) * cols
        for half in range(2):
            out_ref[:, half * cols : (half + 1) * cols] = rows_ref[
                :, pl.ds(pl.multiple_of(half * width + at, 128), cols)
            ]


def load_kernel(after_ref, gates_hbm, upper_hbm, lower_hbm, gates_ref, upper_ref, lower_ref, sems):
    copies = [
        pltpu.make_async_copy(source, target, sems.at[k])
        for k, (source, target) in enumerate(
            ((gates_hbm, gates_ref), (upper_hbm, upper_ref), (lower_hbm, lower_ref))
        )
    ]
    for copy in copies:
        copy.start()
    for copy in copies:
        copy.wait()


def factor_kernel(after_ref, gates_ref, rows_ref, upper_ref, lower_ref, out_ref):
    n_exp = gates_ref.shape[2]
    width, units = upper_ref.shape[1:]
    me = lax.axis_index("expert")
    gate = column(gates_ref, [(me + n_exp - s) % n_exp for s in range(n_exp)])
    pre = jnp.dot(rows_ref[:, :width], upper_ref[0], preferred_element_type=jnp.float32)
    back = jnp.dot(rows_ref[:, width:], lower_ref[0], preferred_element_type=jnp.float32)
    value, slope = gelu_pair(pre)
    out_ref[:, :units] = (back * gate * slope).astype(jnp.bfloat16)
    out_ref[:, units:] = (value * gate).astype(jnp.bfloat16)


def piece_kernel(n_hid, factor_ref, upper_ref, *refs):
    out_ref = refs[-1]
    n_pick, part = out_ref.shape[1:]
    width, units = upper_ref.shape[1:]
    n_exp = out_ref.shape[0] // n_hid
    me = lax.axis_index("expert")
    piece = lax.dot_general(
        factor_ref[:, :units], upper_ref[0], (((1,), (1,)), ((), ())), preferred_element_type=jnp.float32
    )
    for s in range(n_exp):
        owner = ((me + n_exp - s) % n_exp) * n_hid
        for h in range(n_hid):
            out_ref[owner + h] = piece[
                s * n_pick : (s + 1) * n_pick, h * part : (h + 1) * part
            ].astype(jnp.bfloat16)


def weight_kernel(chunks, n_dp, own_ref, *refs):
    part_refs, refs = refs[: n_dp - 1], refs[n_dp - 1 :]
    factor_ref, up_ref, down_ref, side_ref, held, sems = refs
    units = factor_ref.shape[1] // 2
    cols = side_ref.shape[1] // 2
    width = own_ref.shape[1] // 2
    slots = own_ref.shape[0]
    start = lax.axis_index("dp") * cols
    for half in range(2):
        side_ref[:slots, half * cols : (half + 1) * cols] = own_ref[
            :, pl.ds(pl.multiple_of(half * width + start, 128), cols)
        ]
    for s, part in enumerate(part_refs):
        side_ref[(s + 1) * slots : (s + 2) * slots, :] = part[...]
    step = units // chunks
    copies = []
    for which, out in ((0, up_ref), (1, down_ref)):
        for c in range(chunks):
            spot = pl.ds(c * step, step)
            held[which, :, spot] = lax.dot_general(
                side_ref[:, which * cols : (which + 1) * cols],
                factor_ref[:, pl.ds(which * units + c * step, step)],
                (((0,), (0,)), ((), ())),
                preferred_element_type=jnp.float32,
            )
            copy = pltpu.make_async_copy(
                held.at[which, :, spot], out.at[0, :, spot], sems.at[which, c]
            )
            copy.start()
            copies.append(copy)
    for copy in copies:
        copy.wait()


VMEM = pl.BlockSpec(memory_space=pltpu.VMEM)
ANY = pl.BlockSpec(memory_space=pl.ANY)
HBM = pl.BlockSpec(memory_space=pltpu.HBM)
ROOM = pltpu.CompilerParams(vmem_limit_bytes=16 << 20)


def local(layer_input, grad_out, picks, gates, w_up, w_down):
    tok_dev, width = layer_input.shape[1:]
    n_exp, n_pick = picks.shape[2:]
    slots = n_exp * n_pick
    units = w_up.shape[2]
    n_dp = lax.axis_size("dp")
    n_hid = lax.axis_size("hidden")
    cols = width // n_dp
    part = width // n_hid
    bf16 = jnp.bfloat16
    layer_input, grad_out, picks, gates, w_up, w_down = (
        pltpu.with_memory_space_constraint(x, pltpu.HBM)
        for x in (layer_input, grad_out, picks, gates, w_up, w_down)
    )

    send, spread = pl.pallas_call(
        functools.partial(pick_kernel, n_hid),
        out_shape=[
            jax.ShapeDtypeStruct((slots, 2 * width), bf16),
            jax.ShapeDtypeStruct((slots * n_hid, tok_dev), bf16),
        ],
        in_specs=[HBM] * 3,
        out_specs=[VMEM] * 2,
        scratch_shapes=[
            pltpu.VMEM(picks.shape, jnp.int32),
            pltpu.VMEM(layer_input.shape, bf16),
            pltpu.VMEM(grad_out.shape, bf16),
            pltpu.SemaphoreType.DMA((3,)),
        ],
        compiler_params=ROOM,
        name="pick",
    )(picks, layer_input, grad_out)

    rows = jnp.concatenate(
        [hop(send[s * n_pick : (s + 1) * n_pick], "expert", s) for s in range(n_exp)], axis=0
    )
    gate_held, upper, lower = pl.pallas_call(
        load_kernel,
        out_shape=[jax.ShapeDtypeStruct(x.shape, x.dtype) for x in (gates, w_up, w_down)],
        in_specs=[HBM] * 4,
        out_specs=[VMEM] * 3,
        scratch_shapes=[pltpu.SemaphoreType.DMA((3,))],
        cost_estimate=pl.CostEstimate(
            flops=0, bytes_accessed=4 * w_up.size + 4 * w_down.size, transcendentals=0
        ),
        compiler_params=ROOM,
        name="load",
    )(send, gates, w_up, w_down)
    parts = pl.pallas_call(
        cut_kernel,
        out_shape=[jax.ShapeDtypeStruct((slots, 2 * cols), bf16)] * (n_dp - 1),
        in_specs=[ANY, VMEM],
        out_specs=[VMEM] * (n_dp - 1),
        compiler_params=ROOM,
        name="cut",
    )(gate_held, rows)
    parts = [hop(x, "dp", s + 1) for s, x in enumerate(parts)]

    factors = pl.pallas_call(
        factor_kernel,
        out_shape=jax.ShapeDtypeStruct((slots, 2 * units), bf16),
        in_specs=[ANY] + [VMEM] * 4,
        out_specs=VMEM,
        compiler_params=ROOM,
        cost_estimate=pl.CostEstimate(
            flops=4 * slots * w_up.size, bytes_accessed=4 * w_up.size, transcendentals=slots * units
        ),
        name="factor",
    )(parts[0], gate_held, rows, upper, lower)

    gathered = jnp.concatenate([hop(factors, "dp", s) for s in range(n_dp)], axis=0)

    piece = pl.pallas_call(
        functools.partial(piece_kernel, n_hid),
        out_shape=jax.ShapeDtypeStruct((n_exp * n_hid, n_pick, part), bf16),
        in_specs=[VMEM, VMEM] + [ANY] * (n_dp - 2),
        out_specs=VMEM,
        compiler_params=ROOM,
        cost_estimate=pl.CostEstimate(
            flops=2 * slots * w_up.size, bytes_accessed=2 * w_up.size, transcendentals=0
        ),
        name="piece",
    )(factors, upper, *parts[1:])
    returned = lax.all_to_all(piece, ("expert", "hidden"), 0, 0)
    chunks = max(1, units // 256)
    grads = pl.pallas_call(
        functools.partial(weight_kernel, chunks, n_dp),
        out_shape=[jax.ShapeDtypeStruct((1, cols, units), jnp.float32)] * 2,
        in_specs=[VMEM] * (n_dp + 1),
        out_specs=[HBM] * 2,
        scratch_shapes=[
            pltpu.VMEM((n_dp * slots, 2 * cols), bf16),
            pltpu.VMEM((2, cols, units), jnp.float32),
            pltpu.SemaphoreType.DMA((2, chunks)),
        ],
        compiler_params=ROOM,
        cost_estimate=pl.CostEstimate(
            flops=4 * n_dp * slots * cols * units, bytes_accessed=64 * cols * units, transcendentals=0
        ),
        name="weight",
    )(rows, *parts, gathered)
    grad_rows = lax.dot_general(
        spread,
        returned.reshape(slots * n_hid, part),
        (((0,), (0,)), ((), ())),
        preferred_element_type=jnp.float32,
    ).astype(bf16)
    return (grad_rows[None], *grads)


def solution(mesh):
    placed = (
        P("dp", "expert", None),
        P("dp", "expert", None),
        P("dp", "expert", None, None),
        P("dp", "expert", None, None),
        P("expert", None, "hidden"),
        P("expert", None, "hidden"),
    )
    return jax.shard_map(
        local,
        mesh=mesh,
        in_specs=placed,
        out_specs=(
            P("dp", "expert", "hidden"),
            P("expert", "dp", "hidden"),
            P("expert", "dp", "hidden"),
        ),
        check_vma=False,
    )
```

```python
import functools

import jax
import jax.numpy as jnp
from jax import lax
from jax.experimental import pallas as pl
from jax.experimental.pallas import tpu as pltpu
from jax.sharding import PartitionSpec as P

ROOT_TERM = 0.7978845608028654
CUBIC_TERM = 0.044715


def gelu_pair(pre):
    square = pre * pre
    inner = jnp.tanh(ROOT_TERM * (pre + CUBIC_TERM * square * pre))
    value = 0.5 * pre * (1.0 + inner)
    slope = 0.5 * (1.0 + inner) + 0.5 * pre * (1.0 - inner * inner) * ROOT_TERM * (
        1.0 + 3.0 * CUBIC_TERM * square
    )
    return value, slope


def hop(x, axis, step):
    n = lax.axis_size(axis)
    if step % n == 0:
        return x
    return lax.ppermute(x, axis, [(i, (i + step) % n) for i in range(n)])


def column(ref, order):
    n = ref.shape[-1]
    down = lax.broadcasted_iota(jnp.int32, (n, n), 0)
    along = lax.broadcasted_iota(jnp.int32, (n, n), 1)
    out = []
    for at in order:
        row = ref[0, 0, pl.ds(at, 1), :].astype(jnp.float32)
        out.append(jnp.sum(jnp.where(down == along, row, 0.0), axis=1, keepdims=True))
    return jnp.concatenate(out, axis=0)


def pick_kernel(n_hid, picks_hbm, tokens_hbm, upstream_hbm, rows_ref, spread_ref, *refs):
    picks_ref, tokens_ref, upstream_ref, sems = refs
    n_exp = picks_ref.shape[2]
    tok_dev, width = tokens_ref.shape[1:]
    copies = [
        pltpu.make_async_copy(picks_hbm, picks_ref, sems.at[0]),
        pltpu.make_async_copy(tokens_hbm, tokens_ref, sems.at[1]),
        pltpu.make_async_copy(upstream_hbm, upstream_ref, sems.at[2]),
    ]
    for copy in copies:
        copy.start()
    me = lax.axis_index("expert")
    copies[0].wait()

    def one_hot(order):
        wanted = column(picks_ref, order).astype(jnp.int32)
        spots = lax.broadcasted_iota(jnp.int32, (wanted.shape[0], tok_dev), 1)
        return jnp.where(wanted == spots, 1.0, 0.0).astype(jnp.bfloat16)

    selector = one_hot([(me + s) % n_exp for s in range(n_exp)])
    spread_ref[...] = one_hot([e for e in range(n_exp) for _ in range(n_hid)])
    for at, copy, source in ((0, copies[1], tokens_ref), (width, copies[2], upstream_ref)):
        copy.wait()
        rows_ref[:, at : at + width] = jnp.dot(
            selector, source[0], preferred_element_type=jnp.float32
        ).astype(jnp.bfloat16)


def cut_kernel(after_ref, rows_ref, *out_refs):
    n_dp = len(out_refs) + 1
    share, wide = out_refs[0].shape
    cols = wide // 2
    width = rows_ref.shape[1] // 2
    my_dp = lax.axis_index("dp")
    spot = pl.ds(pl.multiple_of(lax.axis_index("hidden") * share, 16), share)
    for s, out_ref in enumerate(out_refs):
        at = ((my_dp + s + 1) % n_dp) * cols
        for half in range(2):
            out_ref[:, half * cols : (half + 1) * cols] = rows_ref[
                spot, pl.ds(pl.multiple_of(half * width + at, 128), cols)
            ]


def load_kernel(after_ref, gates_hbm, upper_hbm, lower_hbm, gates_ref, upper_ref, lower_ref, sems):
    copies = [
        pltpu.make_async_copy(source, target, sems.at[k])
        for k, (source, target) in enumerate(
            ((gates_hbm, gates_ref), (upper_hbm, upper_ref), (lower_hbm, lower_ref))
        )
    ]
    for copy in copies:
        copy.start()
    for copy in copies:
        copy.wait()


def factor_kernel(after_ref, gates_ref, rows_ref, upper_ref, lower_ref, out_ref):
    n_exp = gates_ref.shape[2]
    width, units = upper_ref.shape[1:]
    me = lax.axis_index("expert")
    gate = column(gates_ref, [(me + n_exp - s) % n_exp for s in range(n_exp)])
    pre = jnp.dot(rows_ref[:, :width], upper_ref[0], preferred_element_type=jnp.float32)
    back = jnp.dot(rows_ref[:, width:], lower_ref[0], preferred_element_type=jnp.float32)
    value, slope = gelu_pair(pre)
    out_ref[:, :units] = (back * gate * slope).astype(jnp.bfloat16)
    out_ref[:, units:] = (value * gate).astype(jnp.bfloat16)


def piece_kernel(n_hid, factor_ref, upper_ref, *refs):
    out_ref = refs[-1]
    n_pick, part = out_ref.shape[1:]
    width, units = upper_ref.shape[1:]
    n_exp = out_ref.shape[0] // n_hid
    me = lax.axis_index("expert")
    piece = lax.dot_general(
        factor_ref[:, :units], upper_ref[0], (((1,), (1,)), ((), ())), preferred_element_type=jnp.float32
    )
    for s in range(n_exp):
        owner = ((me + n_exp - s) % n_exp) * n_hid
        for h in range(n_hid):
            out_ref[owner + h] = piece[
                s * n_pick : (s + 1) * n_pick, h * part : (h + 1) * part
            ].astype(jnp.bfloat16)


def weight_kernel(chunks, shape, own_ref, *refs):
    n_dp, n_hid = shape
    part_refs, refs = refs[:n_hid], refs[n_hid:]
    factor_ref, up_ref, down_ref, side_ref, held, sems = refs
    units = factor_ref.shape[1] // 2
    cols = side_ref.shape[1] // 2
    width = own_ref.shape[1] // 2
    slots = own_ref.shape[0]
    rows = slots // n_hid
    my_hid = lax.axis_index("hidden")
    start = lax.axis_index("dp") * cols
    for half in range(2):
        side_ref[:slots, half * cols : (half + 1) * cols] = own_ref[
            :, pl.ds(pl.multiple_of(half * width + start, 128), cols)
        ]
    for t, part in enumerate(part_refs):
        spot = ((my_hid + n_hid - t) % n_hid) * rows
        for s in range(1, n_dp):
            side_ref[pl.ds(pl.multiple_of(s * slots + spot, 16), rows), :] = part[s - 1]
    step = units // chunks
    copies = []
    for which, out in ((0, up_ref), (1, down_ref)):
        for c in range(chunks):
            spot = pl.ds(c * step, step)
            held[which, :, spot] = lax.dot_general(
                side_ref[:, which * cols : (which + 1) * cols],
                factor_ref[:, pl.ds(which * units + c * step, step)],
                (((0,), (0,)), ((), ())),
                preferred_element_type=jnp.float32,
            )
            copy = pltpu.make_async_copy(
                held.at[which, :, spot], out.at[0, :, spot], sems.at[which, c]
            )
            copy.start()
            copies.append(copy)
    for copy in copies:
        copy.wait()


VMEM = pl.BlockSpec(memory_space=pltpu.VMEM)
ANY = pl.BlockSpec(memory_space=pl.ANY)
HBM = pl.BlockSpec(memory_space=pltpu.HBM)
ROOM = pltpu.CompilerParams(vmem_limit_bytes=16 << 20)


def local(layer_input, grad_out, picks, gates, w_up, w_down):
    tok_dev, width = layer_input.shape[1:]
    n_exp, n_pick = picks.shape[2:]
    slots = n_exp * n_pick
    units = w_up.shape[2]
    n_dp = lax.axis_size("dp")
    n_hid = lax.axis_size("hidden")
    cols = width // n_dp
    part = width // n_hid
    bf16 = jnp.bfloat16
    layer_input, grad_out, picks, gates, w_up, w_down = (
        pltpu.with_memory_space_constraint(x, pltpu.HBM)
        for x in (layer_input, grad_out, picks, gates, w_up, w_down)
    )

    send, spread = pl.pallas_call(
        functools.partial(pick_kernel, n_hid),
        out_shape=[
            jax.ShapeDtypeStruct((slots, 2 * width), bf16),
            jax.ShapeDtypeStruct((slots * n_hid, tok_dev), bf16),
        ],
        in_specs=[HBM] * 3,
        out_specs=[VMEM] * 2,
        scratch_shapes=[
            pltpu.VMEM(picks.shape, jnp.int32),
            pltpu.VMEM(layer_input.shape, bf16),
            pltpu.VMEM(grad_out.shape, bf16),
            pltpu.SemaphoreType.DMA((3,)),
        ],
        compiler_params=ROOM,
        name="pick",
    )(picks, layer_input, grad_out)

    rows = jnp.concatenate(
        [hop(send[s * n_pick : (s + 1) * n_pick], "expert", s) for s in range(n_exp)], axis=0
    )
    gate_held, upper, lower = pl.pallas_call(
        load_kernel,
        out_shape=[jax.ShapeDtypeStruct(x.shape, x.dtype) for x in (gates, w_up, w_down)],
        in_specs=[HBM] * 4,
        out_specs=[VMEM] * 3,
        scratch_shapes=[pltpu.SemaphoreType.DMA((3,))],
        cost_estimate=pl.CostEstimate(
            flops=0, bytes_accessed=4 * w_up.size + 4 * w_down.size, transcendentals=0
        ),
        compiler_params=ROOM,
        name="load",
    )(send, gates, w_up, w_down)
    share = slots // n_hid
    parts = pl.pallas_call(
        cut_kernel,
        out_shape=[jax.ShapeDtypeStruct((share, 2 * cols), bf16)] * (n_dp - 1),
        in_specs=[ANY, VMEM],
        out_specs=[VMEM] * (n_dp - 1),
        compiler_params=ROOM,
        name="cut",
    )(gate_held, rows)
    parts = [hop(x, "dp", s + 1) for s, x in enumerate(parts)]

    factors = pl.pallas_call(
        factor_kernel,
        out_shape=jax.ShapeDtypeStruct((slots, 2 * units), bf16),
        in_specs=[ANY] + [VMEM] * 4,
        out_specs=VMEM,
        compiler_params=ROOM,
        cost_estimate=pl.CostEstimate(
            flops=4 * slots * w_up.size, bytes_accessed=4 * w_up.size, transcendentals=slots * units
        ),
        name="factor",
    )(parts[0], gate_held, rows, upper, lower)
    parts = jnp.stack(parts)
    parts = [hop(parts, "hidden", t) for t in range(n_hid)]

    gathered = jnp.concatenate([hop(factors, "dp", s) for s in range(n_dp)], axis=0)

    piece = pl.pallas_call(
        functools.partial(piece_kernel, n_hid),
        out_shape=jax.ShapeDtypeStruct((n_exp * n_hid, n_pick, part), bf16),
        in_specs=[VMEM, VMEM] + [ANY] * n_hid,
        out_specs=VMEM,
        compiler_params=ROOM,
        cost_estimate=pl.CostEstimate(
            flops=2 * slots * w_up.size, bytes_accessed=2 * w_up.size, transcendentals=0
        ),
        name="piece",
    )(factors, upper, *parts)
    returned = lax.all_to_all(piece, ("expert", "hidden"), 0, 0)
    grad_rows = lax.dot_general(
        spread,
        returned.reshape(slots * n_hid, part),
        (((0,), (0,)), ((), ())),
        preferred_element_type=jnp.float32,
    ).astype(bf16)

    chunks = max(1, units // 256)
    grads = pl.pallas_call(
        functools.partial(weight_kernel, chunks, (n_dp, n_hid)),
        out_shape=[jax.ShapeDtypeStruct((1, cols, units), jnp.float32)] * 2,
        in_specs=[VMEM] * (n_hid + 2),
        out_specs=[HBM] * 2,
        scratch_shapes=[
            pltpu.VMEM((n_dp * slots, 2 * cols), bf16),
            pltpu.VMEM((2, cols, units), jnp.float32),
            pltpu.SemaphoreType.DMA((2, chunks)),
        ],
        compiler_params=ROOM,
        cost_estimate=pl.CostEstimate(
            flops=4 * n_dp * slots * cols * units, bytes_accessed=64 * cols * units, transcendentals=0
        ),
        name="weight",
    )(rows, *parts, gathered)
    return (grad_rows[None], *grads)


def solution(mesh):
    placed = (
        P("dp", "expert", None),
        P("dp", "expert", None),
        P("dp", "expert", None, None),
        P("dp", "expert", None, None),
        P("expert", None, "hidden"),
        P("expert", None, "hidden"),
    )
    return jax.shard_map(
        local,
        mesh=mesh,
        in_specs=placed,
        out_specs=(
            P("dp", "expert", "hidden"),
            P("expert", "dp", "hidden"),
            P("expert", "dp", "hidden"),
        ),
        check_vma=False,
    )
```

```python
import functools

import jax
import jax.numpy as jnp
from jax import lax
from jax.experimental import pallas as pl
from jax.experimental.pallas import tpu as pltpu
from jax.sharding import PartitionSpec as P

ROOT_TERM = 0.7978845608028654
CUBIC_TERM = 0.044715


def gelu_pair(pre):
    square = pre * pre
    inner = jnp.tanh(ROOT_TERM * (pre + CUBIC_TERM * square * pre))
    value = 0.5 * pre * (1.0 + inner)
    slope = 0.5 * (1.0 + inner) + 0.5 * pre * (1.0 - inner * inner) * ROOT_TERM * (
        1.0 + 3.0 * CUBIC_TERM * square
    )
    return value, slope


def hop(x, axis, step):
    n = lax.axis_size(axis)
    if step % n == 0:
        return x
    return lax.ppermute(x, axis, [(i, (i + step) % n) for i in range(n)])


def column(ref, order):
    n = ref.shape[-1]
    down = lax.broadcasted_iota(jnp.int32, (n, n), 0)
    along = lax.broadcasted_iota(jnp.int32, (n, n), 1)
    out = []
    for at in order:
        row = ref[0, 0, pl.ds(at, 1), :].astype(jnp.float32)
        out.append(jnp.sum(jnp.where(down == along, row, 0.0), axis=1, keepdims=True))
    return jnp.concatenate(out, axis=0)


def pick_kernel(n_hid, n_share, picks_hbm, tokens_hbm, upstream_hbm, rows_ref, spread_ref, *refs):
    *side_refs, picks_ref, tokens_ref, upstream_ref, sems = refs
    n_exp = picks_ref.shape[2]
    tok_dev, width = tokens_ref.shape[1:]
    copies = [
        pltpu.make_async_copy(picks_hbm, picks_ref, sems.at[0]),
        pltpu.make_async_copy(tokens_hbm, tokens_ref, sems.at[1]),
        pltpu.make_async_copy(upstream_hbm, upstream_ref, sems.at[2]),
    ]
    for copy in copies:
        copy.start()
    me = lax.axis_index("expert")
    copies[0].wait()

    def one_hot(order):
        wanted = column(picks_ref, order).astype(jnp.int32)
        spots = lax.broadcasted_iota(jnp.int32, (wanted.shape[0], tok_dev), 1)
        return jnp.where(wanted == spots, 1.0, 0.0).astype(jnp.bfloat16)

    selector = one_hot([(me + s) % n_exp for s in range(n_exp)])
    spread_ref[...] = one_hot([e for e in range(n_exp) for _ in range(n_hid)])
    for at, copy, source in ((0, copies[1], tokens_ref), (width, copies[2], upstream_ref)):
        copy.wait()
        rows_ref[:, at : at + width] = jnp.dot(
            selector, source[0], preferred_element_type=jnp.float32
        ).astype(jnp.bfloat16)
    n_dp = len(side_refs) + 1
    cols = width // n_dp
    span = side_refs[0].shape[1]
    my_dp = lax.axis_index("dp")
    if n_share == 1:
        starts = [0, width]
    else:
        per_half = n_share // 2
        share = lax.axis_index("hidden")
        starts = [(share // per_half) * width + (share % per_half) * span]
    wide = span // len(starts)
    for s in range(1, n_dp):
        at = ((my_dp + s) % n_dp) * cols
        for k, start in enumerate(starts):
            side_refs[s - 1][:, k * wide : (k + 1) * wide] = rows_ref[
                :, pl.ds(pl.multiple_of(start + at, 128), wide)
            ]


def load_kernel(chunks, after_ref, gates_hbm, upper_hbm, lower_hbm, gates_ref, upper_ref, lower_ref, sems):
    step = upper_ref.shape[1] // chunks
    copies = [pltpu.make_async_copy(gates_hbm, gates_ref, sems.at[2 * chunks])]
    for k, (source, target) in enumerate(((upper_hbm, upper_ref), (lower_hbm, lower_ref))):
        for c in range(chunks):
            spot = pl.ds(c * step, step)
            copies.append(
                pltpu.make_async_copy(
                    source.at[:, spot, :], target.at[:, spot, :], sems.at[k * chunks + c]
                )
            )
    for copy in copies:
        copy.start()
    for copy in copies:
        copy.wait()


def factor_kernel(gates_ref, rows_ref, upper_ref, lower_ref, *refs):
    out_ref = refs[-1]
    n_exp = gates_ref.shape[2]
    width, units = upper_ref.shape[1:]
    me = lax.axis_index("expert")
    gate = column(gates_ref, [(me + n_exp - s) % n_exp for s in range(n_exp)])
    pre = jnp.dot(rows_ref[:, :width], upper_ref[0], preferred_element_type=jnp.float32)
    back = jnp.dot(rows_ref[:, width:], lower_ref[0], preferred_element_type=jnp.float32)
    value, slope = gelu_pair(pre)
    out_ref[:, :units] = (back * gate * slope).astype(jnp.bfloat16)
    out_ref[:, units:] = (value * gate).astype(jnp.bfloat16)


def piece_kernel(n_hid, factor_ref, upper_ref, *refs):
    *side_refs, out_ref = refs
    n_pick = out_ref.shape[1]
    width, units = upper_ref.shape[1:]
    part = width // n_hid
    span = side_refs[0].shape[1]
    n_exp = out_ref.shape[0] // n_hid
    me = lax.axis_index("expert")
    for k, side in enumerate(side_refs):
        rows = side[...].astype(jnp.float32)
        for s in range(n_exp):
            block = rows[s * n_pick : (s + 1) * n_pick].astype(jnp.bfloat16)
            owner = ((me + s) % n_exp) * n_hid
            for h in range(n_hid):
                out_ref[owner + h, :, part + k * span : part + (k + 1) * span] = block
    piece = lax.dot_general(
        factor_ref[:, :units], upper_ref[0], (((1,), (1,)), ((), ())), preferred_element_type=jnp.float32
    )
    for s in range(n_exp):
        owner = ((me + n_exp - s) % n_exp) * n_hid
        for h in range(n_hid):
            out_ref[owner + h, :, :part] = piece[
                s * n_pick : (s + 1) * n_pick, h * part : (h + 1) * part
            ].astype(jnp.bfloat16)


def weight_kernel(chunks, n_dp, n_share, after_ref, own_ref, came_ref, factor_ref, *refs):
    up_ref, down_ref, side_ref, held, sems = refs
    slots = own_ref.shape[0]
    width = own_ref.shape[1] // 2
    units = factor_ref.shape[1] // 2
    cols = side_ref.shape[1] // 2
    span = 2 * cols // n_share
    n_pick = came_ref.shape[1]
    n_exp = slots // n_pick
    n_hid = came_ref.shape[0] // n_exp
    part = width // n_hid
    me = lax.axis_index("expert")
    start = lax.axis_index("dp") * cols
    for half in range(2):
        side_ref[:slots, half * cols : (half + 1) * cols] = own_ref[
            :, pl.ds(pl.multiple_of(half * width + start, 128), cols)
        ]
    for t in range(n_share):
        sender = lax.axis_index("hidden") if n_share == 1 else t
        for s in range(1, n_dp):
            spot = part + (s - 1) * span
            blocks = [
                came_ref[((me + n_exp - b) % n_exp) * n_hid + sender, :, spot : spot + span].astype(jnp.float32)
                for b in range(n_exp)
            ]
            side_ref[s * slots : (s + 1) * slots, t * span : (t + 1) * span] = jnp.concatenate(
                blocks, axis=0
            ).astype(jnp.bfloat16)
    step = units // chunks
    copies = []
    for which, out in ((0, up_ref), (1, down_ref)):
        for c in range(chunks):
            spot = pl.ds(c * step, step)
            held[which, :, spot] = lax.dot_general(
                side_ref[:, which * cols : (which + 1) * cols],
                factor_ref[:, pl.ds(which * units + c * step, step)],
                (((0,), (0,)), ((), ())),
                preferred_element_type=jnp.float32,
            )
            copy = pltpu.make_async_copy(
                held.at[which, :, spot], out.at[0, :, spot], sems.at[which, c]
            )
            copy.start()
            copies.append(copy)
    for copy in copies:
        copy.wait()


VMEM = pl.BlockSpec(memory_space=pltpu.VMEM)
ANY = pl.BlockSpec(memory_space=pl.ANY)
HBM = pl.BlockSpec(memory_space=pltpu.HBM)
ROOM = pltpu.CompilerParams(vmem_limit_bytes=16 << 20)


def local(layer_input, grad_out, picks, gates, w_up, w_down):
    tok_dev, width = layer_input.shape[1:]
    n_exp, n_pick = picks.shape[2:]
    slots = n_exp * n_pick
    units = w_up.shape[2]
    n_dp = lax.axis_size("dp")
    n_hid = lax.axis_size("hidden")
    cols = width // n_dp
    part = width // n_hid
    bf16 = jnp.bfloat16
    layer_input, grad_out, picks, gates, w_up, w_down = (
        pltpu.with_memory_space_constraint(x, pltpu.HBM)
        for x in (layer_input, grad_out, picks, gates, w_up, w_down)
    )

    n_share = n_hid if n_hid % 2 == 0 and 2 * cols % (n_hid * 128) == 0 else 1
    span = 2 * cols // n_share
    send, spread, *side = pl.pallas_call(
        functools.partial(pick_kernel, n_hid, n_share),
        out_shape=[
            jax.ShapeDtypeStruct((slots, 2 * width), bf16),
            jax.ShapeDtypeStruct((slots * n_hid, tok_dev), bf16),
        ]
        + [jax.ShapeDtypeStruct((slots, span), bf16)] * (n_dp - 1),
        in_specs=[HBM] * 3,
        out_specs=[VMEM] * (n_dp + 1),
        scratch_shapes=[
            pltpu.VMEM(picks.shape, jnp.int32),
            pltpu.VMEM(layer_input.shape, bf16),
            pltpu.VMEM(grad_out.shape, bf16),
            pltpu.SemaphoreType.DMA((3,)),
        ],
        compiler_params=ROOM,
        name="pick",
    )(picks, layer_input, grad_out)

    rows = jnp.concatenate(
        [hop(send[s * n_pick : (s + 1) * n_pick], "expert", s) for s in range(n_exp)], axis=0
    )
    side = [hop(x, "dp", s + 1) for s, x in enumerate(side)]

    splits = 4
    gate_held, upper, lower = pl.pallas_call(
        functools.partial(load_kernel, splits),
        out_shape=[jax.ShapeDtypeStruct(x.shape, x.dtype) for x in (gates, w_up, w_down)],
        in_specs=[HBM] * 4,
        out_specs=[VMEM] * 3,
        scratch_shapes=[pltpu.SemaphoreType.DMA((2 * splits + 1,))],
        compiler_params=ROOM,
        cost_estimate=pl.CostEstimate(
            flops=0, bytes_accessed=4 * w_up.size + 4 * w_down.size, transcendentals=0
        ),
        name="load",
    )(send, gates, w_up, w_down)
    factors = pl.pallas_call(
        factor_kernel,
        out_shape=jax.ShapeDtypeStruct((slots, 2 * units), bf16),
        in_specs=[VMEM] * 4 + [ANY] * (n_dp - 2),
        out_specs=VMEM,
        compiler_params=ROOM,
        cost_estimate=pl.CostEstimate(
            flops=4 * slots * w_up.size, bytes_accessed=4 * w_up.size, transcendentals=slots * units
        ),
        name="factor",
    )(gate_held, rows, upper, lower, *side[:-1])

    gathered = jnp.concatenate([hop(factors, "dp", s) for s in range(n_dp)], axis=0)

    piece = pl.pallas_call(
        functools.partial(piece_kernel, n_hid),
        out_shape=jax.ShapeDtypeStruct((n_exp * n_hid, n_pick, part + (n_dp - 1) * span), bf16),
        in_specs=[VMEM] * (n_dp + 1),
        out_specs=VMEM,
        compiler_params=ROOM,
        cost_estimate=pl.CostEstimate(
            flops=2 * slots * w_up.size, bytes_accessed=2 * w_up.size, transcendentals=0
        ),
        name="piece",
    )(factors, upper, *side)
    returned = lax.all_to_all(
        piece.transpose(1, 0, 2), ("expert", "hidden"), split_axis=1, concat_axis=1, tiled=True
    ).transpose(1, 0, 2)
    grad_rows = lax.dot_general(
        spread,
        returned[:, :, :part].reshape(slots * n_hid, part),
        (((0,), (0,)), ((), ())),
        preferred_element_type=jnp.float32,
    ).astype(bf16)

    chunks = max(1, units // 256)
    grads = pl.pallas_call(
        functools.partial(weight_kernel, chunks, n_dp, n_share),
        out_shape=[jax.ShapeDtypeStruct((1, cols, units), jnp.float32)] * 2,
        in_specs=[ANY] + [VMEM] * 3,
        out_specs=[HBM] * 2,
        scratch_shapes=[
            pltpu.VMEM((n_dp * slots, 2 * cols), bf16),
            pltpu.VMEM((2, cols, units), jnp.float32),
            pltpu.SemaphoreType.DMA((2, chunks)),
        ],
        compiler_params=ROOM,
        name="weight",
    )(grad_rows, rows, returned, gathered)
    return (grad_rows[None], *grads)


def solution(mesh):
    placed = (
        P("dp", "expert", None),
        P("dp", "expert", None),
        P("dp", "expert", None, None),
        P("dp", "expert", None, None),
        P("expert", None, "hidden"),
        P("expert", None, "hidden"),
    )
    return jax.shard_map(
        local,
        mesh=mesh,
        in_specs=placed,
        out_specs=(
            P("dp", "expert", "hidden"),
            P("expert", "dp", "hidden"),
            P("expert", "dp", "hidden"),
        ),
        check_vma=False,
    )
```

```python
import functools

import jax
import jax.numpy as jnp
from jax import lax
from jax.experimental import pallas as pl
from jax.experimental.pallas import tpu as pltpu
from jax.sharding import PartitionSpec as P

ROOT_TERM = 0.7978845608028654
CUBIC_TERM = 0.044715


def gelu_pair(pre):
    square = pre * pre
    inner = jnp.tanh(ROOT_TERM * (pre + CUBIC_TERM * square * pre))
    value = 0.5 * pre * (1.0 + inner)
    slope = 0.5 * (1.0 + inner) + 0.5 * pre * (1.0 - inner * inner) * ROOT_TERM * (
        1.0 + 3.0 * CUBIC_TERM * square
    )
    return value, slope


def hop(x, axis, step):
    n = lax.axis_size(axis)
    if step % n == 0:
        return x
    return lax.ppermute(x, axis, [(i, (i + step) % n) for i in range(n)])


def column(ref, order):
    n = ref.shape[-1]
    down = lax.broadcasted_iota(jnp.int32, (n, n), 0)
    along = lax.broadcasted_iota(jnp.int32, (n, n), 1)
    out = []
    for at in order:
        row = ref[0, 0, pl.ds(at, 1), :].astype(jnp.float32)
        out.append(jnp.sum(jnp.where(down == along, row, 0.0), axis=1, keepdims=True))
    return jnp.concatenate(out, axis=0)


def pick_kernel(n_hid, n_share, picks_hbm, tokens_hbm, upstream_hbm, rows_ref, spread_ref, *refs):
    *side_refs, picks_ref, tokens_ref, upstream_ref, sems = refs
    n_exp = picks_ref.shape[2]
    tok_dev, width = tokens_ref.shape[1:]
    copies = [
        pltpu.make_async_copy(picks_hbm, picks_ref, sems.at[0]),
        pltpu.make_async_copy(tokens_hbm, tokens_ref, sems.at[1]),
        pltpu.make_async_copy(upstream_hbm, upstream_ref, sems.at[2]),
    ]
    for copy in copies:
        copy.start()
    me = lax.axis_index("expert")
    copies[0].wait()

    def one_hot(order):
        wanted = column(picks_ref, order).astype(jnp.int32)
        spots = lax.broadcasted_iota(jnp.int32, (wanted.shape[0], tok_dev), 1)
        return jnp.where(wanted == spots, 1.0, 0.0).astype(jnp.bfloat16)

    selector = one_hot([(me + s) % n_exp for s in range(n_exp)])
    spread_ref[...] = one_hot([e for e in range(n_exp) for _ in range(n_hid)])
    for at, copy, source in ((0, copies[1], tokens_ref), (width, copies[2], upstream_ref)):
        copy.wait()
        rows_ref[:, at : at + width] = jnp.dot(
            selector, source[0], preferred_element_type=jnp.float32
        ).astype(jnp.bfloat16)
    n_dp = len(side_refs) + 1
    cols = width // n_dp
    span = side_refs[0].shape[1]
    my_dp = lax.axis_index("dp")
    if n_share == 1:
        starts = [0, width]
    else:
        per_half = n_share // 2
        share = lax.axis_index("hidden")
        starts = [(share // per_half) * width + (share % per_half) * span]
    wide = span // len(starts)
    for s in range(1, n_dp):
        at = ((my_dp + s) % n_dp) * cols
        for k, start in enumerate(starts):
            side_refs[s - 1][:, k * wide : (k + 1) * wide] = rows_ref[
                :, pl.ds(pl.multiple_of(start + at, 128), wide)
            ]


def load_kernel(chunks, after_ref, gates_hbm, upper_hbm, lower_hbm, gates_ref, upper_ref, lower_ref, sems):
    step = upper_ref.shape[1] // chunks
    copies = [pltpu.make_async_copy(gates_hbm, gates_ref, sems.at[2 * chunks])]
    for k, (source, target) in enumerate(((upper_hbm, upper_ref), (lower_hbm, lower_ref))):
        for c in range(chunks):
            spot = pl.ds(c * step, step)
            copies.append(
                pltpu.make_async_copy(
                    source.at[:, spot, :], target.at[:, spot, :], sems.at[k * chunks + c]
                )
            )
    for copy in copies:
        copy.start()
    for copy in copies:
        copy.wait()


def factor_kernel(gates_ref, rows_ref, upper_ref, lower_ref, *refs):
    out_ref = refs[-1]
    n_exp = gates_ref.shape[2]
    width, units = upper_ref.shape[1:]
    me = lax.axis_index("expert")
    gate = column(gates_ref, [(me + n_exp - s) % n_exp for s in range(n_exp)])
    pre = jnp.dot(rows_ref[:, :width], upper_ref[0], preferred_element_type=jnp.float32)
    back = jnp.dot(rows_ref[:, width:], lower_ref[0], preferred_element_type=jnp.float32)
    value, slope = gelu_pair(pre)
    out_ref[:, :units] = (back * gate * slope).astype(jnp.bfloat16)
    out_ref[:, units:] = (value * gate).astype(jnp.bfloat16)


def piece_kernel(n_hid, factor_ref, upper_ref, *refs):
    *side_refs, out_ref = refs
    n_pick = out_ref.shape[1]
    width, units = upper_ref.shape[1:]
    part = width // n_hid
    span = side_refs[0].shape[1]
    n_exp = out_ref.shape[0] // n_hid
    me = lax.axis_index("expert")
    for k, side in enumerate(side_refs):
        rows = side[...].astype(jnp.float32)
        for s in range(n_exp):
            block = rows[s * n_pick : (s + 1) * n_pick].astype(jnp.bfloat16)
            owner = ((me + s) % n_exp) * n_hid
            for h in range(n_hid):
                out_ref[owner + h, :, part + k * span : part + (k + 1) * span] = block
    piece = lax.dot_general(
        factor_ref[:, :units], upper_ref[0], (((1,), (1,)), ((), ())), preferred_element_type=jnp.float32
    )
    for s in range(n_exp):
        owner = ((me + n_exp - s) % n_exp) * n_hid
        for h in range(n_hid):
            out_ref[owner + h, :, :part] = piece[
                s * n_pick : (s + 1) * n_pick, h * part : (h + 1) * part
            ].astype(jnp.bfloat16)


def weight_kernel(chunks, n_dp, n_share, after_ref, own_ref, came_ref, factor_ref, *refs):
    up_ref, down_ref, side_ref, held, sems = refs
    slots = own_ref.shape[0]
    width = own_ref.shape[1] // 2
    units = factor_ref.shape[1] // 2
    cols = side_ref.shape[1] // 2
    span = 2 * cols // n_share
    n_pick = came_ref.shape[1]
    n_exp = slots // n_pick
    n_hid = came_ref.shape[0] // n_exp
    part = width // n_hid
    me = lax.axis_index("expert")
    start = lax.axis_index("dp") * cols
    for half in range(2):
        side_ref[:slots, half * cols : (half + 1) * cols] = own_ref[
            :, pl.ds(pl.multiple_of(half * width + start, 128), cols)
        ]
    for t in range(n_share):
        sender = lax.axis_index("hidden") if n_share == 1 else t
        for s in range(1, n_dp):
            spot = part + (s - 1) * span
            blocks = [
                came_ref[((me + n_exp - b) % n_exp) * n_hid + sender, :, spot : spot + span].astype(jnp.float32)
                for b in range(n_exp)
            ]
            side_ref[s * slots : (s + 1) * slots, t * span : (t + 1) * span] = jnp.concatenate(
                blocks, axis=0
            ).astype(jnp.bfloat16)
    step = units // chunks
    copies = []
    for which, out in ((0, up_ref), (1, down_ref)):
        for c in range(chunks):
            spot = pl.ds(c * step, step)
            held[which, :, spot] = lax.dot_general(
                side_ref[:, which * cols : (which + 1) * cols],
                factor_ref[:, pl.ds(which * units + c * step, step)],
                (((0,), (0,)), ((), ())),
                preferred_element_type=jnp.float32,
            )
            copy = pltpu.make_async_copy(
                held.at[which, :, spot], out.at[0, :, spot], sems.at[which, c]
            )
            copy.start()
            copies.append(copy)
    for copy in copies:
        copy.wait()


VMEM = pl.BlockSpec(memory_space=pltpu.VMEM)
ANY = pl.BlockSpec(memory_space=pl.ANY)
HBM = pl.BlockSpec(memory_space=pltpu.HBM)
ROOM = pltpu.CompilerParams(vmem_limit_bytes=16 << 20)


def local(layer_input, grad_out, picks, gates, w_up, w_down):
    tok_dev, width = layer_input.shape[1:]
    n_exp, n_pick = picks.shape[2:]
    slots = n_exp * n_pick
    units = w_up.shape[2]
    n_dp = lax.axis_size("dp")
    n_hid = lax.axis_size("hidden")
    cols = width // n_dp
    part = width // n_hid
    bf16 = jnp.bfloat16
    layer_input, grad_out, picks, gates, w_up, w_down = (
        pltpu.with_memory_space_constraint(x, pltpu.HBM)
        for x in (layer_input, grad_out, picks, gates, w_up, w_down)
    )

    n_share = n_hid if n_hid % 2 == 0 and 2 * cols % (n_hid * 128) == 0 else 1
    span = 2 * cols // n_share
    send, spread, *side = pl.pallas_call(
        functools.partial(pick_kernel, n_hid, n_share),
        out_shape=[
            jax.ShapeDtypeStruct((slots, 2 * width), bf16),
            jax.ShapeDtypeStruct((slots * n_hid, tok_dev), bf16),
        ]
        + [jax.ShapeDtypeStruct((slots, span), bf16)] * (n_dp - 1),
        in_specs=[HBM] * 3,
        out_specs=[VMEM] * (n_dp + 1),
        scratch_shapes=[
            pltpu.VMEM(picks.shape, jnp.int32),
            pltpu.VMEM(layer_input.shape, bf16),
            pltpu.VMEM(grad_out.shape, bf16),
            pltpu.SemaphoreType.DMA((3,)),
        ],
        compiler_params=ROOM,
        name="pick",
    )(picks, layer_input, grad_out)

    rows = jnp.concatenate(
        [hop(send[s * n_pick : (s + 1) * n_pick], "expert", s) for s in range(n_exp)], axis=0
    )
    side = [hop(x, "dp", s + 1) for s, x in enumerate(side)]

    splits = 4
    gate_held, upper, lower = pl.pallas_call(
        functools.partial(load_kernel, splits),
        out_shape=[jax.ShapeDtypeStruct(x.shape, x.dtype) for x in (gates, w_up, w_down)],
        in_specs=[HBM] * 4,
        out_specs=[VMEM] * 3,
        scratch_shapes=[pltpu.SemaphoreType.DMA((2 * splits + 1,))],
        compiler_params=ROOM,
        cost_estimate=pl.CostEstimate(
            flops=0, bytes_accessed=4 * w_up.size + 4 * w_down.size, transcendentals=0
        ),
        name="load",
    )(send, gates, w_up, w_down)
    factors = pl.pallas_call(
        factor_kernel,
        out_shape=jax.ShapeDtypeStruct((slots, 2 * units), bf16),
        in_specs=[VMEM] * 4 + [ANY] * (n_dp - 2),
        out_specs=VMEM,
        compiler_params=ROOM,
        cost_estimate=pl.CostEstimate(
            flops=4 * slots * w_up.size, bytes_accessed=4 * w_up.size, transcendentals=slots * units
        ),
        name="factor",
    )(gate_held, rows, upper, lower, *side[:-1])

    gathered = jnp.concatenate([hop(factors, "dp", s) for s in range(n_dp)], axis=0)

    piece = pl.pallas_call(
        functools.partial(piece_kernel, n_hid),
        out_shape=jax.ShapeDtypeStruct((n_exp * n_hid, n_pick, part + (n_dp - 1) * span), bf16),
        in_specs=[VMEM] * (n_dp + 1),
        out_specs=VMEM,
        compiler_params=ROOM,
        cost_estimate=pl.CostEstimate(
            flops=2 * slots * w_up.size, bytes_accessed=2 * w_up.size, transcendentals=0
        ),
        name="piece",
    )(factors, upper, *side)
    returned = lax.cond(
        lax.axis_index("dp") >= 0,
        lambda x: lax.all_to_all(x, ("expert", "hidden"), 0, 0),
        lambda x: x,
        piece,
    )
    grad_rows = lax.dot_general(
        spread,
        returned[:, :, :part].reshape(slots * n_hid, part),
        (((0,), (0,)), ((), ())),
        preferred_element_type=jnp.float32,
    ).astype(bf16)

    chunks = max(1, units // 256)
    grads = pl.pallas_call(
        functools.partial(weight_kernel, chunks, n_dp, n_share),
        out_shape=[jax.ShapeDtypeStruct((1, cols, units), jnp.float32)] * 2,
        in_specs=[ANY] + [VMEM] * 3,
        out_specs=[HBM] * 2,
        scratch_shapes=[
            pltpu.VMEM((n_dp * slots, 2 * cols), bf16),
            pltpu.VMEM((2, cols, units), jnp.float32),
            pltpu.SemaphoreType.DMA((2, chunks)),
        ],
        compiler_params=ROOM,
        name="weight",
    )(grad_rows, rows, returned, gathered)
    return (grad_rows[None], *grads)


def solution(mesh):
    placed = (
        P("dp", "expert", None),
        P("dp", "expert", None),
        P("dp", "expert", None, None),
        P("dp", "expert", None, None),
        P("expert", None, "hidden"),
        P("expert", None, "hidden"),
    )
    return jax.shard_map(
        local,
        mesh=mesh,
        in_specs=placed,
        out_specs=(
            P("dp", "expert", "hidden"),
            P("expert", "dp", "hidden"),
            P("expert", "dp", "hidden"),
        ),
        check_vma=False,
    )
```

```python
import functools

import jax
import jax.numpy as jnp
from jax import lax
from jax.experimental import pallas as pl
from jax.experimental.pallas import tpu as pltpu
from jax.sharding import PartitionSpec as P

ROOT_TERM = 0.7978845608028654
CUBIC_TERM = 0.044715


def gelu_pair(pre):
    square = pre * pre
    inner = jnp.tanh(ROOT_TERM * (pre + CUBIC_TERM * square * pre))
    value = 0.5 * pre * (1.0 + inner)
    slope = 0.5 * (1.0 + inner) + 0.5 * pre * (1.0 - inner * inner) * ROOT_TERM * (
        1.0 + 3.0 * CUBIC_TERM * square
    )
    return value, slope


def hop(x, axis, step):
    n = lax.axis_size(axis)
    if step % n == 0:
        return x
    return lax.ppermute(x, axis, [(i, (i + step) % n) for i in range(n)])


def column(ref, order):
    n = ref.shape[-1]
    down = lax.broadcasted_iota(jnp.int32, (n, n), 0)
    along = lax.broadcasted_iota(jnp.int32, (n, n), 1)
    out = []
    for at in order:
        row = ref[0, 0, pl.ds(at, 1), :].astype(jnp.float32)
        out.append(jnp.sum(jnp.where(down == along, row, 0.0), axis=1, keepdims=True))
    return jnp.concatenate(out, axis=0)


def pick_kernel(n_hid, picks_hbm, tokens_hbm, upstream_hbm, rows_ref, spread_ref, *refs):
    picks_ref, tokens_ref, upstream_ref, sems = refs
    n_exp = picks_ref.shape[2]
    tok_dev, width = tokens_ref.shape[1:]
    copies = [
        pltpu.make_async_copy(picks_hbm, picks_ref, sems.at[0]),
        pltpu.make_async_copy(tokens_hbm, tokens_ref, sems.at[1]),
        pltpu.make_async_copy(upstream_hbm, upstream_ref, sems.at[2]),
    ]
    for copy in copies:
        copy.start()
    me = lax.axis_index("expert")
    copies[0].wait()

    def one_hot(order):
        wanted = column(picks_ref, order).astype(jnp.int32)
        spots = lax.broadcasted_iota(jnp.int32, (wanted.shape[0], tok_dev), 1)
        return jnp.where(wanted == spots, 1.0, 0.0).astype(jnp.bfloat16)

    selector = one_hot([(me + s) % n_exp for s in range(n_exp)])
    spread_ref[...] = one_hot([e for e in range(n_exp) for _ in range(n_hid)])
    for at, copy, source in ((0, copies[1], tokens_ref), (width, copies[2], upstream_ref)):
        copy.wait()
        rows_ref[:, at : at + width] = jnp.dot(
            selector, source[0], preferred_element_type=jnp.float32
        ).astype(jnp.bfloat16)


def cut_kernel(after_ref, rows_ref, *out_refs):
    n_dp = len(out_refs) + 1
    share, wide = out_refs[0].shape
    cols = wide // 2
    width = rows_ref.shape[1] // 2
    my_dp = lax.axis_index("dp")
    spot = pl.ds(pl.multiple_of(lax.axis_index("hidden") * share, 16), share)
    for s, out_ref in enumerate(out_refs):
        at = ((my_dp + s + 1) % n_dp) * cols
        for half in range(2):
            out_ref[:, half * cols : (half + 1) * cols] = rows_ref[
                spot, pl.ds(pl.multiple_of(half * width + at, 128), cols)
            ]


def load_kernel(after_ref, always_ref, gates_hbm, upper_hbm, lower_hbm, gates_ref, upper_ref, lower_ref, sems):
    copies = [
        pltpu.make_async_copy(source, target, sems.at[k])
        for k, (source, target) in enumerate(
            ((gates_hbm, gates_ref), (upper_hbm, upper_ref), (lower_hbm, lower_ref))
        )
    ]
    for copy in copies:
        copy.start()
    for copy in copies:
        copy.wait()


def factor_kernel(after_ref, gates_ref, rows_ref, upper_ref, lower_ref, out_ref):
    n_exp = gates_ref.shape[2]
    width, units = upper_ref.shape[1:]
    me = lax.axis_index("expert")
    gate = column(gates_ref, [(me + n_exp - s) % n_exp for s in range(n_exp)])
    pre = jnp.dot(rows_ref[:, :width], upper_ref[0], preferred_element_type=jnp.float32)
    back = jnp.dot(rows_ref[:, width:], lower_ref[0], preferred_element_type=jnp.float32)
    value, slope = gelu_pair(pre)
    out_ref[:, :units] = (back * gate * slope).astype(jnp.bfloat16)
    out_ref[:, units:] = (value * gate).astype(jnp.bfloat16)


def piece_kernel(n_hid, factor_ref, upper_ref, out_ref):
    n_pick, part = out_ref.shape[1:]
    width, units = upper_ref.shape[1:]
    n_exp = out_ref.shape[0] // n_hid
    me = lax.axis_index("expert")
    piece = lax.dot_general(
        factor_ref[:, :units], upper_ref[0], (((1,), (1,)), ((), ())), preferred_element_type=jnp.float32
    )
    for s in range(n_exp):
        owner = ((me + n_exp - s) % n_exp) * n_hid
        for h in range(n_hid):
            out_ref[owner + h] = piece[
                s * n_pick : (s + 1) * n_pick, h * part : (h + 1) * part
            ].astype(jnp.bfloat16)


def weight_kernel(chunks, shape, own_ref, *refs):
    n_dp, n_hid = shape
    part_refs, refs = refs[:n_hid], refs[n_hid:]
    factor_ref, spread_ref, came_ref, up_ref, down_ref, in_ref, side_ref, held, in_held, sems, in_sem = refs
    units = factor_ref.shape[1] // 2
    cols = side_ref.shape[1] // 2
    width = own_ref.shape[1] // 2
    slots = own_ref.shape[0]
    rows = slots // n_hid
    my_hid = lax.axis_index("hidden")
    start = lax.axis_index("dp") * cols
    for half in range(2):
        side_ref[:slots, half * cols : (half + 1) * cols] = own_ref[
            :, pl.ds(pl.multiple_of(half * width + start, 128), cols)
        ]
    for t, part in enumerate(part_refs):
        spot = ((my_hid + n_hid - t) % n_hid) * rows
        for s in range(1, n_dp):
            side_ref[pl.ds(pl.multiple_of(s * slots + spot, 16), rows), :] = part[s - 1]
    step = units // chunks
    copies = []
    for which, out in ((0, up_ref), (1, down_ref)):
        for c in range(chunks):
            spot = pl.ds(c * step, step)
            held[which, :, spot] = lax.dot_general(
                side_ref[:, which * cols : (which + 1) * cols],
                factor_ref[:, pl.ds(which * units + c * step, step)],
                (((0,), (0,)), ((), ())),
                preferred_element_type=jnp.float32,
            )
            copy = pltpu.make_async_copy(
                held.at[which, :, spot], out.at[0, :, spot], sems.at[which, c]
            )
            copy.start()
            copies.append(copy)
    came = jnp.concatenate([came_ref[k].astype(jnp.float32) for k in range(came_ref.shape[0])], axis=0)
    in_held[...] = lax.dot_general(
        spread_ref[...],
        came.astype(jnp.bfloat16),
        (((0,), (0,)), ((), ())),
        preferred_element_type=jnp.float32,
    ).astype(jnp.bfloat16)
    copies.append(pltpu.make_async_copy(in_held, in_ref.at[0], in_sem))
    copies[-1].start()
    for copy in copies:
        copy.wait()


VMEM = pl.BlockSpec(memory_space=pltpu.VMEM)
ANY = pl.BlockSpec(memory_space=pl.ANY)
HBM = pl.BlockSpec(memory_space=pltpu.HBM)
ROOM = pltpu.CompilerParams(vmem_limit_bytes=16 << 20)


def local(layer_input, grad_out, picks, gates, w_up, w_down):
    tok_dev, width = layer_input.shape[1:]
    n_exp, n_pick = picks.shape[2:]
    slots = n_exp * n_pick
    units = w_up.shape[2]
    n_dp = lax.axis_size("dp")
    n_hid = lax.axis_size("hidden")
    cols = width // n_dp
    part = width // n_hid
    bf16 = jnp.bfloat16
    layer_input, grad_out, picks, gates, w_up, w_down = (
        pltpu.with_memory_space_constraint(x, pltpu.HBM)
        for x in (layer_input, grad_out, picks, gates, w_up, w_down)
    )

    send, spread = pl.pallas_call(
        functools.partial(pick_kernel, n_hid),
        out_shape=[
            jax.ShapeDtypeStruct((slots, 2 * width), bf16),
            jax.ShapeDtypeStruct((slots * n_hid, tok_dev), bf16),
        ],
        in_specs=[HBM] * 3,
        out_specs=[VMEM] * 2,
        scratch_shapes=[
            pltpu.VMEM(picks.shape, jnp.int32),
            pltpu.VMEM(layer_input.shape, bf16),
            pltpu.VMEM(grad_out.shape, bf16),
            pltpu.SemaphoreType.DMA((3,)),
        ],
        compiler_params=ROOM,
        name="pick",
    )(picks, layer_input, grad_out)

    rows = jnp.concatenate(
        [hop(send[s * n_pick : (s + 1) * n_pick], "expert", s) for s in range(n_exp)], axis=0
    )
    always = (lax.axis_index("dp") >= 0).astype(jnp.int32)
    gate_held, upper, lower = pl.pallas_call(
        load_kernel,
        out_shape=[jax.ShapeDtypeStruct(x.shape, x.dtype) for x in (gates, w_up, w_down)],
        in_specs=[HBM, pl.BlockSpec(memory_space=pltpu.SMEM)] + [HBM] * 3,
        out_specs=[VMEM] * 3,
        scratch_shapes=[pltpu.SemaphoreType.DMA((3,))],
        cost_estimate=pl.CostEstimate(
            flops=0, bytes_accessed=4 * w_up.size + 4 * w_down.size, transcendentals=0
        ),
        compiler_params=ROOM,
        name="load",
    )(send, lax.clamp(0, always, 1).reshape(1), gates, w_up, w_down)
    share = slots // n_hid
    parts = pl.pallas_call(
        cut_kernel,
        out_shape=[jax.ShapeDtypeStruct((share, 2 * cols), bf16)] * (n_dp - 1),
        in_specs=[ANY, VMEM],
        out_specs=[VMEM] * (n_dp - 1),
        compiler_params=ROOM,
        name="cut",
    )(gate_held, rows)
    parts = [hop(x, "dp", s + 1) for s, x in enumerate(parts)]

    factors = pl.pallas_call(
        factor_kernel,
        out_shape=jax.ShapeDtypeStruct((slots, 2 * units), bf16),
        in_specs=[ANY] + [VMEM] * 4,
        out_specs=VMEM,
        compiler_params=ROOM,
        cost_estimate=pl.CostEstimate(
            flops=4 * slots * w_up.size, bytes_accessed=4 * w_up.size, transcendentals=slots * units
        ),
        name="factor",
    )(parts[0], gate_held, rows, upper, lower)
    parts = jnp.stack(parts)
    parts = [hop(parts, "hidden", t) for t in range(n_hid)]

    gathered = jnp.concatenate([hop(factors, "dp", s) for s in range(n_dp)], axis=0)

    piece = pl.pallas_call(
        functools.partial(piece_kernel, n_hid),
        out_shape=jax.ShapeDtypeStruct((n_exp * n_hid, n_pick, part), bf16),
        in_specs=[VMEM, VMEM],
        out_specs=VMEM,
        compiler_params=ROOM,
        cost_estimate=pl.CostEstimate(
            flops=2 * slots * w_up.size, bytes_accessed=2 * w_up.size, transcendentals=0
        ),
        name="piece",
    )(factors, upper)
    returned = lax.switch(
        always, [lambda x: x, lambda x: lax.all_to_all(x, ("expert", "hidden"), 0, 0)], piece
    )

    chunks = max(1, units // 256)
    grads = pl.pallas_call(
        functools.partial(weight_kernel, chunks, (n_dp, n_hid)),
        out_shape=[jax.ShapeDtypeStruct((1, cols, units), jnp.float32)] * 2
        + [jax.ShapeDtypeStruct((1, tok_dev, part), bf16)],
        in_specs=[VMEM] * (n_hid + 4),
        out_specs=[HBM] * 3,
        scratch_shapes=[
            pltpu.VMEM((n_dp * slots, 2 * cols), bf16),
            pltpu.VMEM((2, cols, units), jnp.float32),
            pltpu.VMEM((tok_dev, part), bf16),
            pltpu.SemaphoreType.DMA((2, chunks)),
            pltpu.SemaphoreType.DMA,
        ],
        compiler_params=ROOM,
        cost_estimate=pl.CostEstimate(
            flops=4 * n_dp * slots * cols * units, bytes_accessed=64 * cols * units, transcendentals=0
        ),
        name="weight",
    )(rows, *parts, gathered, spread, returned)
    grad_up, grad_down, grad_in = grads
    return grad_in, grad_up, grad_down


def solution(mesh):
    placed = (
        P("dp", "expert", None),
        P("dp", "expert", None),
        P("dp", "expert", None, None),
        P("dp", "expert", None, None),
        P("expert", None, "hidden"),
        P("expert", None, "hidden"),
    )
    return jax.shard_map(
        local,
        mesh=mesh,
        in_specs=placed,
        out_specs=(
            P("dp", "expert", "hidden"),
            P("expert", "dp", "hidden"),
            P("expert", "dp", "hidden"),
        ),
        check_vma=False,
    )
```

```python
import functools

import jax
import jax.numpy as jnp
from jax import lax
from jax.experimental import pallas as pl
from jax.experimental.pallas import tpu as pltpu
from jax.sharding import PartitionSpec as P

ROOT_TERM = 0.7978845608028654
CUBIC_TERM = 0.044715


def gelu_pair(pre):
    square = pre * pre
    inner = jnp.tanh(ROOT_TERM * (pre + CUBIC_TERM * square * pre))
    value = 0.5 * pre * (1.0 + inner)
    slope = 0.5 * (1.0 + inner) + 0.5 * pre * (1.0 - inner * inner) * ROOT_TERM * (
        1.0 + 3.0 * CUBIC_TERM * square
    )
    return value, slope


def hop(x, axis, step):
    n = lax.axis_size(axis)
    if step % n == 0:
        return x
    return lax.ppermute(x, axis, [(i, (i + step) % n) for i in range(n)])


def column(ref, order):
    n = ref.shape[-1]
    down = lax.broadcasted_iota(jnp.int32, (n, n), 0)
    along = lax.broadcasted_iota(jnp.int32, (n, n), 1)
    out = []
    for at in order:
        row = ref[0, 0, pl.ds(at, 1), :].astype(jnp.float32)
        out.append(jnp.sum(jnp.where(down == along, row, 0.0), axis=1, keepdims=True))
    return jnp.concatenate(out, axis=0)


def pick_kernel(n_hid, picks_hbm, tokens_hbm, upstream_hbm, rows_ref, spread_ref, *refs):
    picks_ref, tokens_ref, upstream_ref, sems = refs
    n_exp = picks_ref.shape[2]
    tok_dev, width = tokens_ref.shape[1:]
    copies = [
        pltpu.make_async_copy(picks_hbm, picks_ref, sems.at[0]),
        pltpu.make_async_copy(tokens_hbm, tokens_ref, sems.at[1]),
        pltpu.make_async_copy(upstream_hbm, upstream_ref, sems.at[2]),
    ]
    for copy in copies:
        copy.start()
    me = lax.axis_index("expert")
    copies[0].wait()

    def one_hot(order):
        wanted = column(picks_ref, order).astype(jnp.int32)
        spots = lax.broadcasted_iota(jnp.int32, (wanted.shape[0], tok_dev), 1)
        return jnp.where(wanted == spots, 1.0, 0.0).astype(jnp.bfloat16)

    selector = one_hot([(me + s) % n_exp for s in range(n_exp)])
    spread_ref[...] = one_hot([e for e in range(n_exp) for _ in range(n_hid)])
    for at, copy, source in ((0, copies[1], tokens_ref), (width, copies[2], upstream_ref)):
        copy.wait()
        rows_ref[:, at : at + width] = jnp.dot(
            selector, source[0], preferred_element_type=jnp.float32
        ).astype(jnp.bfloat16)


def cut_kernel(after_ref, rows_ref, *out_refs):
    n_dp = len(out_refs) + 1
    share, wide = out_refs[0].shape
    cols = wide // 2
    width = rows_ref.shape[1] // 2
    my_dp = lax.axis_index("dp")
    spot = pl.ds(pl.multiple_of(lax.axis_index("hidden") * share, 16), share)
    for s, out_ref in enumerate(out_refs):
        at = ((my_dp + s + 1) % n_dp) * cols
        for half in range(2):
            out_ref[:, half * cols : (half + 1) * cols] = rows_ref[
                spot, pl.ds(pl.multiple_of(half * width + at, 128), cols)
            ]


def load_kernel(after_ref, gates_hbm, upper_hbm, lower_hbm, gates_ref, upper_ref, lower_ref, sems):
    copies = [
        pltpu.make_async_copy(source, target, sems.at[k])
        for k, (source, target) in enumerate(
            ((gates_hbm, gates_ref), (upper_hbm, upper_ref), (lower_hbm, lower_ref))
        )
    ]
    for copy in copies:
        copy.start()
    for copy in copies:
        copy.wait()


def factor_kernel(after_ref, gates_ref, rows_ref, upper_ref, lower_ref, out_ref):
    n_exp = gates_ref.shape[2]
    width, units = upper_ref.shape[1:]
    me = lax.axis_index("expert")
    gate = column(gates_ref, [(me + n_exp - s) % n_exp for s in range(n_exp)])
    pre = jnp.dot(rows_ref[:, :width], upper_ref[0], preferred_element_type=jnp.float32)
    back = jnp.dot(rows_ref[:, width:], lower_ref[0], preferred_element_type=jnp.float32)
    value, slope = gelu_pair(pre)
    out_ref[:, :units] = (back * gate * slope).astype(jnp.bfloat16)
    out_ref[:, units:] = (value * gate).astype(jnp.bfloat16)


def piece_kernel(n_hid, factor_ref, upper_ref, out_ref):
    n_pick, part = out_ref.shape[1:]
    width, units = upper_ref.shape[1:]
    n_exp = out_ref.shape[0] // n_hid
    me = lax.axis_index("expert")
    piece = lax.dot_general(
        factor_ref[:, :units], upper_ref[0], (((1,), (1,)), ((), ())), preferred_element_type=jnp.float32
    )
    for s in range(n_exp):
        owner = ((me + n_exp - s) % n_exp) * n_hid
        for h in range(n_hid):
            out_ref[owner + h] = piece[
                s * n_pick : (s + 1) * n_pick, h * part : (h + 1) * part
            ].astype(jnp.bfloat16)


def stack_kernel(after_ref, *refs):
    *part_refs, out_ref = refs
    for s, part in enumerate(part_refs):
        out_ref[s] = part[...]


def tie_kernel(*refs):
    pass


def weight_kernel(chunks, shape, own_ref, *refs):
    n_dp, n_hid = shape
    part_refs, refs = refs[:n_hid], refs[n_hid:]
    factor_ref, up_ref, down_ref, side_ref, held, sems = refs
    units = factor_ref.shape[1] // 2
    cols = side_ref.shape[1] // 2
    width = own_ref.shape[1] // 2
    slots = own_ref.shape[0]
    rows = slots // n_hid
    my_hid = lax.axis_index("hidden")
    start = lax.axis_index("dp") * cols
    for half in range(2):
        side_ref[:slots, half * cols : (half + 1) * cols] = own_ref[
            :, pl.ds(pl.multiple_of(half * width + start, 128), cols)
        ]
    for t, part in enumerate(part_refs):
        spot = ((my_hid + n_hid - t) % n_hid) * rows
        for s in range(1, n_dp):
            side_ref[pl.ds(pl.multiple_of(s * slots + spot, 16), rows), :] = part[s - 1]
    step = units // chunks
    copies = []
    for which, out in ((0, up_ref), (1, down_ref)):
        for c in range(chunks):
            spot = pl.ds(c * step, step)
            held[which, :, spot] = lax.dot_general(
                side_ref[:, which * cols : (which + 1) * cols],
                factor_ref[:, pl.ds(which * units + c * step, step)],
                (((0,), (0,)), ((), ())),
                preferred_element_type=jnp.float32,
            )
            copy = pltpu.make_async_copy(
                held.at[which, :, spot], out.at[0, :, spot], sems.at[which, c]
            )
            copy.start()
            copies.append(copy)
    for copy in copies:
        copy.wait()


VMEM = pl.BlockSpec(memory_space=pltpu.VMEM)
ANY = pl.BlockSpec(memory_space=pl.ANY)
HBM = pl.BlockSpec(memory_space=pltpu.HBM)
ROOM = pltpu.CompilerParams(vmem_limit_bytes=16 << 20)


def local(layer_input, grad_out, picks, gates, w_up, w_down):
    tok_dev, width = layer_input.shape[1:]
    n_exp, n_pick = picks.shape[2:]
    slots = n_exp * n_pick
    units = w_up.shape[2]
    n_dp = lax.axis_size("dp")
    n_hid = lax.axis_size("hidden")
    cols = width // n_dp
    part = width // n_hid
    bf16 = jnp.bfloat16
    layer_input, grad_out, picks, gates, w_up, w_down = (
        pltpu.with_memory_space_constraint(x, pltpu.HBM)
        for x in (layer_input, grad_out, picks, gates, w_up, w_down)
    )

    send, spread = pl.pallas_call(
        functools.partial(pick_kernel, n_hid),
        out_shape=[
            jax.ShapeDtypeStruct((slots, 2 * width), bf16),
            jax.ShapeDtypeStruct((slots * n_hid, tok_dev), bf16),
        ],
        in_specs=[HBM] * 3,
        out_specs=[VMEM] * 2,
        scratch_shapes=[
            pltpu.VMEM(picks.shape, jnp.int32),
            pltpu.VMEM(layer_input.shape, bf16),
            pltpu.VMEM(grad_out.shape, bf16),
            pltpu.SemaphoreType.DMA((3,)),
        ],
        compiler_params=ROOM,
        name="pick",
    )(picks, layer_input, grad_out)

    rows = jnp.concatenate(
        [hop(send[s * n_pick : (s + 1) * n_pick], "expert", s) for s in range(n_exp)], axis=0
    )
    gate_held, upper, lower = pl.pallas_call(
        load_kernel,
        out_shape=[jax.ShapeDtypeStruct(x.shape, x.dtype) for x in (gates, w_up, w_down)],
        in_specs=[HBM] * 4,
        out_specs=[VMEM] * 3,
        scratch_shapes=[pltpu.SemaphoreType.DMA((3,))],
        cost_estimate=pl.CostEstimate(
            flops=0, bytes_accessed=4 * w_up.size + 4 * w_down.size, transcendentals=0
        ),
        compiler_params=ROOM,
        name="load",
    )(send, gates, w_up, w_down)
    share = slots // n_hid
    parts = pl.pallas_call(
        cut_kernel,
        out_shape=[jax.ShapeDtypeStruct((share, 2 * cols), bf16)] * (n_dp - 1),
        in_specs=[ANY, VMEM],
        out_specs=[VMEM] * (n_dp - 1),
        compiler_params=ROOM,
        name="cut",
    )(gate_held, rows)
    parts = [hop(x, "dp", s + 1) for s, x in enumerate(parts)]

    factors = pl.pallas_call(
        factor_kernel,
        out_shape=jax.ShapeDtypeStruct((slots, 2 * units), bf16),
        in_specs=[ANY] + [VMEM] * 4,
        out_specs=VMEM,
        compiler_params=ROOM,
        cost_estimate=pl.CostEstimate(
            flops=4 * slots * w_up.size, bytes_accessed=4 * w_up.size, transcendentals=slots * units
        ),
        name="factor",
    )(parts[0], gate_held, rows, upper, lower)
    parts = pl.pallas_call(
        stack_kernel,
        out_shape=jax.ShapeDtypeStruct((n_dp - 1, share, 2 * cols), bf16),
        in_specs=[ANY] + [VMEM] * (n_dp - 1),
        out_specs=VMEM,
        compiler_params=ROOM,
        name="stack",
    )(factors, *parts)
    parts = [hop(parts, "hidden", t) for t in range(n_hid)]

    gathered = jnp.concatenate([hop(factors, "dp", s) for s in range(n_dp)], axis=0)

    piece = pl.pallas_call(
        functools.partial(piece_kernel, n_hid),
        out_shape=jax.ShapeDtypeStruct((n_exp * n_hid, n_pick, part), bf16),
        in_specs=[VMEM, VMEM],
        out_specs=VMEM,
        compiler_params=ROOM,
        cost_estimate=pl.CostEstimate(
            flops=2 * slots * w_up.size, bytes_accessed=2 * w_up.size, transcendentals=0
        ),
        name="piece",
    )(factors, upper)
    piece = pl.pallas_call(
        tie_kernel,
        out_shape=jax.ShapeDtypeStruct(piece.shape, piece.dtype),
        in_specs=[ANY] * n_hid,
        out_specs=ANY,
        input_output_aliases={0: 0},
        compiler_params=ROOM,
        name="tie",
    )(piece, *parts[1:])
    returned = lax.all_to_all(piece, ("expert", "hidden"), 0, 0)
    grad_rows = lax.dot_general(
        spread,
        returned.reshape(slots * n_hid, part),
        (((0,), (0,)), ((), ())),
        preferred_element_type=jnp.float32,
    ).astype(bf16)

    chunks = max(1, units // 256)
    grads = pl.pallas_call(
        functools.partial(weight_kernel, chunks, (n_dp, n_hid)),
        out_shape=[jax.ShapeDtypeStruct((1, cols, units), jnp.float32)] * 2,
        in_specs=[VMEM] * (n_hid + 2),
        out_specs=[HBM] * 2,
        scratch_shapes=[
            pltpu.VMEM((n_dp * slots, 2 * cols), bf16),
            pltpu.VMEM((2, cols, units), jnp.float32),
            pltpu.SemaphoreType.DMA((2, chunks)),
        ],
        compiler_params=ROOM,
        cost_estimate=pl.CostEstimate(
            flops=4 * n_dp * slots * cols * units, bytes_accessed=64 * cols * units, transcendentals=0
        ),
        name="weight",
    )(rows, *parts, gathered)
    return (grad_rows[None], *grads)


def solution(mesh):
    placed = (
        P("dp", "expert", None),
        P("dp", "expert", None),
        P("dp", "expert", None, None),
        P("dp", "expert", None, None),
        P("expert", None, "hidden"),
        P("expert", None, "hidden"),
    )
    return jax.shard_map(
        local,
        mesh=mesh,
        in_specs=placed,
        out_specs=(
            P("dp", "expert", "hidden"),
            P("expert", "dp", "hidden"),
            P("expert", "dp", "hidden"),
        ),
        check_vma=False,
    )
```

```python
import functools

import jax
import jax.numpy as jnp
from jax import lax
from jax.experimental import pallas as pl
from jax.experimental.pallas import tpu as pltpu
from jax.sharding import PartitionSpec as P

ROOT_TERM = 0.7978845608028654
CUBIC_TERM = 0.044715


def gelu_pair(pre):
    square = pre * pre
    inner = jnp.tanh(ROOT_TERM * (pre + CUBIC_TERM * square * pre))
    value = 0.5 * pre * (1.0 + inner)
    slope = 0.5 * (1.0 + inner) + 0.5 * pre * (1.0 - inner * inner) * ROOT_TERM * (
        1.0 + 3.0 * CUBIC_TERM * square
    )
    return value, slope


def hop(x, axis, step):
    n = lax.axis_size(axis)
    if step % n == 0:
        return x
    return lax.ppermute(x, axis, [(i, (i + step) % n) for i in range(n)])


def column(ref, order):
    n = ref.shape[-1]
    down = lax.broadcasted_iota(jnp.int32, (n, n), 0)
    along = lax.broadcasted_iota(jnp.int32, (n, n), 1)
    out = []
    for at in order:
        row = ref[0, 0, pl.ds(at, 1), :].astype(jnp.float32)
        out.append(jnp.sum(jnp.where(down == along, row, 0.0), axis=1, keepdims=True))
    return jnp.concatenate(out, axis=0)


def pick_kernel(n_hid, picks_hbm, tokens_hbm, upstream_hbm, rows_ref, spread_ref, *refs):
    picks_ref, tokens_ref, upstream_ref, sems = refs
    n_exp = picks_ref.shape[2]
    tok_dev, width = tokens_ref.shape[1:]
    copies = [
        pltpu.make_async_copy(picks_hbm, picks_ref, sems.at[0]),
        pltpu.make_async_copy(tokens_hbm, tokens_ref, sems.at[1]),
        pltpu.make_async_copy(upstream_hbm, upstream_ref, sems.at[2]),
    ]
    for copy in copies:
        copy.start()
    me = lax.axis_index("expert")
    copies[0].wait()

    def one_hot(order):
        wanted = column(picks_ref, order).astype(jnp.int32)
        spots = lax.broadcasted_iota(jnp.int32, (wanted.shape[0], tok_dev), 1)
        return jnp.where(wanted == spots, 1.0, 0.0).astype(jnp.bfloat16)

    selector = one_hot([(me + s) % n_exp for s in range(n_exp)])
    spread_ref[...] = one_hot([e for e in range(n_exp) for _ in range(n_hid)])
    for at, copy, source in ((0, copies[1], tokens_ref), (width, copies[2], upstream_ref)):
        copy.wait()
        rows_ref[:, at : at + width] = jnp.dot(
            selector, source[0], preferred_element_type=jnp.float32
        ).astype(jnp.bfloat16)


def cut_kernel(after_ref, rows_ref, *out_refs):
    n_dp = len(out_refs) + 1
    cols = out_refs[0].shape[1] // 2
    width = rows_ref.shape[1] // 2
    my_dp = lax.axis_index("dp")
    for s, out_ref in enumerate(out_refs):
        at = ((my_dp + s + 1) % n_dp) * cols
        for half in range(2):
            out_ref[:, half * cols : (half + 1) * cols] = rows_ref[
                :, pl.ds(pl.multiple_of(half * width + at, 128), cols)
            ]


def load_kernel(after_ref, gates_hbm, upper_hbm, lower_hbm, gates_ref, upper_ref, lower_ref, sems):
    copies = [
        pltpu.make_async_copy(source, target, sems.at[k])
        for k, (source, target) in enumerate(
            ((gates_hbm, gates_ref), (upper_hbm, upper_ref), (lower_hbm, lower_ref))
        )
    ]
    for copy in copies:
        copy.start()
    for copy in copies:
        copy.wait()


def factor_kernel(gates_ref, rows_ref, upper_ref, lower_ref, out_ref):
    n_exp = gates_ref.shape[2]
    width, units = upper_ref.shape[1:]
    me = lax.axis_index("expert")
    gate = column(gates_ref, [(me + n_exp - s) % n_exp for s in range(n_exp)])
    pre = jnp.dot(rows_ref[:, :width], upper_ref[0], preferred_element_type=jnp.float32)
    back = jnp.dot(rows_ref[:, width:], lower_ref[0], preferred_element_type=jnp.float32)
    value, slope = gelu_pair(pre)
    out_ref[:, :units] = (back * gate * slope).astype(jnp.bfloat16)
    out_ref[:, units:] = (value * gate).astype(jnp.bfloat16)


def piece_kernel(n_hid, factor_ref, upper_ref, out_ref):
    n_pick, part = out_ref.shape[1:]
    width, units = upper_ref.shape[1:]
    n_exp = out_ref.shape[0] // n_hid
    me = lax.axis_index("expert")
    piece = lax.dot_general(
        factor_ref[:, :units], upper_ref[0], (((1,), (1,)), ((), ())), preferred_element_type=jnp.float32
    )
    for s in range(n_exp):
        owner = ((me + n_exp - s) % n_exp) * n_hid
        for h in range(n_hid):
            out_ref[owner + h] = piece[
                s * n_pick : (s + 1) * n_pick, h * part : (h + 1) * part
            ].astype(jnp.bfloat16)


def tie_kernel(*refs):
    pass


def weight_kernel(chunks, own_ref, part_ref, factor_ref, up_ref, down_ref, side_ref, held, sems):
    units = factor_ref.shape[1] // 2
    cols = side_ref.shape[1] // 2
    width = own_ref.shape[1] // 2
    slots = own_ref.shape[0]
    start = lax.axis_index("dp") * cols
    for half in range(2):
        side_ref[:slots, half * cols : (half + 1) * cols] = own_ref[
            :, pl.ds(pl.multiple_of(half * width + start, 128), cols)
        ]
    side_ref[slots:, :] = part_ref[...]
    step = units // chunks
    copies = []
    for which, out in ((0, up_ref), (1, down_ref)):
        for c in range(chunks):
            spot = pl.ds(c * step, step)
            held[which, :, spot] = lax.dot_general(
                side_ref[:, which * cols : (which + 1) * cols],
                factor_ref[:, pl.ds(which * units + c * step, step)],
                (((0,), (0,)), ((), ())),
                preferred_element_type=jnp.float32,
            )
            copy = pltpu.make_async_copy(
                held.at[which, :, spot], out.at[0, :, spot], sems.at[which, c]
            )
            copy.start()
            copies.append(copy)
    for copy in copies:
        copy.wait()


VMEM = pl.BlockSpec(memory_space=pltpu.VMEM)
ANY = pl.BlockSpec(memory_space=pl.ANY)
HBM = pl.BlockSpec(memory_space=pltpu.HBM)
ROOM = pltpu.CompilerParams(vmem_limit_bytes=16 << 20)


def local(layer_input, grad_out, picks, gates, w_up, w_down):
    tok_dev, width = layer_input.shape[1:]
    n_exp, n_pick = picks.shape[2:]
    slots = n_exp * n_pick
    units = w_up.shape[2]
    n_dp = lax.axis_size("dp")
    n_hid = lax.axis_size("hidden")
    cols = width // n_dp
    part = width // n_hid
    bf16 = jnp.bfloat16
    layer_input, grad_out, picks, gates, w_up, w_down = (
        pltpu.with_memory_space_constraint(x, pltpu.HBM)
        for x in (layer_input, grad_out, picks, gates, w_up, w_down)
    )

    send, spread = pl.pallas_call(
        functools.partial(pick_kernel, n_hid),
        out_shape=[
            jax.ShapeDtypeStruct((slots, 2 * width), bf16),
            jax.ShapeDtypeStruct((slots * n_hid, tok_dev), bf16),
        ],
        in_specs=[HBM] * 3,
        out_specs=[VMEM] * 2,
        scratch_shapes=[
            pltpu.VMEM(picks.shape, jnp.int32),
            pltpu.VMEM(layer_input.shape, bf16),
            pltpu.VMEM(grad_out.shape, bf16),
            pltpu.SemaphoreType.DMA((3,)),
        ],
        compiler_params=ROOM,
        name="pick",
    )(picks, layer_input, grad_out)

    rows = jnp.concatenate(
        [hop(send[s * n_pick : (s + 1) * n_pick], "expert", s) for s in range(n_exp)], axis=0
    )
    gate_held, upper, lower = pl.pallas_call(
        load_kernel,
        out_shape=[jax.ShapeDtypeStruct(x.shape, x.dtype) for x in (gates, w_up, w_down)],
        in_specs=[HBM] * 4,
        out_specs=[VMEM] * 3,
        scratch_shapes=[pltpu.SemaphoreType.DMA((3,))],
        cost_estimate=pl.CostEstimate(
            flops=0, bytes_accessed=4 * w_up.size + 4 * w_down.size, transcendentals=0
        ),
        compiler_params=ROOM,
        name="load",
    )(send, gates, w_up, w_down)
    parts = pl.pallas_call(
        cut_kernel,
        out_shape=[jax.ShapeDtypeStruct((slots, 2 * cols), bf16)] * (n_dp - 1),
        in_specs=[ANY, VMEM],
        out_specs=[VMEM] * (n_dp - 1),
        compiler_params=ROOM,
        name="cut",
    )(gate_held, rows)
    parts = [hop(x, "dp", s + 1) for s, x in enumerate(parts)]

    factors = pl.pallas_call(
        factor_kernel,
        out_shape=jax.ShapeDtypeStruct((slots, 2 * units), bf16),
        in_specs=[VMEM] * 4,
        out_specs=VMEM,
        compiler_params=ROOM,
        cost_estimate=pl.CostEstimate(
            flops=4 * slots * w_up.size, bytes_accessed=4 * w_up.size, transcendentals=slots * units
        ),
        name="factor",
    )(gate_held, rows, upper, lower)
    parts = jnp.concatenate(parts, axis=0)

    gathered = jnp.concatenate([hop(factors, "dp", s) for s in range(n_dp)], axis=0)

    piece = pl.pallas_call(
        functools.partial(piece_kernel, n_hid),
        out_shape=jax.ShapeDtypeStruct((n_exp * n_hid, n_pick, part), bf16),
        in_specs=[VMEM, VMEM],
        out_specs=VMEM,
        compiler_params=ROOM,
        cost_estimate=pl.CostEstimate(
            flops=2 * slots * w_up.size, bytes_accessed=2 * w_up.size, transcendentals=0
        ),
        name="piece",
    )(factors, upper)
    piece = pl.pallas_call(
        tie_kernel,
        out_shape=jax.ShapeDtypeStruct(piece.shape, piece.dtype),
        in_specs=[ANY] * 2,
        out_specs=ANY,
        input_output_aliases={0: 0},
        compiler_params=ROOM,
        name="tie",
    )(piece, parts)
    returned = lax.all_to_all(piece, ("expert", "hidden"), 0, 0)
    grad_rows = lax.dot_general(
        spread,
        returned.reshape(slots * n_hid, part),
        (((0,), (0,)), ((), ())),
        preferred_element_type=jnp.float32,
    ).astype(bf16)

    chunks = max(1, units // 256)
    grads = pl.pallas_call(
        functools.partial(weight_kernel, chunks),
        out_shape=[jax.ShapeDtypeStruct((1, cols, units), jnp.float32)] * 2,
        in_specs=[VMEM] * 3,
        out_specs=[HBM] * 2,
        scratch_shapes=[
            pltpu.VMEM((n_dp * slots, 2 * cols), bf16),
            pltpu.VMEM((2, cols, units), jnp.float32),
            pltpu.SemaphoreType.DMA((2, chunks)),
        ],
        compiler_params=ROOM,
        cost_estimate=pl.CostEstimate(
            flops=4 * n_dp * slots * cols * units, bytes_accessed=64 * cols * units, transcendentals=0
        ),
        name="weight",
    )(rows, parts, gathered)
    return (grad_rows[None], *grads)


def solution(mesh):
    placed = (
        P("dp", "expert", None),
        P("dp", "expert", None),
        P("dp", "expert", None, None),
        P("dp", "expert", None, None),
        P("expert", None, "hidden"),
        P("expert", None, "hidden"),
    )
    return jax.shard_map(
        local,
        mesh=mesh,
        in_specs=placed,
        out_specs=(
            P("dp", "expert", "hidden"),
            P("expert", "dp", "hidden"),
            P("expert", "dp", "hidden"),
        ),
        check_vma=False,
    )
```

```python
import functools

import jax
import jax.numpy as jnp
from jax import lax
from jax.experimental import pallas as pl
from jax.experimental.pallas import tpu as pltpu
from jax.sharding import PartitionSpec as P

ROOT_TERM = 0.7978845608028654
CUBIC_TERM = 0.044715


def gelu_pair(pre):
    square = pre * pre
    inner = jnp.tanh(ROOT_TERM * (pre + CUBIC_TERM * square * pre))
    value = 0.5 * pre * (1.0 + inner)
    slope = 0.5 * (1.0 + inner) + 0.5 * pre * (1.0 - inner * inner) * ROOT_TERM * (
        1.0 + 3.0 * CUBIC_TERM * square
    )
    return value, slope


def hop(x, axis, step):
    n = lax.axis_size(axis)
    assert n & (n - 1) == 0
    return lax.ppermute(x, axis, [(i, i ^ step) for i in range(n)]) if step else x


def column(ref, order):
    n = ref.shape[-1]
    down = lax.broadcasted_iota(jnp.int32, (n, n), 0)
    along = lax.broadcasted_iota(jnp.int32, (n, n), 1)
    out = []
    for at in order:
        row = ref[0, 0, pl.ds(at, 1), :].astype(jnp.float32)
        out.append(jnp.sum(jnp.where(down == along, row, 0.0), axis=1, keepdims=True))
    return jnp.concatenate(out, axis=0)


def pick_kernel(n_hid, picks_hbm, tokens_hbm, upstream_hbm, rows_ref, spread_ref, *refs):
    picks_ref, tokens_ref, upstream_ref, sems = refs
    n_exp = picks_ref.shape[2]
    tok_dev, width = tokens_ref.shape[1:]
    copies = [
        pltpu.make_async_copy(picks_hbm, picks_ref, sems.at[0]),
        pltpu.make_async_copy(tokens_hbm, tokens_ref, sems.at[1]),
        pltpu.make_async_copy(upstream_hbm, upstream_ref, sems.at[2]),
    ]
    for copy in copies:
        copy.start()
    me = lax.axis_index("expert")
    copies[0].wait()

    def one_hot(order):
        wanted = column(picks_ref, order).astype(jnp.int32)
        spots = lax.broadcasted_iota(jnp.int32, (wanted.shape[0], tok_dev), 1)
        return jnp.where(wanted == spots, 1.0, 0.0).astype(jnp.bfloat16)

    selector = one_hot([me ^ s for s in range(n_exp)])
    spread_ref[...] = one_hot([e for e in range(n_exp) for _ in range(n_hid)])
    for at, copy, source in ((0, copies[1], tokens_ref), (width, copies[2], upstream_ref)):
        copy.wait()
        rows_ref[:, at : at + width] = jnp.dot(
            selector, source[0], preferred_element_type=jnp.float32
        ).astype(jnp.bfloat16)


def cut_kernel(after_ref, rows_ref, *out_refs):
    n_dp = len(out_refs) + 1
    share, wide = out_refs[0].shape
    cols = wide // 2
    width = rows_ref.shape[1] // 2
    my_dp = lax.axis_index("dp")
    spot = pl.ds(pl.multiple_of(lax.axis_index("hidden") * share, 16), share)
    for s, out_ref in enumerate(out_refs):
        at = (my_dp ^ (s + 1)) * cols
        for half in range(2):
            out_ref[:, half * cols : (half + 1) * cols] = rows_ref[
                spot, pl.ds(pl.multiple_of(half * width + at, 128), cols)
            ]


def load_kernel(after_ref, gates_hbm, upper_hbm, lower_hbm, gates_ref, upper_ref, lower_ref, sems):
    copies = [
        pltpu.make_async_copy(source, target, sems.at[k])
        for k, (source, target) in enumerate(
            ((gates_hbm, gates_ref), (upper_hbm, upper_ref), (lower_hbm, lower_ref))
        )
    ]
    for copy in copies:
        copy.start()
    for copy in copies:
        copy.wait()


def factor_kernel(after_ref, gates_ref, rows_ref, upper_ref, lower_ref, out_ref):
    n_exp = gates_ref.shape[2]
    width, units = upper_ref.shape[1:]
    me = lax.axis_index("expert")
    gate = column(gates_ref, [me ^ s for s in range(n_exp)])
    pre = jnp.dot(rows_ref[:, :width], upper_ref[0], preferred_element_type=jnp.float32)
    back = jnp.dot(rows_ref[:, width:], lower_ref[0], preferred_element_type=jnp.float32)
    value, slope = gelu_pair(pre)
    out_ref[:, :units] = (back * gate * slope).astype(jnp.bfloat16)
    out_ref[:, units:] = (value * gate).astype(jnp.bfloat16)


def piece_kernel(n_hid, factor_ref, upper_ref, out_ref):
    n_pick, part = out_ref.shape[1:]
    width, units = upper_ref.shape[1:]
    n_exp = out_ref.shape[0] // n_hid
    me = lax.axis_index("expert")
    piece = lax.dot_general(
        factor_ref[:, :units], upper_ref[0], (((1,), (1,)), ((), ())), preferred_element_type=jnp.float32
    )
    for s in range(n_exp):
        owner = (me ^ s) * n_hid
        for h in range(n_hid):
            out_ref[owner + h] = piece[
                s * n_pick : (s + 1) * n_pick, h * part : (h + 1) * part
            ].astype(jnp.bfloat16)


def stack_kernel(after_ref, *refs):
    *part_refs, out_ref = refs
    for s, part in enumerate(part_refs):
        out_ref[s] = part[...]


def tie_kernel(*refs):
    pass


def weight_kernel(chunks, shape, own_ref, *refs):
    n_dp, n_hid = shape
    part_refs, refs = refs[:n_hid], refs[n_hid:]
    factor_ref, up_ref, down_ref, side_ref, held, sems = refs
    units = factor_ref.shape[1] // 2
    cols = side_ref.shape[1] // 2
    width = own_ref.shape[1] // 2
    slots = own_ref.shape[0]
    rows = slots // n_hid
    my_hid = lax.axis_index("hidden")
    start = lax.axis_index("dp") * cols
    for half in range(2):
        side_ref[:slots, half * cols : (half + 1) * cols] = own_ref[
            :, pl.ds(pl.multiple_of(half * width + start, 128), cols)
        ]
    for t, part in enumerate(part_refs):
        spot = (my_hid ^ t) * rows
        for s in range(1, n_dp):
            side_ref[pl.ds(pl.multiple_of(s * slots + spot, 16), rows), :] = part[s - 1]
    step = units // chunks
    copies = []
    for which, out in ((0, up_ref), (1, down_ref)):
        for c in range(chunks):
            spot = pl.ds(c * step, step)
            held[which, :, spot] = lax.dot_general(
                side_ref[:, which * cols : (which + 1) * cols],
                factor_ref[:, pl.ds(which * units + c * step, step)],
                (((0,), (0,)), ((), ())),
                preferred_element_type=jnp.float32,
            )
            copy = pltpu.make_async_copy(
                held.at[which, :, spot], out.at[0, :, spot], sems.at[which, c]
            )
            copy.start()
            copies.append(copy)
    for copy in copies:
        copy.wait()


VMEM = pl.BlockSpec(memory_space=pltpu.VMEM)
ANY = pl.BlockSpec(memory_space=pl.ANY)
HBM = pl.BlockSpec(memory_space=pltpu.HBM)
ROOM = pltpu.CompilerParams(vmem_limit_bytes=16 << 20)


def local(layer_input, grad_out, picks, gates, w_up, w_down):
    tok_dev, width = layer_input.shape[1:]
    n_exp, n_pick = picks.shape[2:]
    slots = n_exp * n_pick
    units = w_up.shape[2]
    n_dp = lax.axis_size("dp")
    n_hid = lax.axis_size("hidden")
    cols = width // n_dp
    part = width // n_hid
    bf16 = jnp.bfloat16
    layer_input, grad_out, picks, gates, w_up, w_down = (
        pltpu.with_memory_space_constraint(x, pltpu.HBM)
        for x in (layer_input, grad_out, picks, gates, w_up, w_down)
    )

    send, spread = pl.pallas_call(
        functools.partial(pick_kernel, n_hid),
        out_shape=[
            jax.ShapeDtypeStruct((slots, 2 * width), bf16),
            jax.ShapeDtypeStruct((slots * n_hid, tok_dev), bf16),
        ],
        in_specs=[HBM] * 3,
        out_specs=[VMEM] * 2,
        scratch_shapes=[
            pltpu.VMEM(picks.shape, jnp.int32),
            pltpu.VMEM(layer_input.shape, bf16),
            pltpu.VMEM(grad_out.shape, bf16),
            pltpu.SemaphoreType.DMA((3,)),
        ],
        compiler_params=ROOM,
        name="pick",
    )(picks, layer_input, grad_out)

    rows = jnp.concatenate(
        [hop(send[s * n_pick : (s + 1) * n_pick], "expert", s) for s in range(n_exp)], axis=0
    )
    gate_held, upper, lower = pl.pallas_call(
        load_kernel,
        out_shape=[jax.ShapeDtypeStruct(x.shape, x.dtype) for x in (gates, w_up, w_down)],
        in_specs=[HBM] * 4,
        out_specs=[VMEM] * 3,
        scratch_shapes=[pltpu.SemaphoreType.DMA((3,))],
        cost_estimate=pl.CostEstimate(
            flops=0, bytes_accessed=4 * w_up.size + 4 * w_down.size, transcendentals=0
        ),
        compiler_params=ROOM,
        name="load",
    )(send, gates, w_up, w_down)
    share = slots // n_hid
    parts = pl.pallas_call(
        cut_kernel,
        out_shape=[jax.ShapeDtypeStruct((share, 2 * cols), bf16)] * (n_dp - 1),
        in_specs=[ANY, VMEM],
        out_specs=[VMEM] * (n_dp - 1),
        compiler_params=ROOM,
        name="cut",
    )(gate_held, rows)
    parts = [hop(x, "dp", s + 1) for s, x in enumerate(parts)]

    factors = pl.pallas_call(
        factor_kernel,
        out_shape=jax.ShapeDtypeStruct((slots, 2 * units), bf16),
        in_specs=[ANY] + [VMEM] * 4,
        out_specs=VMEM,
        compiler_params=ROOM,
        cost_estimate=pl.CostEstimate(
            flops=4 * slots * w_up.size, bytes_accessed=4 * w_up.size, transcendentals=slots * units
        ),
        name="factor",
    )(parts[0], gate_held, rows, upper, lower)
    parts = pl.pallas_call(
        stack_kernel,
        out_shape=jax.ShapeDtypeStruct((n_dp - 1, share, 2 * cols), bf16),
        in_specs=[ANY] + [VMEM] * (n_dp - 1),
        out_specs=VMEM,
        compiler_params=ROOM,
        name="stack",
    )(factors, *parts)
    parts = [hop(parts, "hidden", t) for t in range(n_hid)]

    gathered = jnp.concatenate([hop(factors, "dp", s) for s in range(n_dp)], axis=0)

    piece = pl.pallas_call(
        functools.partial(piece_kernel, n_hid),
        out_shape=jax.ShapeDtypeStruct((n_exp * n_hid, n_pick, part), bf16),
        in_specs=[VMEM, VMEM],
        out_specs=VMEM,
        compiler_params=ROOM,
        cost_estimate=pl.CostEstimate(
            flops=2 * slots * w_up.size, bytes_accessed=2 * w_up.size, transcendentals=0
        ),
        name="piece",
    )(factors, upper)
    piece = pl.pallas_call(
        tie_kernel,
        out_shape=jax.ShapeDtypeStruct(piece.shape, piece.dtype),
        in_specs=[ANY] * n_hid,
        out_specs=ANY,
        input_output_aliases={0: 0},
        compiler_params=ROOM,
        name="tie",
    )(piece, *parts[1:])
    returned = lax.all_to_all(piece, ("expert", "hidden"), 0, 0)
    grad_rows = lax.dot_general(
        spread,
        returned.reshape(slots * n_hid, part),
        (((0,), (0,)), ((), ())),
        preferred_element_type=jnp.float32,
    ).astype(bf16)

    chunks = max(1, units // 256)
    grads = pl.pallas_call(
        functools.partial(weight_kernel, chunks, (n_dp, n_hid)),
        out_shape=[jax.ShapeDtypeStruct((1, cols, units), jnp.float32)] * 2,
        in_specs=[VMEM] * (n_hid + 2),
        out_specs=[HBM] * 2,
        scratch_shapes=[
            pltpu.VMEM((n_dp * slots, 2 * cols), bf16),
            pltpu.VMEM((2, cols, units), jnp.float32),
            pltpu.SemaphoreType.DMA((2, chunks)),
        ],
        compiler_params=ROOM,
        cost_estimate=pl.CostEstimate(
            flops=4 * n_dp * slots * cols * units, bytes_accessed=64 * cols * units, transcendentals=0
        ),
        name="weight",
    )(rows, *parts, gathered)
    return (grad_rows[None], *grads)


def solution(mesh):
    placed = (
        P("dp", "expert", None),
        P("dp", "expert", None),
        P("dp", "expert", None, None),
        P("dp", "expert", None, None),
        P("expert", None, "hidden"),
        P("expert", None, "hidden"),
    )
    return jax.shard_map(
        local,
        mesh=mesh,
        in_specs=placed,
        out_specs=(
            P("dp", "expert", "hidden"),
            P("expert", "dp", "hidden"),
            P("expert", "dp", "hidden"),
        ),
        check_vma=False,
    )
```

```python
import functools

import jax
import jax.numpy as jnp
from jax import lax
from jax.experimental import pallas as pl
from jax.experimental.pallas import tpu as pltpu
from jax.sharding import PartitionSpec as P

ROOT_TERM = 0.7978845608028654
CUBIC_TERM = 0.044715


def gelu_pair(pre):
    square = pre * pre
    inner = jnp.tanh(ROOT_TERM * (pre + CUBIC_TERM * square * pre))
    value = 0.5 * pre * (1.0 + inner)
    slope = 0.5 * (1.0 + inner) + 0.5 * pre * (1.0 - inner * inner) * ROOT_TERM * (
        1.0 + 3.0 * CUBIC_TERM * square
    )
    return value, slope


def hop(x, axis, step):
    n = lax.axis_size(axis)
    assert n & (n - 1) == 0
    return lax.ppermute(x, axis, [(i, i ^ step) for i in range(n)]) if step else x


def column(ref, order):
    n = ref.shape[-1]
    down = lax.broadcasted_iota(jnp.int32, (n, n), 0)
    along = lax.broadcasted_iota(jnp.int32, (n, n), 1)
    out = []
    for at in order:
        row = ref[0, 0, pl.ds(at, 1), :].astype(jnp.float32)
        out.append(jnp.sum(jnp.where(down == along, row, 0.0), axis=1, keepdims=True))
    return jnp.concatenate(out, axis=0)


def pick_kernel(n_hid, picks_hbm, tokens_hbm, upstream_hbm, rows_ref, spread_ref, *refs):
    picks_ref, tokens_ref, upstream_ref, sems = refs
    n_exp = picks_ref.shape[2]
    tok_dev, width = tokens_ref.shape[1:]
    copies = [
        pltpu.make_async_copy(picks_hbm, picks_ref, sems.at[0]),
        pltpu.make_async_copy(tokens_hbm, tokens_ref, sems.at[1]),
        pltpu.make_async_copy(upstream_hbm, upstream_ref, sems.at[2]),
    ]
    for copy in copies:
        copy.start()
    me = lax.axis_index("expert")
    copies[0].wait()

    def one_hot(order):
        wanted = column(picks_ref, order).astype(jnp.int32)
        spots = lax.broadcasted_iota(jnp.int32, (wanted.shape[0], tok_dev), 1)
        return jnp.where(wanted == spots, 1.0, 0.0).astype(jnp.bfloat16)

    selector = one_hot([me ^ s for s in range(n_exp)])
    spread_ref[...] = one_hot([e for e in range(n_exp) for _ in range(n_hid)])
    for at, copy, source in ((0, copies[1], tokens_ref), (width, copies[2], upstream_ref)):
        copy.wait()
        rows_ref[:, at : at + width] = jnp.dot(
            selector, source[0], preferred_element_type=jnp.float32
        ).astype(jnp.bfloat16)


def cut_kernel(after_ref, rows_ref, *out_refs):
    n_dp = len(out_refs) + 1
    share, wide = out_refs[0].shape
    cols = wide // 2
    width = rows_ref.shape[1] // 2
    my_dp = lax.axis_index("dp")
    spot = pl.ds(pl.multiple_of(lax.axis_index("hidden") * share, 16), share)
    for s, out_ref in enumerate(out_refs):
        at = (my_dp ^ (s + 1)) * cols
        for half in range(2):
            out_ref[:, half * cols : (half + 1) * cols] = rows_ref[
                spot, pl.ds(pl.multiple_of(half * width + at, 128), cols)
            ]


def load_kernel(after_ref, gates_hbm, upper_hbm, lower_hbm, gates_ref, upper_ref, lower_ref, sems):
    copies = [
        pltpu.make_async_copy(source, target, sems.at[k])
        for k, (source, target) in enumerate(
            ((gates_hbm, gates_ref), (upper_hbm, upper_ref), (lower_hbm, lower_ref))
        )
    ]
    for copy in copies:
        copy.start()
    for copy in copies:
        copy.wait()


def factor_kernel(after_ref, gates_ref, rows_ref, upper_ref, lower_ref, out_ref):
    n_exp = gates_ref.shape[2]
    width, units = upper_ref.shape[1:]
    me = lax.axis_index("expert")
    gate = column(gates_ref, [me ^ s for s in range(n_exp)])
    pre = jnp.dot(rows_ref[:, :width], upper_ref[0], preferred_element_type=jnp.float32)
    back = jnp.dot(rows_ref[:, width:], lower_ref[0], preferred_element_type=jnp.float32)
    value, slope = gelu_pair(pre)
    out_ref[:, :units] = (back * gate * slope).astype(jnp.bfloat16)
    out_ref[:, units:] = (value * gate).astype(jnp.bfloat16)


def piece_kernel(n_hid, factor_ref, upper_ref, out_ref):
    n_pick, part = out_ref.shape[1:]
    width, units = upper_ref.shape[1:]
    n_exp = out_ref.shape[0] // n_hid
    me = lax.axis_index("expert")
    piece = lax.dot_general(
        factor_ref[:, :units], upper_ref[0], (((1,), (1,)), ((), ())), preferred_element_type=jnp.float32
    )
    for s in range(n_exp):
        owner = (me ^ s) * n_hid
        for h in range(n_hid):
            out_ref[owner + h] = piece[
                s * n_pick : (s + 1) * n_pick, h * part : (h + 1) * part
            ].astype(jnp.bfloat16)


def stack_kernel(after_ref, *refs):
    *part_refs, out_ref = refs
    for s, part in enumerate(part_refs):
        out_ref[s] = part[...]


def weight_kernel(chunks, shape, own_ref, *refs):
    n_dp, n_hid = shape
    part_ref, factor_ref, up_ref, down_ref, side_ref, held, sems = refs
    units = factor_ref.shape[1] // 2
    cols = side_ref.shape[1] // 2
    width = own_ref.shape[1] // 2
    slots = own_ref.shape[0]
    rows = slots // n_hid
    my_hid = lax.axis_index("hidden")
    start = lax.axis_index("dp") * cols
    for half in range(2):
        side_ref[:slots, half * cols : (half + 1) * cols] = own_ref[
            :, pl.ds(pl.multiple_of(half * width + start, 128), cols)
        ]
    for t in range(n_hid):
        spot = (my_hid ^ t) * rows
        for s in range(1, n_dp):
            side_ref[pl.ds(pl.multiple_of(s * slots + spot, 16), rows), :] = part_ref[
                s - 1, t * rows : (t + 1) * rows
            ]
    step = units // chunks
    copies = []
    for which, out in ((0, up_ref), (1, down_ref)):
        for c in range(chunks):
            spot = pl.ds(c * step, step)
            held[which, :, spot] = lax.dot_general(
                side_ref[:, which * cols : (which + 1) * cols],
                factor_ref[:, pl.ds(which * units + c * step, step)],
                (((0,), (0,)), ((), ())),
                preferred_element_type=jnp.float32,
            )
            copy = pltpu.make_async_copy(
                held.at[which, :, spot], out.at[0, :, spot], sems.at[which, c]
            )
            copy.start()
            copies.append(copy)
    for copy in copies:
        copy.wait()


VMEM = pl.BlockSpec(memory_space=pltpu.VMEM)
ANY = pl.BlockSpec(memory_space=pl.ANY)
HBM = pl.BlockSpec(memory_space=pltpu.HBM)
ROOM = pltpu.CompilerParams(vmem_limit_bytes=16 << 20)


def local(layer_input, grad_out, picks, gates, w_up, w_down):
    tok_dev, width = layer_input.shape[1:]
    n_exp, n_pick = picks.shape[2:]
    slots = n_exp * n_pick
    units = w_up.shape[2]
    n_dp = lax.axis_size("dp")
    n_hid = lax.axis_size("hidden")
    cols = width // n_dp
    part = width // n_hid
    bf16 = jnp.bfloat16
    layer_input, grad_out, picks, gates, w_up, w_down = (
        pltpu.with_memory_space_constraint(x, pltpu.HBM)
        for x in (layer_input, grad_out, picks, gates, w_up, w_down)
    )

    send, spread = pl.pallas_call(
        functools.partial(pick_kernel, n_hid),
        out_shape=[
            jax.ShapeDtypeStruct((slots, 2 * width), bf16),
            jax.ShapeDtypeStruct((slots * n_hid, tok_dev), bf16),
        ],
        in_specs=[HBM] * 3,
        out_specs=[VMEM] * 2,
        scratch_shapes=[
            pltpu.VMEM(picks.shape, jnp.int32),
            pltpu.VMEM(layer_input.shape, bf16),
            pltpu.VMEM(grad_out.shape, bf16),
            pltpu.SemaphoreType.DMA((3,)),
        ],
        compiler_params=ROOM,
        name="pick",
    )(picks, layer_input, grad_out)

    rows = jnp.concatenate(
        [hop(send[s * n_pick : (s + 1) * n_pick], "expert", s) for s in range(n_exp)], axis=0
    )
    gate_held, upper, lower = pl.pallas_call(
        load_kernel,
        out_shape=[jax.ShapeDtypeStruct(x.shape, x.dtype) for x in (gates, w_up, w_down)],
        in_specs=[HBM] * 4,
        out_specs=[VMEM] * 3,
        scratch_shapes=[pltpu.SemaphoreType.DMA((3,))],
        cost_estimate=pl.CostEstimate(
            flops=0, bytes_accessed=4 * w_up.size + 4 * w_down.size, transcendentals=0
        ),
        compiler_params=ROOM,
        name="load",
    )(send, gates, w_up, w_down)
    share = slots // n_hid
    parts = pl.pallas_call(
        cut_kernel,
        out_shape=[jax.ShapeDtypeStruct((share, 2 * cols), bf16)] * (n_dp - 1),
        in_specs=[ANY, VMEM],
        out_specs=[VMEM] * (n_dp - 1),
        compiler_params=ROOM,
        name="cut",
    )(gate_held, rows)
    parts = [hop(x, "dp", s + 1) for s, x in enumerate(parts)]

    factors = pl.pallas_call(
        factor_kernel,
        out_shape=jax.ShapeDtypeStruct((slots, 2 * units), bf16),
        in_specs=[ANY] + [VMEM] * 4,
        out_specs=VMEM,
        compiler_params=ROOM,
        cost_estimate=pl.CostEstimate(
            flops=4 * slots * w_up.size, bytes_accessed=4 * w_up.size, transcendentals=slots * units
        ),
        name="factor",
    )(parts[0], gate_held, rows, upper, lower)
    parts = pl.pallas_call(
        stack_kernel,
        out_shape=jax.ShapeDtypeStruct((n_dp - 1, share, 2 * cols), bf16),
        in_specs=[ANY] + [VMEM] * (n_dp - 1),
        out_specs=VMEM,
        compiler_params=ROOM,
        name="stack",
    )(factors, *parts)
    parts = jnp.concatenate([hop(parts, "hidden", t) for t in range(n_hid)], axis=1)

    gathered = jnp.concatenate([hop(factors, "dp", s) for s in range(n_dp)], axis=0)

    piece = pl.pallas_call(
        functools.partial(piece_kernel, n_hid),
        out_shape=jax.ShapeDtypeStruct((n_exp * n_hid, n_pick, part), bf16),
        in_specs=[VMEM, VMEM],
        out_specs=VMEM,
        compiler_params=ROOM,
        cost_estimate=pl.CostEstimate(
            flops=2 * slots * w_up.size, bytes_accessed=2 * w_up.size, transcendentals=0
        ),
        name="piece",
    )(factors, upper)
    returned = lax.all_to_all(piece, ("expert", "hidden"), 0, 0)
    grad_rows = lax.dot_general(
        spread,
        returned.reshape(slots * n_hid, part),
        (((0,), (0,)), ((), ())),
        preferred_element_type=jnp.float32,
    ).astype(bf16)

    chunks = max(1, units // 256)
    grads = pl.pallas_call(
        functools.partial(weight_kernel, chunks, (n_dp, n_hid)),
        out_shape=[jax.ShapeDtypeStruct((1, cols, units), jnp.float32)] * 2,
        in_specs=[VMEM] * 3,
        out_specs=[HBM] * 2,
        scratch_shapes=[
            pltpu.VMEM((n_dp * slots, 2 * cols), bf16),
            pltpu.VMEM((2, cols, units), jnp.float32),
            pltpu.SemaphoreType.DMA((2, chunks)),
        ],
        compiler_params=ROOM,
        cost_estimate=pl.CostEstimate(
            flops=4 * n_dp * slots * cols * units, bytes_accessed=64 * cols * units, transcendentals=0
        ),
        name="weight",
    )(rows, parts, gathered)
    return (grad_rows[None], *grads)


def solution(mesh):
    placed = (
        P("dp", "expert", None),
        P("dp", "expert", None),
        P("dp", "expert", None, None),
        P("dp", "expert", None, None),
        P("expert", None, "hidden"),
        P("expert", None, "hidden"),
    )
    return jax.shard_map(
        local,
        mesh=mesh,
        in_specs=placed,
        out_specs=(
            P("dp", "expert", "hidden"),
            P("expert", "dp", "hidden"),
            P("expert", "dp", "hidden"),
        ),
        check_vma=False,
    )
```

```python
import functools

import jax
import jax.numpy as jnp
from jax import lax
from jax.experimental import pallas as pl
from jax.experimental.pallas import tpu as pltpu
from jax.sharding import PartitionSpec as P

ROOT_TERM = 0.7978845608028654
CUBIC_TERM = 0.044715


def gelu_pair(pre):
    square = pre * pre
    inner = jnp.tanh(ROOT_TERM * (pre + CUBIC_TERM * square * pre))
    value = 0.5 * pre * (1.0 + inner)
    slope = 0.5 * (1.0 + inner) + 0.5 * pre * (1.0 - inner * inner) * ROOT_TERM * (
        1.0 + 3.0 * CUBIC_TERM * square
    )
    return value, slope


def hop(x, axis, step):
    n = lax.axis_size(axis)
    assert n & (n - 1) == 0
    return lax.ppermute(x, axis, [(i, i ^ step) for i in range(n)]) if step else x


def column(ref, order):
    n = ref.shape[-1]
    down = lax.broadcasted_iota(jnp.int32, (n, n), 0)
    along = lax.broadcasted_iota(jnp.int32, (n, n), 1)
    out = []
    for at in order:
        row = ref[0, 0, pl.ds(at, 1), :].astype(jnp.float32)
        out.append(jnp.sum(jnp.where(down == along, row, 0.0), axis=1, keepdims=True))
    return jnp.concatenate(out, axis=0)


def pick_kernel(n_hid, picks_hbm, tokens_hbm, upstream_hbm, rows_ref, spread_ref, *refs):
    picks_ref, tokens_ref, upstream_ref, sems = refs
    n_exp = picks_ref.shape[2]
    tok_dev, width = tokens_ref.shape[1:]
    copies = [
        pltpu.make_async_copy(picks_hbm, picks_ref, sems.at[0]),
        pltpu.make_async_copy(tokens_hbm, tokens_ref, sems.at[1]),
        pltpu.make_async_copy(upstream_hbm, upstream_ref, sems.at[2]),
    ]
    for copy in copies:
        copy.start()
    me = lax.axis_index("expert")
    copies[0].wait()

    def one_hot(order):
        wanted = column(picks_ref, order).astype(jnp.int32)
        spots = lax.broadcasted_iota(jnp.int32, (wanted.shape[0], tok_dev), 1)
        return jnp.where(wanted == spots, 1.0, 0.0).astype(jnp.bfloat16)

    selector = one_hot([me ^ s for s in range(n_exp)])
    spread_ref[...] = one_hot([e for e in range(n_exp) for _ in range(n_hid)])
    for at, copy, source in ((0, copies[1], tokens_ref), (width, copies[2], upstream_ref)):
        copy.wait()
        rows_ref[:, at : at + width] = jnp.dot(
            selector, source[0], preferred_element_type=jnp.float32
        ).astype(jnp.bfloat16)


def cut_kernel(after_ref, rows_ref, *out_refs):
    n_dp = len(out_refs) + 1
    share, wide = out_refs[0].shape
    cols = wide // 2
    width = rows_ref.shape[1] // 2
    my_dp = lax.axis_index("dp")
    spot = pl.ds(pl.multiple_of(lax.axis_index("hidden") * share, 16), share)
    for s, out_ref in enumerate(out_refs):
        at = (my_dp ^ (s + 1)) * cols
        for half in range(2):
            out_ref[:, half * cols : (half + 1) * cols] = rows_ref[
                spot, pl.ds(pl.multiple_of(half * width + at, 128), cols)
            ]


def load_kernel(after_ref, gates_hbm, upper_hbm, lower_hbm, gates_ref, upper_ref, lower_ref, sems):
    copies = [
        pltpu.make_async_copy(source, target, sems.at[k])
        for k, (source, target) in enumerate(
            ((gates_hbm, gates_ref), (upper_hbm, upper_ref), (lower_hbm, lower_ref))
        )
    ]
    for copy in copies:
        copy.start()
    for copy in copies:
        copy.wait()


def factor_kernel(after_ref, gates_ref, rows_ref, upper_ref, lower_ref, out_ref):
    n_exp = gates_ref.shape[2]
    width, units = upper_ref.shape[1:]
    me = lax.axis_index("expert")
    gate = column(gates_ref, [me ^ s for s in range(n_exp)])
    pre = jnp.dot(rows_ref[:, :width], upper_ref[0], preferred_element_type=jnp.float32)
    back = jnp.dot(rows_ref[:, width:], lower_ref[0], preferred_element_type=jnp.float32)
    value, slope = gelu_pair(pre)
    out_ref[:, :units] = (back * gate * slope).astype(jnp.bfloat16)
    out_ref[:, units:] = (value * gate).astype(jnp.bfloat16)


def piece_kernel(n_hid, factor_ref, upper_ref, out_ref):
    n_pick, part = out_ref.shape[1:]
    width, units = upper_ref.shape[1:]
    n_exp = out_ref.shape[0] // n_hid
    me = lax.axis_index("expert")
    piece = lax.dot_general(
        factor_ref[:, :units], upper_ref[0], (((1,), (1,)), ((), ())), preferred_element_type=jnp.float32
    )
    for s in range(n_exp):
        owner = (me ^ s) * n_hid
        for h in range(n_hid):
            out_ref[owner + h] = piece[
                s * n_pick : (s + 1) * n_pick, h * part : (h + 1) * part
            ].astype(jnp.bfloat16)


def stack_kernel(after_ref, *refs):
    *part_refs, out_ref = refs
    for s, part in enumerate(part_refs):
        out_ref[s] = part[...]


def tie_kernel(*refs):
    pass


def weight_kernel(chunks, shape, own_ref, *refs):
    n_dp, n_hid = shape
    part_refs, refs = refs[:n_hid], refs[n_hid:]
    factor_ref, up_ref, down_ref, side_ref, held, sems = refs
    units = factor_ref.shape[1] // 2
    cols = side_ref.shape[1] // 2
    width = own_ref.shape[1] // 2
    slots = own_ref.shape[0]
    rows = slots // n_hid
    my_hid = lax.axis_index("hidden")
    start = lax.axis_index("dp") * cols
    for half in range(2):
        side_ref[:slots, half * cols : (half + 1) * cols] = own_ref[
            :, pl.ds(pl.multiple_of(half * width + start, 128), cols)
        ]
    for t, part in enumerate(part_refs):
        spot = (my_hid ^ t) * rows
        for s in range(1, n_dp):
            side_ref[pl.ds(pl.multiple_of(s * slots + spot, 16), rows), :] = part[s - 1]
    step = units // chunks
    copies = []
    for which, out in ((0, up_ref), (1, down_ref)):
        for c in range(chunks):
            spot = pl.ds(c * step, step)
            held[which, :, spot] = lax.dot_general(
                side_ref[:, which * cols : (which + 1) * cols],
                factor_ref[:, pl.ds(which * units + c * step, step)],
                (((0,), (0,)), ((), ())),
                preferred_element_type=jnp.float32,
            )
            copy = pltpu.make_async_copy(
                held.at[which, :, spot], out.at[0, :, spot], sems.at[which, c]
            )
            copy.start()
            copies.append(copy)
    for copy in copies:
        copy.wait()


VMEM = pl.BlockSpec(memory_space=pltpu.VMEM)
ANY = pl.BlockSpec(memory_space=pl.ANY)
HBM = pl.BlockSpec(memory_space=pltpu.HBM)
ROOM = pltpu.CompilerParams(vmem_limit_bytes=16 << 20)


def local(layer_input, grad_out, picks, gates, w_up, w_down):
    tok_dev, width = layer_input.shape[1:]
    n_exp, n_pick = picks.shape[2:]
    slots = n_exp * n_pick
    units = w_up.shape[2]
    n_dp = lax.axis_size("dp")
    n_hid = lax.axis_size("hidden")
    cols = width // n_dp
    part = width // n_hid
    bf16 = jnp.bfloat16
    layer_input, grad_out, picks, gates, w_up, w_down = (
        pltpu.with_memory_space_constraint(x, pltpu.HBM)
        for x in (layer_input, grad_out, picks, gates, w_up, w_down)
    )

    send, spread = pl.pallas_call(
        functools.partial(pick_kernel, n_hid),
        out_shape=[
            jax.ShapeDtypeStruct((slots, 2 * width), bf16),
            jax.ShapeDtypeStruct((slots * n_hid, tok_dev), bf16),
        ],
        in_specs=[HBM] * 3,
        out_specs=[VMEM] * 2,
        scratch_shapes=[
            pltpu.VMEM(picks.shape, jnp.int32),
            pltpu.VMEM(layer_input.shape, bf16),
            pltpu.VMEM(grad_out.shape, bf16),
            pltpu.SemaphoreType.DMA((3,)),
        ],
        compiler_params=ROOM,
        name="pick",
    )(picks, layer_input, grad_out)

    rows = jnp.concatenate(
        [hop(send[s * n_pick : (s + 1) * n_pick], "expert", s) for s in range(n_exp)], axis=0
    )
    gate_held, upper, lower = pl.pallas_call(
        load_kernel,
        out_shape=[jax.ShapeDtypeStruct(x.shape, x.dtype) for x in (gates, w_up, w_down)],
        in_specs=[HBM] * 4,
        out_specs=[VMEM] * 3,
        scratch_shapes=[pltpu.SemaphoreType.DMA((3,))],
        cost_estimate=pl.CostEstimate(
            flops=0, bytes_accessed=4 * w_up.size + 4 * w_down.size, transcendentals=0
        ),
        compiler_params=ROOM,
        name="load",
    )(send, gates, w_up, w_down)
    share = slots // n_hid
    parts = pl.pallas_call(
        cut_kernel,
        out_shape=[jax.ShapeDtypeStruct((share, 2 * cols), bf16)] * (n_dp - 1),
        in_specs=[ANY, VMEM],
        out_specs=[VMEM] * (n_dp - 1),
        compiler_params=ROOM,
        name="cut",
    )(gate_held, rows)
    parts = [hop(x, "dp", s + 1) for s, x in enumerate(parts)]

    factors = pl.pallas_call(
        factor_kernel,
        out_shape=jax.ShapeDtypeStruct((slots, 2 * units), bf16),
        in_specs=[ANY] + [VMEM] * 4,
        out_specs=VMEM,
        compiler_params=ROOM,
        cost_estimate=pl.CostEstimate(
            flops=4 * slots * w_up.size, bytes_accessed=4 * w_up.size, transcendentals=slots * units
        ),
        name="factor",
    )(parts[0], gate_held, rows, upper, lower)
    parts = pl.pallas_call(
        stack_kernel,
        out_shape=jax.ShapeDtypeStruct((n_dp - 1, share, 2 * cols), bf16),
        in_specs=[ANY] + [VMEM] * (n_dp - 1),
        out_specs=VMEM,
        compiler_params=ROOM,
        name="stack",
    )(factors, *parts)
    parts = [hop(parts, "hidden", t) for t in range(n_hid)]

    gathered = [hop(factors, "dp", s) for s in range(n_dp)]
    while len(gathered) > 1:
        pairs = [jnp.concatenate(gathered[k : k + 2], axis=0) for k in range(0, len(gathered), 2)]
        gathered = lax.optimization_barrier(pairs)
    gathered = gathered[0]

    piece = pl.pallas_call(
        functools.partial(piece_kernel, n_hid),
        out_shape=jax.ShapeDtypeStruct((n_exp * n_hid, n_pick, part), bf16),
        in_specs=[VMEM, VMEM],
        out_specs=VMEM,
        compiler_params=ROOM,
        cost_estimate=pl.CostEstimate(
            flops=2 * slots * w_up.size, bytes_accessed=2 * w_up.size, transcendentals=0
        ),
        name="piece",
    )(factors, upper)
    piece = pl.pallas_call(
        tie_kernel,
        out_shape=jax.ShapeDtypeStruct(piece.shape, piece.dtype),
        in_specs=[ANY] * n_hid,
        out_specs=ANY,
        input_output_aliases={0: 0},
        compiler_params=ROOM,
        name="tie",
    )(piece, *parts[1:])
    returned = lax.all_to_all(piece, ("expert", "hidden"), 0, 0)
    grad_rows = lax.dot_general(
        spread,
        returned.reshape(slots * n_hid, part),
        (((0,), (0,)), ((), ())),
        preferred_element_type=jnp.float32,
    ).astype(bf16)

    chunks = max(1, units // 256)
    grads = pl.pallas_call(
        functools.partial(weight_kernel, chunks, (n_dp, n_hid)),
        out_shape=[jax.ShapeDtypeStruct((1, cols, units), jnp.float32)] * 2,
        in_specs=[VMEM] * (n_hid + 2),
        out_specs=[HBM] * 2,
        scratch_shapes=[
            pltpu.VMEM((n_dp * slots, 2 * cols), bf16),
            pltpu.VMEM((2, cols, units), jnp.float32),
            pltpu.SemaphoreType.DMA((2, chunks)),
        ],
        compiler_params=ROOM,
        cost_estimate=pl.CostEstimate(
            flops=4 * n_dp * slots * cols * units, bytes_accessed=64 * cols * units, transcendentals=0
        ),
        name="weight",
    )(rows, *parts, gathered)
    return (grad_rows[None], *grads)


def solution(mesh):
    placed = (
        P("dp", "expert", None),
        P("dp", "expert", None),
        P("dp", "expert", None, None),
        P("dp", "expert", None, None),
        P("expert", None, "hidden"),
        P("expert", None, "hidden"),
    )
    return jax.shard_map(
        local,
        mesh=mesh,
        in_specs=placed,
        out_specs=(
            P("dp", "expert", "hidden"),
            P("expert", "dp", "hidden"),
            P("expert", "dp", "hidden"),
        ),
        check_vma=False,
    )
```

```python
import functools

import jax
import jax.numpy as jnp
from jax import lax
from jax.experimental import pallas as pl
from jax.experimental.pallas import tpu as pltpu
from jax.sharding import PartitionSpec as P

ROOT_TERM = 0.7978845608028654
CUBIC_TERM = 0.044715


def gelu_pair(pre):
    square = pre * pre
    inner = jnp.tanh(ROOT_TERM * (pre + CUBIC_TERM * square * pre))
    value = 0.5 * pre * (1.0 + inner)
    slope = 0.5 * (1.0 + inner) + 0.5 * pre * (1.0 - inner * inner) * ROOT_TERM * (
        1.0 + 3.0 * CUBIC_TERM * square
    )
    return value, slope


def hop(x, axis, step):
    n = lax.axis_size(axis)
    assert n & (n - 1) == 0
    return lax.ppermute(x, axis, [(i, i ^ step) for i in range(n)]) if step else x


def column(ref, order):
    n = ref.shape[-1]
    down = lax.broadcasted_iota(jnp.int32, (n, n), 0)
    along = lax.broadcasted_iota(jnp.int32, (n, n), 1)
    out = []
    for at in order:
        row = ref[0, 0, pl.ds(at, 1), :].astype(jnp.float32)
        out.append(jnp.sum(jnp.where(down == along, row, 0.0), axis=1, keepdims=True))
    return jnp.concatenate(out, axis=0)


def pick_kernel(n_hid, picks_hbm, tokens_hbm, upstream_hbm, rows_ref, spread_ref, *refs):
    picks_ref, tokens_ref, upstream_ref, sems = refs
    n_exp = picks_ref.shape[2]
    tok_dev, width = tokens_ref.shape[1:]
    copies = [
        pltpu.make_async_copy(picks_hbm, picks_ref, sems.at[0]),
        pltpu.make_async_copy(tokens_hbm, tokens_ref, sems.at[1]),
        pltpu.make_async_copy(upstream_hbm, upstream_ref, sems.at[2]),
    ]
    for copy in copies:
        copy.start()
    me = lax.axis_index("expert")
    copies[0].wait()

    def one_hot(order):
        wanted = column(picks_ref, order).astype(jnp.int32)
        spots = lax.broadcasted_iota(jnp.int32, (wanted.shape[0], tok_dev), 1)
        return jnp.where(wanted == spots, 1.0, 0.0).astype(jnp.bfloat16)

    selector = one_hot([me ^ s for s in range(n_exp)])
    spread_ref[...] = one_hot([e for e in range(n_exp) for _ in range(n_hid)])
    for at, copy, source in ((0, copies[1], tokens_ref), (width, copies[2], upstream_ref)):
        copy.wait()
        rows_ref[:, at : at + width] = jnp.dot(
            selector, source[0], preferred_element_type=jnp.float32
        ).astype(jnp.bfloat16)


def cut_kernel(after_ref, rows_ref, *out_refs):
    n_dp = len(out_refs) + 1
    share, wide = out_refs[0].shape
    cols = wide // 2
    width = rows_ref.shape[1] // 2
    my_dp = lax.axis_index("dp")
    spot = pl.ds(pl.multiple_of(lax.axis_index("hidden") * share, 16), share)
    for s, out_ref in enumerate(out_refs):
        at = (my_dp ^ (s + 1)) * cols
        for half in range(2):
            out_ref[:, half * cols : (half + 1) * cols] = rows_ref[
                spot, pl.ds(pl.multiple_of(half * width + at, 128), cols)
            ]


def load_kernel(after_ref, gates_hbm, upper_hbm, lower_hbm, gates_ref, upper_ref, lower_ref, sems):
    copies = [
        pltpu.make_async_copy(source, target, sems.at[k])
        for k, (source, target) in enumerate(
            ((gates_hbm, gates_ref), (upper_hbm, upper_ref), (lower_hbm, lower_ref))
        )
    ]
    for copy in copies:
        copy.start()
    for copy in copies:
        copy.wait()


def factor_kernel(after_ref, gates_ref, rows_ref, upper_ref, lower_ref, out_ref):
    n_exp = gates_ref.shape[2]
    width, units = upper_ref.shape[1:]
    me = lax.axis_index("expert")
    gate = column(gates_ref, [me ^ s for s in range(n_exp)])
    pre = jnp.dot(rows_ref[:, :width], upper_ref[0], preferred_element_type=jnp.float32)
    back = jnp.dot(rows_ref[:, width:], lower_ref[0], preferred_element_type=jnp.float32)
    value, slope = gelu_pair(pre)
    out_ref[:, :units] = (back * gate * slope).astype(jnp.bfloat16)
    out_ref[:, units:] = (value * gate).astype(jnp.bfloat16)


def piece_kernel(n_hid, factor_ref, upper_ref, out_ref):
    n_pick, part = out_ref.shape[1:]
    width, units = upper_ref.shape[1:]
    n_exp = out_ref.shape[0] // n_hid
    me = lax.axis_index("expert")
    piece = lax.dot_general(
        factor_ref[:, :units], upper_ref[0], (((1,), (1,)), ((), ())), preferred_element_type=jnp.float32
    )
    for s in range(n_exp):
        owner = (me ^ s) * n_hid
        for h in range(n_hid):
            out_ref[owner + h] = piece[
                s * n_pick : (s + 1) * n_pick, h * part : (h + 1) * part
            ].astype(jnp.bfloat16)


def stack_kernel(after_ref, *refs):
    *part_refs, out_ref = refs
    for s, part in enumerate(part_refs):
        out_ref[s] = part[...]


def tie_kernel(*refs):
    pass


def weight_kernel(chunks, shape, own_ref, *refs):
    n_dp, n_hid = shape
    part_refs, refs = refs[:n_hid], refs[n_hid:]
    factor_ref, up_ref, down_ref, side_ref, held, sems = refs
    units = factor_ref.shape[1] // 2
    cols = side_ref.shape[1] // 2
    width = own_ref.shape[1] // 2
    slots = own_ref.shape[0]
    rows = slots // n_hid
    my_hid = lax.axis_index("hidden")
    start = lax.axis_index("dp") * cols
    for half in range(2):
        side_ref[:slots, half * cols : (half + 1) * cols] = own_ref[
            :, pl.ds(pl.multiple_of(half * width + start, 128), cols)
        ]
    for t, part in enumerate(part_refs):
        spot = (my_hid ^ t) * rows
        for s in range(1, n_dp):
            side_ref[pl.ds(pl.multiple_of(s * slots + spot, 16), rows), :] = part[s - 1]
    step = units // chunks
    copies = []
    for which, out in ((0, up_ref), (1, down_ref)):
        for c in range(chunks):
            spot = pl.ds(c * step, step)
            held[which, :, spot] = lax.dot_general(
                side_ref[:, which * cols : (which + 1) * cols],
                factor_ref[:, pl.ds(which * units + c * step, step)],
                (((0,), (0,)), ((), ())),
                preferred_element_type=jnp.float32,
            )
            copy = pltpu.make_async_copy(
                held.at[which, :, spot], out.at[0, :, spot], sems.at[which, c]
            )
            copy.start()
            copies.append(copy)
    for copy in copies:
        copy.wait()


VMEM = pl.BlockSpec(memory_space=pltpu.VMEM)
ANY = pl.BlockSpec(memory_space=pl.ANY)
HBM = pl.BlockSpec(memory_space=pltpu.HBM)
ROOM = pltpu.CompilerParams(vmem_limit_bytes=16 << 20)


def local(layer_input, grad_out, picks, gates, w_up, w_down):
    tok_dev, width = layer_input.shape[1:]
    n_exp, n_pick = picks.shape[2:]
    slots = n_exp * n_pick
    units = w_up.shape[2]
    n_dp = lax.axis_size("dp")
    n_hid = lax.axis_size("hidden")
    cols = width // n_dp
    part = width // n_hid
    bf16 = jnp.bfloat16
    layer_input, grad_out, picks, gates, w_up, w_down = (
        pltpu.with_memory_space_constraint(x, pltpu.HBM)
        for x in (layer_input, grad_out, picks, gates, w_up, w_down)
    )

    send, spread = pl.pallas_call(
        functools.partial(pick_kernel, n_hid),
        out_shape=[
            jax.ShapeDtypeStruct((slots, 2 * width), bf16),
            jax.ShapeDtypeStruct((slots * n_hid, tok_dev), bf16),
        ],
        in_specs=[HBM] * 3,
        out_specs=[VMEM] * 2,
        scratch_shapes=[
            pltpu.VMEM(picks.shape, jnp.int32),
            pltpu.VMEM(layer_input.shape, bf16),
            pltpu.VMEM(grad_out.shape, bf16),
            pltpu.SemaphoreType.DMA((3,)),
        ],
        compiler_params=ROOM,
        name="pick",
    )(picks, layer_input, grad_out)

    rows = jnp.concatenate(
        [hop(send[s * n_pick : (s + 1) * n_pick], "expert", s) for s in range(n_exp)], axis=0
    )
    gate_held, upper, lower = pl.pallas_call(
        load_kernel,
        out_shape=[jax.ShapeDtypeStruct(x.shape, x.dtype) for x in (gates, w_up, w_down)],
        in_specs=[HBM] * 4,
        out_specs=[VMEM] * 3,
        scratch_shapes=[pltpu.SemaphoreType.DMA((3,))],
        cost_estimate=pl.CostEstimate(
            flops=0, bytes_accessed=4 * w_up.size + 4 * w_down.size, transcendentals=0
        ),
        compiler_params=ROOM,
        name="load",
    )(send, gates, w_up, w_down)
    share = slots // n_hid
    parts = pl.pallas_call(
        cut_kernel,
        out_shape=[jax.ShapeDtypeStruct((share, 2 * cols), bf16)] * (n_dp - 1),
        in_specs=[ANY, VMEM],
        out_specs=[VMEM] * (n_dp - 1),
        compiler_params=ROOM,
        name="cut",
    )(gate_held, rows)
    parts = [hop(parts[s], "dp", s + 1) for s in reversed(range(n_dp - 1))][::-1]

    factors = pl.pallas_call(
        factor_kernel,
        out_shape=jax.ShapeDtypeStruct((slots, 2 * units), bf16),
        in_specs=[ANY] + [VMEM] * 4,
        out_specs=VMEM,
        compiler_params=ROOM,
        cost_estimate=pl.CostEstimate(
            flops=4 * slots * w_up.size, bytes_accessed=4 * w_up.size, transcendentals=slots * units
        ),
        name="factor",
    )(parts[-1], gate_held, rows, upper, lower)
    parts = pl.pallas_call(
        stack_kernel,
        out_shape=jax.ShapeDtypeStruct((n_dp - 1, share, 2 * cols), bf16),
        in_specs=[ANY] + [VMEM] * (n_dp - 1),
        out_specs=VMEM,
        compiler_params=ROOM,
        name="stack",
    )(factors, *parts)
    parts = [hop(parts, "hidden", t) for t in range(n_hid)]

    gathered = jnp.concatenate([hop(factors, "dp", s) for s in range(n_dp)], axis=0)

    piece = pl.pallas_call(
        functools.partial(piece_kernel, n_hid),
        out_shape=jax.ShapeDtypeStruct((n_exp * n_hid, n_pick, part), bf16),
        in_specs=[VMEM, VMEM],
        out_specs=VMEM,
        compiler_params=ROOM,
        cost_estimate=pl.CostEstimate(
            flops=2 * slots * w_up.size, bytes_accessed=2 * w_up.size, transcendentals=0
        ),
        name="piece",
    )(factors, upper)
    piece = pl.pallas_call(
        tie_kernel,
        out_shape=jax.ShapeDtypeStruct(piece.shape, piece.dtype),
        in_specs=[ANY] * n_hid,
        out_specs=ANY,
        input_output_aliases={0: 0},
        compiler_params=ROOM,
        name="tie",
    )(piece, *parts[1:])
    returned = lax.all_to_all(piece, ("expert", "hidden"), 0, 0)
    grad_rows = lax.dot_general(
        spread,
        returned.reshape(slots * n_hid, part),
        (((0,), (0,)), ((), ())),
        preferred_element_type=jnp.float32,
    ).astype(bf16)

    chunks = max(1, units // 256)
    grads = pl.pallas_call(
        functools.partial(weight_kernel, chunks, (n_dp, n_hid)),
        out_shape=[jax.ShapeDtypeStruct((1, cols, units), jnp.float32)] * 2,
        in_specs=[VMEM] * (n_hid + 2),
        out_specs=[HBM] * 2,
        scratch_shapes=[
            pltpu.VMEM((n_dp * slots, 2 * cols), bf16),
            pltpu.VMEM((2, cols, units), jnp.float32),
            pltpu.SemaphoreType.DMA((2, chunks)),
        ],
        compiler_params=ROOM,
        cost_estimate=pl.CostEstimate(
            flops=4 * n_dp * slots * cols * units, bytes_accessed=64 * cols * units, transcendentals=0
        ),
        name="weight",
    )(rows, *parts, gathered)
    return (grad_rows[None], *grads)


def solution(mesh):
    placed = (
        P("dp", "expert", None),
        P("dp", "expert", None),
        P("dp", "expert", None, None),
        P("dp", "expert", None, None),
        P("expert", None, "hidden"),
        P("expert", None, "hidden"),
    )
    return jax.shard_map(
        local,
        mesh=mesh,
        in_specs=placed,
        out_specs=(
            P("dp", "expert", "hidden"),
            P("expert", "dp", "hidden"),
            P("expert", "dp", "hidden"),
        ),
        check_vma=False,
    )
```

```python
import functools

import jax
import jax.numpy as jnp
from jax import lax
from jax.experimental import pallas as pl
from jax.experimental.pallas import tpu as pltpu
from jax.sharding import PartitionSpec as P

ROOT_TERM = 0.7978845608028654
CUBIC_TERM = 0.044715


def gelu_pair(pre):
    square = pre * pre
    inner = jnp.tanh(ROOT_TERM * (pre + CUBIC_TERM * square * pre))
    value = 0.5 * pre * (1.0 + inner)
    slope = 0.5 * (1.0 + inner) + 0.5 * pre * (1.0 - inner * inner) * ROOT_TERM * (
        1.0 + 3.0 * CUBIC_TERM * square
    )
    return value, slope


def hop(x, axis, step):
    n = lax.axis_size(axis)
    assert n & (n - 1) == 0
    return lax.ppermute(x, axis, [(i, i ^ step) for i in range(n)]) if step else x


def column(ref, order):
    n = ref.shape[-1]
    down = lax.broadcasted_iota(jnp.int32, (n, n), 0)
    along = lax.broadcasted_iota(jnp.int32, (n, n), 1)
    out = []
    for at in order:
        row = ref[0, 0, pl.ds(at, 1), :].astype(jnp.float32)
        out.append(jnp.sum(jnp.where(down == along, row, 0.0), axis=1, keepdims=True))
    return jnp.concatenate(out, axis=0)


def pick_kernel(n_hid, picks_hbm, tokens_hbm, upstream_hbm, rows_ref, spread_ref, *refs):
    picks_ref, tokens_ref, upstream_ref, sems = refs
    n_exp = picks_ref.shape[2]
    tok_dev, width = tokens_ref.shape[1:]
    copies = [
        pltpu.make_async_copy(picks_hbm, picks_ref, sems.at[0]),
        pltpu.make_async_copy(tokens_hbm, tokens_ref, sems.at[1]),
        pltpu.make_async_copy(upstream_hbm, upstream_ref, sems.at[2]),
    ]
    for copy in copies:
        copy.start()
    me = lax.axis_index("expert")
    copies[0].wait()

    def one_hot(order):
        wanted = column(picks_ref, order).astype(jnp.int32)
        spots = lax.broadcasted_iota(jnp.int32, (wanted.shape[0], tok_dev), 1)
        return jnp.where(wanted == spots, 1.0, 0.0).astype(jnp.bfloat16)

    selector = one_hot([me ^ s for s in range(n_exp)])
    spread_ref[...] = one_hot([e for e in range(n_exp) for _ in range(n_hid)])
    for at, copy, source in ((0, copies[1], tokens_ref), (width, copies[2], upstream_ref)):
        copy.wait()
        rows_ref[:, at : at + width] = jnp.dot(
            selector, source[0], preferred_element_type=jnp.float32
        ).astype(jnp.bfloat16)


def cut_kernel(after_ref, rows_ref, *out_refs):
    n_dp = len(out_refs) + 1
    share, wide = out_refs[0].shape
    cols = wide // 2
    width = rows_ref.shape[1] // 2
    my_dp = lax.axis_index("dp")
    spot = pl.ds(pl.multiple_of(lax.axis_index("hidden") * share, 16), share)
    for s, out_ref in enumerate(out_refs):
        at = (my_dp ^ (s + 1)) * cols
        for half in range(2):
            out_ref[:, half * cols : (half + 1) * cols] = rows_ref[
                spot, pl.ds(pl.multiple_of(half * width + at, 128), cols)
            ]


def load_kernel(after_ref, gates_hbm, upper_hbm, lower_hbm, gates_ref, upper_ref, lower_ref, sems):
    copies = [
        pltpu.make_async_copy(source, target, sems.at[k])
        for k, (source, target) in enumerate(
            ((gates_hbm, gates_ref), (upper_hbm, upper_ref), (lower_hbm, lower_ref))
        )
    ]
    for copy in copies:
        copy.start()
    for copy in copies:
        copy.wait()


def factor_kernel(after_ref, gates_ref, rows_ref, upper_ref, lower_ref, out_ref):
    n_exp = gates_ref.shape[2]
    width, units = upper_ref.shape[1:]
    me = lax.axis_index("expert")
    gate = column(gates_ref, [me ^ s for s in range(n_exp)])
    pre = jnp.dot(rows_ref[:, :width], upper_ref[0], preferred_element_type=jnp.float32)
    back = jnp.dot(rows_ref[:, width:], lower_ref[0], preferred_element_type=jnp.float32)
    value, slope = gelu_pair(pre)
    out_ref[:, :units] = (back * gate * slope).astype(jnp.bfloat16)
    out_ref[:, units:] = (value * gate).astype(jnp.bfloat16)


def piece_kernel(n_hid, factor_ref, upper_ref, out_ref):
    n_pick, part = out_ref.shape[1:]
    width, units = upper_ref.shape[1:]
    n_exp = out_ref.shape[0] // n_hid
    me = lax.axis_index("expert")
    piece = lax.dot_general(
        factor_ref[:, :units], upper_ref[0], (((1,), (1,)), ((), ())), preferred_element_type=jnp.float32
    )
    for s in range(n_exp):
        owner = (me ^ s) * n_hid
        for h in range(n_hid):
            out_ref[owner + h] = piece[
                s * n_pick : (s + 1) * n_pick, h * part : (h + 1) * part
            ].astype(jnp.bfloat16)


def tie_kernel(*refs):
    pass


def weight_kernel(chunks, shape, own_ref, *refs):
    n_dp, n_hid = shape
    part_refs, refs = refs[: 2 * n_hid], refs[2 * n_hid :]
    factor_ref, up_ref, down_ref, side_ref, held, sems = refs
    units = factor_ref.shape[1] // 2
    cols = side_ref.shape[1] // 2
    width = own_ref.shape[1] // 2
    slots = own_ref.shape[0]
    rows = slots // n_hid
    my_hid = lax.axis_index("hidden")
    start = lax.axis_index("dp") * cols
    for half in range(2):
        side_ref[:slots, half * cols : (half + 1) * cols] = own_ref[
            :, pl.ds(pl.multiple_of(half * width + start, 128), cols)
        ]
    for k, part in enumerate(part_refs):
        spot = (my_hid ^ (k // 2)) * rows
        half = k % 2
        for s in range(1, n_dp):
            side_ref[
                pl.ds(pl.multiple_of(s * slots + spot, 16), rows), half * cols : (half + 1) * cols
            ] = part[s - 1]
    step = units // chunks
    copies = []
    for which, out in ((0, up_ref), (1, down_ref)):
        for c in range(chunks):
            spot = pl.ds(c * step, step)
            held[which, :, spot] = lax.dot_general(
                side_ref[:, which * cols : (which + 1) * cols],
                factor_ref[:, pl.ds(which * units + c * step, step)],
                (((0,), (0,)), ((), ())),
                preferred_element_type=jnp.float32,
            )
            copy = pltpu.make_async_copy(
                held.at[which, :, spot], out.at[0, :, spot], sems.at[which, c]
            )
            copy.start()
            copies.append(copy)
    for copy in copies:
        copy.wait()


VMEM = pl.BlockSpec(memory_space=pltpu.VMEM)
ANY = pl.BlockSpec(memory_space=pl.ANY)
HBM = pl.BlockSpec(memory_space=pltpu.HBM)
ROOM = pltpu.CompilerParams(vmem_limit_bytes=16 << 20)


def local(layer_input, grad_out, picks, gates, w_up, w_down):
    tok_dev, width = layer_input.shape[1:]
    n_exp, n_pick = picks.shape[2:]
    slots = n_exp * n_pick
    units = w_up.shape[2]
    n_dp = lax.axis_size("dp")
    n_hid = lax.axis_size("hidden")
    cols = width // n_dp
    part = width // n_hid
    bf16 = jnp.bfloat16
    layer_input, grad_out, picks, gates, w_up, w_down = (
        pltpu.with_memory_space_constraint(x, pltpu.HBM)
        for x in (layer_input, grad_out, picks, gates, w_up, w_down)
    )

    send, spread = pl.pallas_call(
        functools.partial(pick_kernel, n_hid),
        out_shape=[
            jax.ShapeDtypeStruct((slots, 2 * width), bf16),
            jax.ShapeDtypeStruct((slots * n_hid, tok_dev), bf16),
        ],
        in_specs=[HBM] * 3,
        out_specs=[VMEM] * 2,
        scratch_shapes=[
            pltpu.VMEM(picks.shape, jnp.int32),
            pltpu.VMEM(layer_input.shape, bf16),
            pltpu.VMEM(grad_out.shape, bf16),
            pltpu.SemaphoreType.DMA((3,)),
        ],
        compiler_params=ROOM,
        name="pick",
    )(picks, layer_input, grad_out)

    rows = jnp.concatenate(
        [hop(send[s * n_pick : (s + 1) * n_pick], "expert", s) for s in range(n_exp)], axis=0
    )
    gate_held, upper, lower = pl.pallas_call(
        load_kernel,
        out_shape=[jax.ShapeDtypeStruct(x.shape, x.dtype) for x in (gates, w_up, w_down)],
        in_specs=[HBM] * 4,
        out_specs=[VMEM] * 3,
        scratch_shapes=[pltpu.SemaphoreType.DMA((3,))],
        cost_estimate=pl.CostEstimate(
            flops=0, bytes_accessed=4 * w_up.size + 4 * w_down.size, transcendentals=0
        ),
        compiler_params=ROOM,
        name="load",
    )(send, gates, w_up, w_down)
    share = slots // n_hid
    parts = pl.pallas_call(
        cut_kernel,
        out_shape=[jax.ShapeDtypeStruct((share, 2 * cols), bf16)] * (n_dp - 1),
        in_specs=[ANY, VMEM],
        out_specs=[VMEM] * (n_dp - 1),
        compiler_params=ROOM,
        name="cut",
    )(gate_held, rows)
    parts = [hop(parts[s], "dp", s + 1) for s in reversed(range(n_dp - 1))][::-1]

    factors = pl.pallas_call(
        factor_kernel,
        out_shape=jax.ShapeDtypeStruct((slots, 2 * units), bf16),
        in_specs=[ANY] + [VMEM] * 4,
        out_specs=VMEM,
        compiler_params=ROOM,
        cost_estimate=pl.CostEstimate(
            flops=4 * slots * w_up.size, bytes_accessed=4 * w_up.size, transcendentals=slots * units
        ),
        name="factor",
    )(parts[-1], gate_held, rows, upper, lower)
    parts = [jnp.stack([x[:, k * cols : (k + 1) * cols] for x in parts]) for k in range(2)]
    others = [hop(x, "hidden", t) for t in range(1, n_hid) for x in parts]

    gathered = jnp.concatenate([hop(factors, "dp", s) for s in range(n_dp)], axis=0)

    piece = pl.pallas_call(
        functools.partial(piece_kernel, n_hid),
        out_shape=jax.ShapeDtypeStruct((n_exp * n_hid, n_pick, part), bf16),
        in_specs=[VMEM, VMEM],
        out_specs=VMEM,
        compiler_params=ROOM,
        cost_estimate=pl.CostEstimate(
            flops=2 * slots * w_up.size, bytes_accessed=2 * w_up.size, transcendentals=0
        ),
        name="piece",
    )(factors, upper)
    piece = pl.pallas_call(
        tie_kernel,
        out_shape=jax.ShapeDtypeStruct(piece.shape, piece.dtype),
        in_specs=[ANY] * (2 * n_hid - 1),
        out_specs=ANY,
        input_output_aliases={0: 0},
        compiler_params=ROOM,
        name="tie",
    )(piece, *others)
    returned = lax.all_to_all(piece, ("expert", "hidden"), 0, 0)
    grad_rows = lax.dot_general(
        spread,
        returned.reshape(slots * n_hid, part),
        (((0,), (0,)), ((), ())),
        preferred_element_type=jnp.float32,
    ).astype(bf16)

    chunks = max(1, units // 256)
    grads = pl.pallas_call(
        functools.partial(weight_kernel, chunks, (n_dp, n_hid)),
        out_shape=[jax.ShapeDtypeStruct((1, cols, units), jnp.float32)] * 2,
        in_specs=[VMEM] * (2 * n_hid + 2),
        out_specs=[HBM] * 2,
        scratch_shapes=[
            pltpu.VMEM((n_dp * slots, 2 * cols), bf16),
            pltpu.VMEM((2, cols, units), jnp.float32),
            pltpu.SemaphoreType.DMA((2, chunks)),
        ],
        compiler_params=ROOM,
        cost_estimate=pl.CostEstimate(
            flops=4 * n_dp * slots * cols * units, bytes_accessed=64 * cols * units, transcendentals=0
        ),
        name="weight",
    )(rows, *parts, *others, gathered)
    return (grad_rows[None], *grads)


def solution(mesh):
    placed = (
        P("dp", "expert", None),
        P("dp", "expert", None),
        P("dp", "expert", None, None),
        P("dp", "expert", None, None),
        P("expert", None, "hidden"),
        P("expert", None, "hidden"),
    )
    return jax.shard_map(
        local,
        mesh=mesh,
        in_specs=placed,
        out_specs=(
            P("dp", "expert", "hidden"),
            P("expert", "dp", "hidden"),
            P("expert", "dp", "hidden"),
        ),
        check_vma=False,
    )
```

```python
import functools

import jax
import jax.numpy as jnp
from jax import lax
from jax.experimental import pallas as pl
from jax.experimental.pallas import tpu as pltpu
from jax.sharding import PartitionSpec as P

ROOT_TERM = 0.7978845608028654
CUBIC_TERM = 0.044715


def gelu_pair(pre):
    square = pre * pre
    inner = jnp.tanh(ROOT_TERM * (pre + CUBIC_TERM * square * pre))
    value = 0.5 * pre * (1.0 + inner)
    slope = 0.5 * (1.0 + inner) + 0.5 * pre * (1.0 - inner * inner) * ROOT_TERM * (
        1.0 + 3.0 * CUBIC_TERM * square
    )
    return value, slope


def hop(x, axis, step):
    n = lax.axis_size(axis)
    assert n & (n - 1) == 0
    return lax.ppermute(x, axis, [(i, i ^ step) for i in range(n)]) if step else x


def column(ref, order):
    n = ref.shape[-1]
    down = lax.broadcasted_iota(jnp.int32, (n, n), 0)
    along = lax.broadcasted_iota(jnp.int32, (n, n), 1)
    out = []
    for at in order:
        row = ref[0, 0, pl.ds(at, 1), :].astype(jnp.float32)
        out.append(jnp.sum(jnp.where(down == along, row, 0.0), axis=1, keepdims=True))
    return jnp.concatenate(out, axis=0)


def pick_kernel(n_hid, picks_hbm, tokens_hbm, upstream_hbm, rows_ref, spread_ref, *refs):
    picks_ref, tokens_ref, upstream_ref, sems = refs
    n_exp = picks_ref.shape[2]
    tok_dev, width = tokens_ref.shape[1:]
    copies = [
        pltpu.make_async_copy(picks_hbm, picks_ref, sems.at[0]),
        pltpu.make_async_copy(tokens_hbm, tokens_ref, sems.at[1]),
        pltpu.make_async_copy(upstream_hbm, upstream_ref, sems.at[2]),
    ]
    for copy in copies:
        copy.start()
    me = lax.axis_index("expert")
    copies[0].wait()

    def one_hot(order):
        wanted = column(picks_ref, order).astype(jnp.int32)
        spots = lax.broadcasted_iota(jnp.int32, (wanted.shape[0], tok_dev), 1)
        return jnp.where(wanted == spots, 1.0, 0.0).astype(jnp.bfloat16)

    selector = one_hot([me ^ s for s in range(n_exp)])
    spread_ref[...] = one_hot([e for e in range(n_exp) for _ in range(n_hid)])
    for at, copy, source in ((0, copies[1], tokens_ref), (width, copies[2], upstream_ref)):
        copy.wait()
        rows_ref[:, at : at + width] = jnp.dot(
            selector, source[0], preferred_element_type=jnp.float32
        ).astype(jnp.bfloat16)


def cut_kernel(after_ref, rows_ref, *out_refs):
    n_dp = len(out_refs) + 1
    share, wide = out_refs[0].shape
    cols = wide // 2
    width = rows_ref.shape[1] // 2
    my_dp = lax.axis_index("dp")
    spot = pl.ds(pl.multiple_of(lax.axis_index("hidden") * share, 16), share)
    for s, out_ref in enumerate(out_refs):
        at = (my_dp ^ (s + 1)) * cols
        for half in range(2):
            out_ref[:, half * cols : (half + 1) * cols] = rows_ref[
                spot, pl.ds(pl.multiple_of(half * width + at, 128), cols)
            ]


def load_kernel(after_ref, gates_hbm, upper_hbm, lower_hbm, gates_ref, upper_ref, lower_ref, sems):
    copies = [
        pltpu.make_async_copy(source, target, sems.at[k])
        for k, (source, target) in enumerate(
            ((gates_hbm, gates_ref), (upper_hbm, upper_ref), (lower_hbm, lower_ref))
        )
    ]
    for copy in copies:
        copy.start()
    for copy in copies:
        copy.wait()


def factor_kernel(after_ref, gates_ref, rows_ref, upper_ref, lower_ref, out_ref):
    n_exp = gates_ref.shape[2]
    width, units = upper_ref.shape[1:]
    me = lax.axis_index("expert")
    gate = column(gates_ref, [me ^ s for s in range(n_exp)])
    pre = jnp.dot(rows_ref[:, :width], upper_ref[0], preferred_element_type=jnp.float32)
    back = jnp.dot(rows_ref[:, width:], lower_ref[0], preferred_element_type=jnp.float32)
    value, slope = gelu_pair(pre)
    out_ref[:, :units] = (back * gate * slope).astype(jnp.bfloat16)
    out_ref[:, units:] = (value * gate).astype(jnp.bfloat16)


def piece_kernel(n_hid, factor_ref, upper_ref, out_ref):
    n_pick, part = out_ref.shape[1:]
    width, units = upper_ref.shape[1:]
    n_exp = out_ref.shape[0] // n_hid
    me = lax.axis_index("expert")
    piece = lax.dot_general(
        factor_ref[:, :units], upper_ref[0], (((1,), (1,)), ((), ())), preferred_element_type=jnp.float32
    )
    for s in range(n_exp):
        owner = (me ^ s) * n_hid
        for h in range(n_hid):
            out_ref[owner + h] = piece[
                s * n_pick : (s + 1) * n_pick, h * part : (h + 1) * part
            ].astype(jnp.bfloat16)


def stack_kernel(after_ref, *refs):
    *part_refs, out_ref = refs
    for s, part in enumerate(part_refs):
        out_ref[s] = part[...]


def tie_kernel(*refs):
    pass


def weight_kernel(chunks, shape, own_ref, *refs):
    n_dp, n_hid = shape
    part_refs, refs = refs[:n_hid], refs[n_hid:]
    factor_ref, up_ref, down_ref, side_ref, held, sems = refs
    units = factor_ref.shape[1] // 2
    cols = side_ref.shape[1] // 2
    width = own_ref.shape[1] // 2
    slots = own_ref.shape[0]
    rows = slots // n_hid
    my_hid = lax.axis_index("hidden")
    start = lax.axis_index("dp") * cols
    for half in range(2):
        side_ref[:slots, half * cols : (half + 1) * cols] = own_ref[
            :, pl.ds(pl.multiple_of(half * width + start, 128), cols)
        ]
    for t, part in enumerate(part_refs):
        spot = (my_hid ^ t) * rows
        for s in range(1, n_dp):
            side_ref[pl.ds(pl.multiple_of(s * slots + spot, 16), rows), :] = part[s - 1]
    step = cols // chunks
    copies = []
    for which, out in ((0, up_ref), (1, down_ref)):
        for c in range(chunks):
            spot = pl.ds(c * step, step)
            held[which, spot, :] = lax.dot_general(
                side_ref[:, pl.ds(which * cols + c * step, step)],
                factor_ref[:, which * units : (which + 1) * units],
                (((0,), (0,)), ((), ())),
                preferred_element_type=jnp.float32,
            )
            copy = pltpu.make_async_copy(
                held.at[which, spot, :], out.at[0, spot, :], sems.at[which, c]
            )
            copy.start()
            copies.append(copy)
    for copy in copies:
        copy.wait()


def return_kernel(spread_ref, came_ref, out_ref):
    came = jnp.concatenate([came_ref[k].astype(jnp.float32) for k in range(came_ref.shape[0])], axis=0)
    out_ref[0] = lax.dot_general(
        spread_ref[...],
        came.astype(jnp.bfloat16),
        (((0,), (0,)), ((), ())),
        preferred_element_type=jnp.float32,
    ).astype(jnp.bfloat16)


VMEM = pl.BlockSpec(memory_space=pltpu.VMEM)
ANY = pl.BlockSpec(memory_space=pl.ANY)
HBM = pl.BlockSpec(memory_space=pltpu.HBM)
ROOM = pltpu.CompilerParams(vmem_limit_bytes=16 << 20)


def local(layer_input, grad_out, picks, gates, w_up, w_down):
    tok_dev, width = layer_input.shape[1:]
    n_exp, n_pick = picks.shape[2:]
    slots = n_exp * n_pick
    units = w_up.shape[2]
    n_dp = lax.axis_size("dp")
    n_hid = lax.axis_size("hidden")
    cols = width // n_dp
    part = width // n_hid
    bf16 = jnp.bfloat16
    layer_input, grad_out, picks, gates, w_up, w_down = (
        pltpu.with_memory_space_constraint(x, pltpu.HBM)
        for x in (layer_input, grad_out, picks, gates, w_up, w_down)
    )

    send, spread = pl.pallas_call(
        functools.partial(pick_kernel, n_hid),
        out_shape=[
            jax.ShapeDtypeStruct((slots, 2 * width), bf16),
            jax.ShapeDtypeStruct((slots * n_hid, tok_dev), bf16),
        ],
        in_specs=[HBM] * 3,
        out_specs=[VMEM] * 2,
        scratch_shapes=[
            pltpu.VMEM(picks.shape, jnp.int32),
            pltpu.VMEM(layer_input.shape, bf16),
            pltpu.VMEM(grad_out.shape, bf16),
            pltpu.SemaphoreType.DMA((3,)),
        ],
        compiler_params=ROOM,
        name="pick",
    )(picks, layer_input, grad_out)

    rows = jnp.concatenate(
        [hop(send[s * n_pick : (s + 1) * n_pick], "expert", s) for s in range(n_exp)], axis=0
    )
    gate_held, upper, lower = pl.pallas_call(
        load_kernel,
        out_shape=[jax.ShapeDtypeStruct(x.shape, x.dtype) for x in (gates, w_up, w_down)],
        in_specs=[HBM] * 4,
        out_specs=[VMEM] * 3,
        scratch_shapes=[pltpu.SemaphoreType.DMA((3,))],
        cost_estimate=pl.CostEstimate(
            flops=0, bytes_accessed=4 * w_up.size + 4 * w_down.size, transcendentals=0
        ),
        compiler_params=ROOM,
        name="load",
    )(send, gates, w_up, w_down)
    share = slots // n_hid
    parts = pl.pallas_call(
        cut_kernel,
        out_shape=[jax.ShapeDtypeStruct((share, 2 * cols), bf16)] * (n_dp - 1),
        in_specs=[ANY, VMEM],
        out_specs=[VMEM] * (n_dp - 1),
        compiler_params=ROOM,
        name="cut",
    )(gate_held, rows)
    parts = [hop(parts[s], "dp", s + 1) for s in reversed(range(n_dp - 1))][::-1]

    factors = pl.pallas_call(
        factor_kernel,
        out_shape=jax.ShapeDtypeStruct((slots, 2 * units), bf16),
        in_specs=[ANY] + [VMEM] * 4,
        out_specs=VMEM,
        compiler_params=ROOM,
        cost_estimate=pl.CostEstimate(
            flops=4 * slots * w_up.size, bytes_accessed=4 * w_up.size, transcendentals=slots * units
        ),
        name="factor",
    )(parts[-1], gate_held, rows, upper, lower)
    parts = pl.pallas_call(
        stack_kernel,
        out_shape=jax.ShapeDtypeStruct((n_dp - 1, share, 2 * cols), bf16),
        in_specs=[ANY] + [VMEM] * (n_dp - 1),
        out_specs=VMEM,
        compiler_params=ROOM,
        name="stack",
    )(factors, *parts)
    parts = [hop(parts, "hidden", t) for t in range(n_hid)]

    gathered = jnp.concatenate([hop(factors, "dp", s) for s in range(n_dp)], axis=0)

    piece = pl.pallas_call(
        functools.partial(piece_kernel, n_hid),
        out_shape=jax.ShapeDtypeStruct((n_exp * n_hid, n_pick, part), bf16),
        in_specs=[VMEM, VMEM],
        out_specs=VMEM,
        compiler_params=ROOM,
        cost_estimate=pl.CostEstimate(
            flops=2 * slots * w_up.size, bytes_accessed=2 * w_up.size, transcendentals=0
        ),
        name="piece",
    )(factors, upper)
    piece = pl.pallas_call(
        tie_kernel,
        out_shape=jax.ShapeDtypeStruct(piece.shape, piece.dtype),
        in_specs=[ANY] * n_hid,
        out_specs=ANY,
        input_output_aliases={0: 0},
        compiler_params=ROOM,
        name="tie",
    )(piece, *parts[1:])
    returned = lax.all_to_all(piece, ("expert", "hidden"), 0, 0)
    grad_in = pl.pallas_call(
        return_kernel,
        out_shape=jax.ShapeDtypeStruct((1, tok_dev, part), bf16),
        in_specs=[VMEM] * 2,
        out_specs=VMEM,
        compiler_params=ROOM,
        name="return",
    )(spread, returned)

    chunks = cols // 128
    grads = pl.pallas_call(
        functools.partial(weight_kernel, chunks, (n_dp, n_hid)),
        out_shape=[jax.ShapeDtypeStruct((1, cols, units), jnp.float32)] * 2,
        in_specs=[VMEM] * (n_hid + 2),
        out_specs=[HBM] * 2,
        scratch_shapes=[
            pltpu.VMEM((n_dp * slots, 2 * cols), bf16),
            pltpu.VMEM((2, cols, units), jnp.float32),
            pltpu.SemaphoreType.DMA((2, chunks)),
        ],
        compiler_params=ROOM,
        cost_estimate=pl.CostEstimate(
            flops=4 * n_dp * slots * cols * units, bytes_accessed=64 * cols * units, transcendentals=0
        ),
        name="weight",
    )(rows, *parts, gathered)
    return (grad_in, *grads)


def solution(mesh):
    placed = (
        P("dp", "expert", None),
        P("dp", "expert", None),
        P("dp", "expert", None, None),
        P("dp", "expert", None, None),
        P("expert", None, "hidden"),
        P("expert", None, "hidden"),
    )
    return jax.shard_map(
        local,
        mesh=mesh,
        in_specs=placed,
        out_specs=(
            P("dp", "expert", "hidden"),
            P("expert", "dp", "hidden"),
            P("expert", "dp", "hidden"),
        ),
        check_vma=False,
    )
```

```python
import functools

import jax
import jax.numpy as jnp
from jax import lax
from jax.experimental import pallas as pl
from jax.experimental.pallas import tpu as pltpu
from jax.sharding import PartitionSpec as P

ROOT_TERM = 0.7978845608028654
CUBIC_TERM = 0.044715


def gelu_pair(pre):
    square = pre * pre
    inner = jnp.tanh(ROOT_TERM * (pre + CUBIC_TERM * square * pre))
    value = 0.5 * pre * (1.0 + inner)
    slope = 0.5 * (1.0 + inner) + 0.5 * pre * (1.0 - inner * inner) * ROOT_TERM * (
        1.0 + 3.0 * CUBIC_TERM * square
    )
    return value, slope


def hop(x, axis, step):
    n = lax.axis_size(axis)
    assert n & (n - 1) == 0
    return lax.ppermute(x, axis, [(i, i ^ step) for i in range(n)]) if step else x


def column(ref, order):
    n = ref.shape[-1]
    down = lax.broadcasted_iota(jnp.int32, (n, n), 0)
    along = lax.broadcasted_iota(jnp.int32, (n, n), 1)
    out = []
    for at in order:
        row = ref[0, 0, pl.ds(at, 1), :].astype(jnp.float32)
        out.append(jnp.sum(jnp.where(down == along, row, 0.0), axis=1, keepdims=True))
    return jnp.concatenate(out, axis=0)


def pick_kernel(n_hid, picks_hbm, tokens_hbm, upstream_hbm, rows_ref, spread_ref, *refs):
    picks_ref, tokens_ref, upstream_ref, sems = refs
    n_exp = picks_ref.shape[2]
    tok_dev, width = tokens_ref.shape[1:]
    copies = [
        pltpu.make_async_copy(picks_hbm, picks_ref, sems.at[0]),
        pltpu.make_async_copy(tokens_hbm, tokens_ref, sems.at[1]),
        pltpu.make_async_copy(upstream_hbm, upstream_ref, sems.at[2]),
    ]
    for copy in copies:
        copy.start()
    me = lax.axis_index("expert")
    copies[0].wait()

    def one_hot(order):
        wanted = column(picks_ref, order).astype(jnp.int32)
        spots = lax.broadcasted_iota(jnp.int32, (wanted.shape[0], tok_dev), 1)
        return jnp.where(wanted == spots, 1.0, 0.0).astype(jnp.bfloat16)

    selector = one_hot([me ^ s for s in range(n_exp)])
    spread_ref[...] = one_hot([e for e in range(n_exp) for _ in range(n_hid)])
    for at, copy, source in ((0, copies[1], tokens_ref), (width, copies[2], upstream_ref)):
        copy.wait()
        rows_ref[:, at : at + width] = jnp.dot(
            selector, source[0], preferred_element_type=jnp.float32
        ).astype(jnp.bfloat16)


def cut_kernel(after_ref, rows_ref, *out_refs):
    n_dp = len(out_refs) + 1
    share, wide = out_refs[0].shape
    cols = wide // 2
    width = rows_ref.shape[1] // 2
    my_dp = lax.axis_index("dp")
    spot = pl.ds(pl.multiple_of(lax.axis_index("hidden") * share, 16), share)
    for s, out_ref in enumerate(out_refs):
        at = (my_dp ^ (s + 1)) * cols
        for half in range(2):
            out_ref[:, half * cols : (half + 1) * cols] = rows_ref[
                spot, pl.ds(pl.multiple_of(half * width + at, 128), cols)
            ]


def load_kernel(after_ref, gates_hbm, upper_hbm, lower_hbm, gates_ref, upper_ref, lower_ref, sems):
    copies = [
        pltpu.make_async_copy(source, target, sems.at[k])
        for k, (source, target) in enumerate(
            ((gates_hbm, gates_ref), (upper_hbm, upper_ref), (lower_hbm, lower_ref))
        )
    ]
    for copy in copies:
        copy.start()
    for copy in copies:
        copy.wait()


def factor_kernel(gates_ref, rows_ref, upper_ref, lower_ref, out_ref):
    n_exp = gates_ref.shape[2]
    width, units = upper_ref.shape[1:]
    me = lax.axis_index("expert")
    gate = column(gates_ref, [me ^ s for s in range(n_exp)])
    pre = jnp.dot(rows_ref[:, :width], upper_ref[0], preferred_element_type=jnp.float32)
    back = jnp.dot(rows_ref[:, width:], lower_ref[0], preferred_element_type=jnp.float32)
    value, slope = gelu_pair(pre)
    out_ref[:, :units] = (back * gate * slope).astype(jnp.bfloat16)
    out_ref[:, units:] = (value * gate).astype(jnp.bfloat16)


def piece_kernel(n_hid, factor_ref, upper_ref, out_ref):
    n_pick, part = out_ref.shape[1:]
    width, units = upper_ref.shape[1:]
    n_exp = out_ref.shape[0] // n_hid
    me = lax.axis_index("expert")
    piece = lax.dot_general(
        factor_ref[:, :units], upper_ref[0], (((1,), (1,)), ((), ())), preferred_element_type=jnp.float32
    )
    for s in range(n_exp):
        owner = (me ^ s) * n_hid
        for h in range(n_hid):
            out_ref[owner + h] = piece[
                s * n_pick : (s + 1) * n_pick, h * part : (h + 1) * part
            ].astype(jnp.bfloat16)


def stack_kernel(after_ref, *refs):
    *part_refs, out_ref = refs
    for s, part in enumerate(part_refs):
        out_ref[s] = part[...]


def tie_kernel(*refs):
    pass


def weight_kernel(chunks, shape, own_ref, *refs):
    n_dp, n_hid = shape
    part_refs, refs = refs[:n_hid], refs[n_hid:]
    factor_ref, up_ref, down_ref, side_ref, held, sems = refs
    units = factor_ref.shape[1] // 2
    cols = side_ref.shape[1] // 2
    width = own_ref.shape[1] // 2
    slots = own_ref.shape[0]
    rows = slots // n_hid
    my_hid = lax.axis_index("hidden")
    start = lax.axis_index("dp") * cols
    for half in range(2):
        side_ref[:slots, half * cols : (half + 1) * cols] = own_ref[
            :, pl.ds(pl.multiple_of(half * width + start, 128), cols)
        ]
    for t, part in enumerate(part_refs):
        spot = (my_hid ^ t) * rows
        for s in range(1, n_dp):
            side_ref[pl.ds(pl.multiple_of(s * slots + spot, 16), rows), :] = part[s - 1]
    step = cols // chunks
    copies = []
    for which, out in ((0, up_ref), (1, down_ref)):
        for c in range(chunks):
            spot = pl.ds(c * step, step)
            held[which, spot, :] = lax.dot_general(
                side_ref[:, pl.ds(which * cols + c * step, step)],
                factor_ref[:, which * units : (which + 1) * units],
                (((0,), (0,)), ((), ())),
                preferred_element_type=jnp.float32,
            )
            copy = pltpu.make_async_copy(
                held.at[which, spot, :], out.at[0, spot, :], sems.at[which, c]
            )
            copy.start()
            copies.append(copy)
    for copy in copies:
        copy.wait()


def return_kernel(spread_ref, came_ref, out_ref):
    came = jnp.concatenate([came_ref[k].astype(jnp.float32) for k in range(came_ref.shape[0])], axis=0)
    out_ref[0] = lax.dot_general(
        spread_ref[...],
        came.astype(jnp.bfloat16),
        (((0,), (0,)), ((), ())),
        preferred_element_type=jnp.float32,
    ).astype(jnp.bfloat16)


VMEM = pl.BlockSpec(memory_space=pltpu.VMEM)
ANY = pl.BlockSpec(memory_space=pl.ANY)
HBM = pl.BlockSpec(memory_space=pltpu.HBM)
ROOM = pltpu.CompilerParams(vmem_limit_bytes=16 << 20)


def local(layer_input, grad_out, picks, gates, w_up, w_down):
    tok_dev, width = layer_input.shape[1:]
    n_exp, n_pick = picks.shape[2:]
    slots = n_exp * n_pick
    units = w_up.shape[2]
    n_dp = lax.axis_size("dp")
    n_hid = lax.axis_size("hidden")
    cols = width // n_dp
    part = width // n_hid
    bf16 = jnp.bfloat16
    layer_input, grad_out, picks, gates, w_up, w_down = (
        pltpu.with_memory_space_constraint(x, pltpu.HBM)
        for x in (layer_input, grad_out, picks, gates, w_up, w_down)
    )

    send, spread = pl.pallas_call(
        functools.partial(pick_kernel, n_hid),
        out_shape=[
            jax.ShapeDtypeStruct((slots, 2 * width), bf16),
            jax.ShapeDtypeStruct((slots * n_hid, tok_dev), bf16),
        ],
        in_specs=[HBM] * 3,
        out_specs=[VMEM] * 2,
        scratch_shapes=[
            pltpu.VMEM(picks.shape, jnp.int32),
            pltpu.VMEM(layer_input.shape, bf16),
            pltpu.VMEM(grad_out.shape, bf16),
            pltpu.SemaphoreType.DMA((3,)),
        ],
        compiler_params=ROOM,
        name="pick",
    )(picks, layer_input, grad_out)

    rows = jnp.concatenate(
        [hop(send[s * n_pick : (s + 1) * n_pick], "expert", s) for s in range(n_exp)], axis=0
    )
    gate_held, upper, lower = pl.pallas_call(
        load_kernel,
        out_shape=[jax.ShapeDtypeStruct(x.shape, x.dtype) for x in (gates, w_up, w_down)],
        in_specs=[HBM] * 4,
        out_specs=[VMEM] * 3,
        scratch_shapes=[pltpu.SemaphoreType.DMA((3,))],
        cost_estimate=pl.CostEstimate(
            flops=0, bytes_accessed=4 * w_up.size + 4 * w_down.size, transcendentals=0
        ),
        compiler_params=ROOM,
        name="load",
    )(send, gates, w_up, w_down)
    share = slots // n_hid
    parts = pl.pallas_call(
        cut_kernel,
        out_shape=[jax.ShapeDtypeStruct((share, 2 * cols), bf16)] * (n_dp - 1),
        in_specs=[ANY, VMEM],
        out_specs=[VMEM] * (n_dp - 1),
        compiler_params=ROOM,
        name="cut",
    )(gate_held, rows)
    parts = [hop(parts[s], "dp", s + 1) for s in reversed(range(n_dp - 1))][::-1]

    factors = pl.pallas_call(
        factor_kernel,
        out_shape=jax.ShapeDtypeStruct((slots, 2 * units), bf16),
        in_specs=[VMEM] * 4,
        out_specs=VMEM,
        compiler_params=ROOM,
        cost_estimate=pl.CostEstimate(
            flops=4 * slots * w_up.size, bytes_accessed=4 * w_up.size, transcendentals=slots * units
        ),
        name="factor",
    )(gate_held, rows, upper, lower)
    parts = pl.pallas_call(
        stack_kernel,
        out_shape=jax.ShapeDtypeStruct((n_dp - 1, share, 2 * cols), bf16),
        in_specs=[ANY] + [VMEM] * (n_dp - 1),
        out_specs=VMEM,
        compiler_params=ROOM,
        name="stack",
    )(factors, *parts)
    parts = [hop(parts, "hidden", t) for t in range(n_hid)]

    gathered = jnp.concatenate([hop(factors, "dp", s) for s in range(n_dp)], axis=0)

    piece = pl.pallas_call(
        functools.partial(piece_kernel, n_hid),
        out_shape=jax.ShapeDtypeStruct((n_exp * n_hid, n_pick, part), bf16),
        in_specs=[VMEM, VMEM],
        out_specs=VMEM,
        compiler_params=ROOM,
        cost_estimate=pl.CostEstimate(
            flops=2 * slots * w_up.size, bytes_accessed=2 * w_up.size, transcendentals=0
        ),
        name="piece",
    )(factors, upper)
    piece = pl.pallas_call(
        tie_kernel,
        out_shape=jax.ShapeDtypeStruct(piece.shape, piece.dtype),
        in_specs=[ANY] * n_hid,
        out_specs=ANY,
        input_output_aliases={0: 0},
        compiler_params=ROOM,
        name="tie",
    )(piece, *parts[1:])
    returned = lax.all_to_all(piece, ("expert", "hidden"), 0, 0)
    grad_in = pl.pallas_call(
        return_kernel,
        out_shape=jax.ShapeDtypeStruct((1, tok_dev, part), bf16),
        in_specs=[VMEM] * 2,
        out_specs=VMEM,
        compiler_params=ROOM,
        name="return",
    )(spread, returned)

    chunks = cols // 128
    grads = pl.pallas_call(
        functools.partial(weight_kernel, chunks, (n_dp, n_hid)),
        out_shape=[jax.ShapeDtypeStruct((1, cols, units), jnp.float32)] * 2,
        in_specs=[VMEM] * (n_hid + 2),
        out_specs=[HBM] * 2,
        scratch_shapes=[
            pltpu.VMEM((n_dp * slots, 2 * cols), bf16),
            pltpu.VMEM((2, cols, units), jnp.float32),
            pltpu.SemaphoreType.DMA((2, chunks)),
        ],
        compiler_params=ROOM,
        cost_estimate=pl.CostEstimate(
            flops=4 * n_dp * slots * cols * units, bytes_accessed=64 * cols * units, transcendentals=0
        ),
        name="weight",
    )(rows, *parts, gathered)
    return (grad_in, *grads)


def solution(mesh):
    placed = (
        P("dp", "expert", None),
        P("dp", "expert", None),
        P("dp", "expert", None, None),
        P("dp", "expert", None, None),
        P("expert", None, "hidden"),
        P("expert", None, "hidden"),
    )
    return jax.shard_map(
        local,
        mesh=mesh,
        in_specs=placed,
        out_specs=(
            P("dp", "expert", "hidden"),
            P("expert", "dp", "hidden"),
            P("expert", "dp", "hidden"),
        ),
        check_vma=False,
    )
```

```python
import functools

import jax
import jax.numpy as jnp
from jax import lax
from jax.experimental import pallas as pl
from jax.experimental.pallas import tpu as pltpu
from jax.sharding import PartitionSpec as P

ROOT_TERM = 0.7978845608028654
CUBIC_TERM = 0.044715


def gelu_pair(pre):
    square = pre * pre
    inner = jnp.tanh(ROOT_TERM * (pre + CUBIC_TERM * square * pre))
    value = 0.5 * pre * (1.0 + inner)
    slope = 0.5 * (1.0 + inner) + 0.5 * pre * (1.0 - inner * inner) * ROOT_TERM * (
        1.0 + 3.0 * CUBIC_TERM * square
    )
    return value, slope


def hop(x, axis, step):
    n = lax.axis_size(axis)
    assert n & (n - 1) == 0
    return lax.ppermute(x, axis, [(i, i ^ step) for i in range(n)]) if step else x


def column(ref, order):
    n = ref.shape[-1]
    down = lax.broadcasted_iota(jnp.int32, (n, n), 0)
    along = lax.broadcasted_iota(jnp.int32, (n, n), 1)
    out = []
    for at in order:
        row = ref[0, 0, pl.ds(at, 1), :].astype(jnp.float32)
        out.append(jnp.sum(jnp.where(down == along, row, 0.0), axis=1, keepdims=True))
    return jnp.concatenate(out, axis=0)


def pick_kernel(n_hid, picks_hbm, tokens_hbm, upstream_hbm, rows_ref, spread_ref, *refs):
    picks_ref, tokens_ref, upstream_ref, sems = refs
    n_exp = picks_ref.shape[2]
    tok_dev, width = tokens_ref.shape[1:]
    copies = [
        pltpu.make_async_copy(picks_hbm, picks_ref, sems.at[0]),
        pltpu.make_async_copy(tokens_hbm, tokens_ref, sems.at[1]),
        pltpu.make_async_copy(upstream_hbm, upstream_ref, sems.at[2]),
    ]
    for copy in copies:
        copy.start()
    me = lax.axis_index("expert")
    copies[0].wait()

    def one_hot(order):
        wanted = column(picks_ref, order).astype(jnp.int32)
        spots = lax.broadcasted_iota(jnp.int32, (wanted.shape[0], tok_dev), 1)
        return jnp.where(wanted == spots, 1.0, 0.0).astype(jnp.bfloat16)

    selector = one_hot([me ^ s for s in range(n_exp)])
    spread_ref[...] = one_hot([e for e in range(n_exp) for _ in range(n_hid)])
    for at, copy, source in ((0, copies[1], tokens_ref), (width, copies[2], upstream_ref)):
        copy.wait()
        rows_ref[:, at : at + width] = jnp.dot(
            selector, source[0], preferred_element_type=jnp.float32
        ).astype(jnp.bfloat16)


def cut_kernel(after_ref, rows_ref, *out_refs):
    n_dp = len(out_refs) + 1
    share, wide = out_refs[0].shape
    cols = wide // 2
    width = rows_ref.shape[1] // 2
    my_dp = lax.axis_index("dp")
    spot = pl.ds(pl.multiple_of(lax.axis_index("hidden") * share, 16), share)
    for s, out_ref in enumerate(out_refs):
        at = (my_dp ^ (s + 1)) * cols
        for half in range(2):
            out_ref[:, half * cols : (half + 1) * cols] = rows_ref[
                spot, pl.ds(pl.multiple_of(half * width + at, 128), cols)
            ]


def load_kernel(after_ref, gates_hbm, upper_hbm, lower_hbm, gates_ref, upper_ref, lower_ref, sems):
    copies = [
        pltpu.make_async_copy(source, target, sems.at[k])
        for k, (source, target) in enumerate(
            ((gates_hbm, gates_ref), (upper_hbm, upper_ref), (lower_hbm, lower_ref))
        )
    ]
    for copy in copies:
        copy.start()
    for copy in copies:
        copy.wait()


def factor_kernel(gates_ref, rows_ref, upper_ref, lower_ref, out_ref):
    n_exp = gates_ref.shape[2]
    width, units = upper_ref.shape[1:]
    me = lax.axis_index("expert")
    gate = column(gates_ref, [me ^ s for s in range(n_exp)])
    pre = jnp.dot(rows_ref[:, :width], upper_ref[0], preferred_element_type=jnp.float32)
    back = jnp.dot(rows_ref[:, width:], lower_ref[0], preferred_element_type=jnp.float32)
    value, slope = gelu_pair(pre)
    out_ref[:, :units] = (back * gate * slope).astype(jnp.bfloat16)
    out_ref[:, units:] = (value * gate).astype(jnp.bfloat16)


def piece_kernel(n_hid, factor_ref, upper_ref, out_ref):
    n_pick, part = out_ref.shape[1:]
    width, units = upper_ref.shape[1:]
    n_exp = out_ref.shape[0] // n_hid
    me = lax.axis_index("expert")
    piece = lax.dot_general(
        factor_ref[:, :units], upper_ref[0], (((1,), (1,)), ((), ())), preferred_element_type=jnp.float32
    )
    for s in range(n_exp):
        owner = (me ^ s) * n_hid
        for h in range(n_hid):
            out_ref[owner + h] = piece[
                s * n_pick : (s + 1) * n_pick, h * part : (h + 1) * part
            ].astype(jnp.bfloat16)


def stack_kernel(after_ref, *refs):
    *part_refs, out_ref = refs
    for s, part in enumerate(part_refs):
        out_ref[len(part_refs) - 1 - s] = part[...]


def tie_kernel(*refs):
    pass


def weight_kernel(chunks, shape, own_ref, *refs):
    n_dp, n_hid = shape
    part_refs, refs = refs[:n_hid], refs[n_hid:]
    factor_ref, up_ref, down_ref, side_ref, held, sems = refs
    units = factor_ref.shape[1] // 2
    cols = side_ref.shape[1] // 2
    width = own_ref.shape[1] // 2
    slots = own_ref.shape[0]
    rows = slots // n_hid
    my_hid = lax.axis_index("hidden")
    start = lax.axis_index("dp") * cols
    for half in range(2):
        side_ref[:slots, half * cols : (half + 1) * cols] = own_ref[
            :, pl.ds(pl.multiple_of(half * width + start, 128), cols)
        ]
    for t, part in enumerate(part_refs):
        spot = (my_hid ^ t) * rows
        for s in range(1, n_dp):
            side_ref[pl.ds(pl.multiple_of(s * slots + spot, 16), rows), :] = part[s - 1]
    step = cols // chunks
    copies = []
    for which, out in ((0, up_ref), (1, down_ref)):
        for c in range(chunks):
            spot = pl.ds(c * step, step)
            held[which, spot, :] = lax.dot_general(
                side_ref[:, pl.ds(which * cols + c * step, step)],
                factor_ref[:, which * units : (which + 1) * units],
                (((0,), (0,)), ((), ())),
                preferred_element_type=jnp.float32,
            )
            copy = pltpu.make_async_copy(
                held.at[which, spot, :], out.at[0, spot, :], sems.at[which, c]
            )
            copy.start()
            copies.append(copy)
    for copy in copies:
        copy.wait()


def return_kernel(spread_ref, came_ref, out_ref):
    came = jnp.concatenate([came_ref[k].astype(jnp.float32) for k in range(came_ref.shape[0])], axis=0)
    out_ref[0] = lax.dot_general(
        spread_ref[...],
        came.astype(jnp.bfloat16),
        (((0,), (0,)), ((), ())),
        preferred_element_type=jnp.float32,
    ).astype(jnp.bfloat16)


VMEM = pl.BlockSpec(memory_space=pltpu.VMEM)
ANY = pl.BlockSpec(memory_space=pl.ANY)
HBM = pl.BlockSpec(memory_space=pltpu.HBM)
ROOM = pltpu.CompilerParams(vmem_limit_bytes=16 << 20)


def local(layer_input, grad_out, picks, gates, w_up, w_down):
    tok_dev, width = layer_input.shape[1:]
    n_exp, n_pick = picks.shape[2:]
    slots = n_exp * n_pick
    units = w_up.shape[2]
    n_dp = lax.axis_size("dp")
    n_hid = lax.axis_size("hidden")
    cols = width // n_dp
    part = width // n_hid
    bf16 = jnp.bfloat16
    layer_input, grad_out, picks, gates, w_up, w_down = (
        pltpu.with_memory_space_constraint(x, pltpu.HBM)
        for x in (layer_input, grad_out, picks, gates, w_up, w_down)
    )

    send, spread = pl.pallas_call(
        functools.partial(pick_kernel, n_hid),
        out_shape=[
            jax.ShapeDtypeStruct((slots, 2 * width), bf16),
            jax.ShapeDtypeStruct((slots * n_hid, tok_dev), bf16),
        ],
        in_specs=[HBM] * 3,
        out_specs=[VMEM] * 2,
        scratch_shapes=[
            pltpu.VMEM(picks.shape, jnp.int32),
            pltpu.VMEM(layer_input.shape, bf16),
            pltpu.VMEM(grad_out.shape, bf16),
            pltpu.SemaphoreType.DMA((3,)),
        ],
        compiler_params=ROOM,
        name="pick",
    )(picks, layer_input, grad_out)

    rows = jnp.concatenate(
        [hop(send[s * n_pick : (s + 1) * n_pick], "expert", s) for s in range(n_exp)], axis=0
    )
    gate_held, upper, lower = pl.pallas_call(
        load_kernel,
        out_shape=[jax.ShapeDtypeStruct(x.shape, x.dtype) for x in (gates, w_up, w_down)],
        in_specs=[HBM] * 4,
        out_specs=[VMEM] * 3,
        scratch_shapes=[pltpu.SemaphoreType.DMA((3,))],
        cost_estimate=pl.CostEstimate(
            flops=0, bytes_accessed=4 * w_up.size + 4 * w_down.size, transcendentals=0
        ),
        compiler_params=ROOM,
        name="load",
    )(send, gates, w_up, w_down)
    share = slots // n_hid
    parts = pl.pallas_call(
        cut_kernel,
        out_shape=[jax.ShapeDtypeStruct((share, 2 * cols), bf16)] * (n_dp - 1),
        in_specs=[ANY, VMEM],
        out_specs=[VMEM] * (n_dp - 1),
        compiler_params=ROOM,
        name="cut",
    )(gate_held, rows)
    parts = [hop(parts[s], "dp", s + 1) for s in reversed(range(n_dp - 1))][::-1]

    factors = pl.pallas_call(
        factor_kernel,
        out_shape=jax.ShapeDtypeStruct((slots, 2 * units), bf16),
        in_specs=[VMEM] * 4,
        out_specs=VMEM,
        compiler_params=ROOM,
        cost_estimate=pl.CostEstimate(
            flops=4 * slots * w_up.size, bytes_accessed=4 * w_up.size, transcendentals=slots * units
        ),
        name="factor",
    )(gate_held, rows, upper, lower)
    parts = pl.pallas_call(
        stack_kernel,
        out_shape=jax.ShapeDtypeStruct((n_dp - 1, share, 2 * cols), bf16),
        in_specs=[ANY] + [VMEM] * (n_dp - 1),
        out_specs=VMEM,
        compiler_params=ROOM,
        name="stack",
    )(factors, *parts[::-1])
    parts = [hop(parts, "hidden", t) for t in range(n_hid)]

    gathered = jnp.concatenate([hop(factors, "dp", s) for s in range(n_dp)], axis=0)

    piece = pl.pallas_call(
        functools.partial(piece_kernel, n_hid),
        out_shape=jax.ShapeDtypeStruct((n_exp * n_hid, n_pick, part), bf16),
        in_specs=[VMEM, VMEM],
        out_specs=VMEM,
        compiler_params=ROOM,
        cost_estimate=pl.CostEstimate(
            flops=2 * slots * w_up.size, bytes_accessed=2 * w_up.size, transcendentals=0
        ),
        name="piece",
    )(factors, upper)
    piece = pl.pallas_call(
        tie_kernel,
        out_shape=jax.ShapeDtypeStruct(piece.shape, piece.dtype),
        in_specs=[ANY] * n_hid,
        out_specs=ANY,
        input_output_aliases={0: 0},
        compiler_params=ROOM,
        name="tie",
    )(piece, *parts[1:])
    returned = lax.all_to_all(piece, ("expert", "hidden"), 0, 0)
    grad_in = pl.pallas_call(
        return_kernel,
        out_shape=jax.ShapeDtypeStruct((1, tok_dev, part), bf16),
        in_specs=[VMEM] * 2,
        out_specs=VMEM,
        compiler_params=ROOM,
        name="return",
    )(spread, returned)

    chunks = cols // 128
    grads = pl.pallas_call(
        functools.partial(weight_kernel, chunks, (n_dp, n_hid)),
        out_shape=[jax.ShapeDtypeStruct((1, cols, units), jnp.float32)] * 2,
        in_specs=[VMEM] * (n_hid + 2),
        out_specs=[HBM] * 2,
        scratch_shapes=[
            pltpu.VMEM((n_dp * slots, 2 * cols), bf16),
            pltpu.VMEM((2, cols, units), jnp.float32),
            pltpu.SemaphoreType.DMA((2, chunks)),
        ],
        compiler_params=ROOM,
        cost_estimate=pl.CostEstimate(
            flops=4 * n_dp * slots * cols * units, bytes_accessed=64 * cols * units, transcendentals=0
        ),
        name="weight",
    )(rows, *parts, gathered)
    return (grad_in, *grads)


def solution(mesh):
    placed = (
        P("dp", "expert", None),
        P("dp", "expert", None),
        P("dp", "expert", None, None),
        P("dp", "expert", None, None),
        P("expert", None, "hidden"),
        P("expert", None, "hidden"),
    )
    return jax.shard_map(
        local,
        mesh=mesh,
        in_specs=placed,
        out_specs=(
            P("dp", "expert", "hidden"),
            P("expert", "dp", "hidden"),
            P("expert", "dp", "hidden"),
        ),
        check_vma=False,
    )
```
